32 devices in a mesh: grp: 2 (over y), blk: 4 (over x, core), dep: 4 (over z).
Axes of the slice: x: 2, y: 2, z: 4, core: 2. Of those that a mesh axis runs over, the one named last changes fastest.
Arguments:
- velocity: float32 [3, 1024, 32, 64], P(None, 'blk', 'dep', 'grp'), may hold values from -6 to 6
- scalar: float32 [32, 64, 8192], P('dep', 'grp', 'blk'), may hold values from -6 to 6
- spline_base: int32 [8192], P('blk'), may hold values from -1 to 1023, as said below
- spline_frac: float32 [8192], P('blk'), may hold values from 0 to 1
Outputs:
- segment_velocity: float32 [3, 1024, 32, 64], P(None, 'blk', 'dep', 'grp')
- scalar_segment: float32 [32, 64, 8192], P('dep', 'grp', 'blk')
The draws below stay inside these ranges and needn't reach their ends.
Inputs may be any that keep to these rules, and one draw needn't show every extreme that they name: spline_base[i] is i // 8 or i // 8 - 1; the spline reads velocity cells spline_base[i] - 1 to spline_base[i] + 2 modulo 1024.
All inputs are finite; a program needn't handle non-finite values.
Results may differ from the reference program's by a relative error of at most 0.00007.
Values sent between devices are 32-bit elements; how exact they have to be, the bound alone decides.
No kernel may reach another device: no remote copies, remote signals or barrier semaphores. Data moves between devices by JAX's collectives and lax.ppermute only.
A program may use at most 64 MiB of HBM per device.

```python
import math
import jax
import jax.numpy as jnp
from jax import lax

NX = 1024
REFINE = 8
FX = 8192
Z = 32
Y = 64


def draw_spline_base(key, part):
    cells = lax.iota(jnp.int32, FX)
    jitter = jax.random.randint(jax.random.fold_in(key, 11), (FX,), 0, 2)
    base = cells // REFINE - jitter
    base = jnp.where(cells == 0, -1, base)
    base = jnp.where(cells == FX - 1, NX - 1, base)
    return base.astype(jnp.int32)


def level_of(stream_key, dims, cuts, least, top_value):
    gain, own = 1.0, jax.random.fold_in(stream_key, 6)
    for axis_at, parts in cuts:
        heights = jnp.exp(jax.random.uniform(jax.random.fold_in(own, axis_at), (parts,), jnp.float32, least / len(cuts), top_value / len(cuts)))
        gain = gain * jnp.repeat(heights, dims[axis_at] // parts).reshape([-1 if axis == axis_at else 1 for axis in range(len(dims))])
    return gain


def scatter_about(rng, shape, scale, most, split=(), kind=jnp.bfloat16):
    result = scale * jax.random.normal(rng, shape, jnp.float32)
    if split:
        result = result * level_of(rng, shape, split, -0.22, 0.18)
    return jnp.clip(result, -most, most).astype(kind)


def setup_inputs(seed: int = 0) -> dict:
    keys = jax.random.split(jax.random.key(seed), 5)
    return {
        "velocity": scatter_about(keys[0], (3, NX, Z, Y), 1.0, 6.0, ((1, 4), (2, 4), (3, 2)), jnp.float32),
        "scalar": scatter_about(keys[1], (Z, Y, FX), 1.0, 6.0, ((0, 4), (1, 2), (2, 4)), jnp.float32),
        "spline_base": draw_spline_base(jax.random.fold_in(keys[4], 71), 0),
        "spline_frac": jnp.clip(1.0 * jax.random.uniform(keys[3], (FX,), jnp.float32) ** level_of(keys[3], (FX,), ((0, 4),), -0.2, 0.2), 0.0, 1.0),
    }


velocity_step = 0.002
viscosity = 0.00125
advect_rate = 0.2
diffuse_rate = 0.05
first_coeffs = (1.0 / 280.0, -4.0 / 105.0, 0.2, -0.8, 0.0, 0.8, -0.2, 4.0 / 105.0, -1.0 / 280.0)
second_coeffs = (-1.0 / 560.0, 8.0 / 315.0, -0.2, 1.6, -205.0 / 72.0, 1.6, -0.2, 8.0 / 315.0, -1.0 / 560.0)
highest = lax.Precision.HIGHEST


def derivative_rows(first_row, count, length):
    rows = first_row + lax.iota(jnp.int32, count)
    columns = lax.iota(jnp.int32, length)
    offset = (rows[:, None] - columns[None, :]) % length
    signed = jnp.where(offset > length // 2, offset - length, offset)
    angle = signed.astype(jnp.float32) * (math.pi / length)
    parity = 1.0 - 2.0 * (offset % 2).astype(jnp.float32)
    same = offset == 0
    sine = jnp.where(same, 1.0, jnp.sin(angle))
    first = jnp.where(same, 0.0, 0.5 * parity * jnp.cos(angle) / sine)
    second = jnp.where(same, -(length * length) / 12.0 - 1.0 / 6.0, -0.5 * parity / (sine * sine))
    average = jnp.full((count, length), 1.0 / length, jnp.float32)
    return jnp.concatenate([first, second, average], axis=0)


def catmull_weights(fraction):
    square = fraction * fraction
    cube = square * fraction
    return ((-cube + 2.0 * square - fraction) * 0.5,
            (3.0 * cube - 5.0 * square + 2.0) * 0.5,
            (-3.0 * cube + 4.0 * square + fraction) * 0.5,
            (cube - square) * 0.5)


def scalar_update(padded, fine):
    extent = (padded.shape[0] - 8, padded.shape[1] - 8, padded.shape[2] - 8)
    centre = lax.slice(padded, (4, 4, 4), (4 + extent[0], 4 + extent[1], 4 + extent[2]))
    gradients = []
    curvature = jnp.zeros(extent, jnp.float32)
    for axis_index in range(3):
        slope = jnp.zeros(extent, jnp.float32)
        for offset in range(9):
            begin = [4, 4, 4]
            begin[axis_index] = offset
            finish = (begin[0] + extent[0], begin[1] + extent[1], begin[2] + extent[2])
            window = lax.slice(padded, tuple(begin), finish)
            if first_coeffs[offset] != 0.0:
                slope = slope + first_coeffs[offset] * window
            curvature = curvature + second_coeffs[offset] * window
        gradients.append(slope)
    advection = fine[2] * gradients[0] + fine[1] * gradients[1] + fine[0] * gradients[2]
    return centre - advect_rate * advection + diffuse_rate * curvature


def reference(velocity, scalar, spline_base, spline_frac):
    length = velocity.shape[1]
    table = derivative_rows(0, length, length)
    both = jnp.einsum("kx,cxzy->ckzy", table, velocity, precision=highest)
    segment = velocity - both[:, 2 * length:] + velocity_step * (viscosity * both[:, length:2 * length] - velocity[0:1] * both[:, :length])
    weights = catmull_weights(spline_frac)
    padded = jnp.pad(scalar, 4, mode="wrap")
    depth = scalar.shape[0]

    def one_layer(layer):
        coarse = lax.dynamic_index_in_dim(segment, layer, 2, keepdims=False)
        fine = jnp.zeros((3, spline_base.shape[0], coarse.shape[2]), jnp.float32)
        for tap_index in range(4):
            index = ((spline_base + (tap_index - 1)) % length).astype(jnp.int32)
            taps = jnp.take(coarse, index, axis=1)
            fine = fine + weights[tap_index][None, :, None] * taps
        fine = jnp.transpose(fine, (0, 2, 1))[:, None]
        slab = lax.dynamic_slice_in_dim(padded, layer, 9, 0)
        return scalar_update(slab, fine)[0]

    scalar_segment = lax.map(one_layer, jnp.arange(depth, dtype=jnp.int32))
    return segment, scalar_segment
```

```python
import functools

import jax
import jax.numpy as jnp
import ml_dtypes
import numpy as np
from jax import lax
from jax.experimental import pallas as pl
from jax.experimental.pallas import tpu as pltpu
from jax.sharding import PartitionSpec as P

velocity_step = 0.002
viscosity = 0.00125
advect_rate = 0.2
diffuse_rate = 0.05
first_side = (0.8, -0.2, 4.0 / 105.0, -1.0 / 280.0)
second_side = (1.6, -0.2, 8.0 / 315.0, -1.0 / 560.0)
second_centre = -205.0 / 72.0
slope = tuple(-advect_rate * a for a in first_side)
bend = tuple(diffuse_rate * b for b in second_side)
centre_weight = 1.0 + 3.0 * diffuse_rate * second_centre
reach = 4
lanes = 128
vmem_bytes = 48 * 1024 * 1024


def ring(axis, step):
    count = lax.axis_size(axis)
    return [(i, (i + step) % count) for i in range(count)]


def exclusive(axis, mask):
    return [(i, i ^ mask) for i in range(lax.axis_size(axis))]


def split_table(values):
    high = values.astype(np.float32).astype(ml_dtypes.bfloat16)
    low = (values - high.astype(np.float64)).astype(np.float32).astype(ml_dtypes.bfloat16)
    return high, low


def circulant_tables(length, cells):
    s = np.arange(length)
    signed = np.where(s > length // 2, s - length, s)
    angle = signed * (np.pi / length)
    sine = np.where(s == 0, 1.0, np.sin(angle))
    parity = 1.0 - 2.0 * (s % 2)
    first = np.where(s == 0, 0.0, 0.5 * parity * np.cos(angle) / sine) * velocity_step
    second = np.where(s == 0, -(length * length) / 12.0 - 1.0 / 6.0, -0.5 * parity / (sine * sine))
    second = second * (velocity_step * viscosity)
    own = np.arange(cells)
    outer = np.zeros(lanes, np.int64)
    used = np.zeros(lanes)
    for lane, cell in ((0, cells), (1, cells + 1), (lanes - 2, -2), (lanes - 1, -1)):
        outer[lane] = cell
        used[lane] = 1.0
    blocks = []
    for distance in range(length // cells):
        main = (distance * cells + own[None, :] - own[:, None]) % length
        side = (distance * cells + outer[None, :] - own[:, None]) % length
        blocks.append(
            np.concatenate([first[main], second[main], first[side] * used, second[side] * used], axis=1)
        )
    return split_table(np.stack(blocks))


def dot(a, b):
    return jnp.dot(a, b, preferred_element_type=jnp.float32)


def split(value):
    high = value.astype(jnp.bfloat16)
    return high, (value - high.astype(jnp.float32)).astype(jnp.bfloat16)


def segment_kernel(length, info, *refs):
    v_refs, high_refs, low_refs = refs[:4], refs[4:8], refs[8:12]
    main_ref, outer_ref = refs[12:]
    kinds, rows, cells = v_refs[0].shape
    blocks = [ref[...].reshape(kinds * rows, cells) for ref in v_refs]
    total = jnp.zeros((kinds * rows, 2 * cells + 2 * lanes), jnp.float32)
    sums = jnp.zeros((kinds * rows, 1), jnp.float32)
    for block, high_ref, low_ref in zip(blocks, high_refs, low_refs):
        high, low = split(block)
        total += dot(high, high_ref[0]) + (dot(low, high_ref[0]) + dot(high, low_ref[0]))
        sums += jnp.sum(block, axis=1, keepdims=True)
    mean = sums * (1.0 / length)
    even = info[4] == 0
    after = jnp.where(even, blocks[1][:, :lanes], blocks[3][:, :lanes])
    before = jnp.where(even, blocks[3][:, cells - lanes :], blocks[1][:, cells - lanes :])
    place = lax.broadcasted_iota(jnp.int32, after.shape, 1)
    outer = jnp.where(place < lanes // 2, after, before)

    def advance(own, first, second):
        lead = jnp.concatenate([own[:rows]] * kinds, axis=0)
        return own - mean + (second - lead * first)

    main = advance(blocks[0], total[:, :cells], total[:, cells : 2 * cells])
    side = advance(outer, total[:, 2 * cells : 2 * cells + lanes], total[:, 2 * cells + lanes :])
    main_ref[...] = main.reshape(kinds, rows, cells)
    outer_ref[...] = side.reshape(kinds, rows, lanes)


def segment_call(blocks, info, length):
    kinds, rows, cells = blocks[0].shape
    steps = 2
    part = rows // steps
    high, low = circulant_tables(length, cells)
    width = high.shape[2]
    whole = pl.BlockSpec((kinds, part, cells), lambda g, info: (0, g, 0))
    tables = [
        pl.BlockSpec((1, cells, width), functools.partial(lambda j, g, info: (info[j], 0, 0), j))
        for j in range(4)
    ]
    return pl.pallas_call(
        functools.partial(segment_kernel, length),
        grid_spec=pltpu.PrefetchScalarGridSpec(
            num_scalar_prefetch=1,
            grid=(steps,),
            in_specs=[whole] * 4 + tables + tables,
            out_specs=[whole, pl.BlockSpec((kinds, part, lanes), lambda g, info: (0, g, 0))],
        ),
        out_shape=[
            jax.ShapeDtypeStruct((kinds, rows, cells), jnp.float32),
            jax.ShapeDtypeStruct((kinds, rows, lanes), jnp.float32),
        ],
        compiler_params=pltpu.CompilerParams(vmem_limit_bytes=vmem_bytes),
        cost_estimate=pl.CostEstimate(
            flops=6 * kinds * rows * length * width, bytes_accessed=8 * 2**20, transcendentals=0
        ),
        name="segment",
    )(info, *blocks, *([jnp.asarray(high)] * 4), *([jnp.asarray(low)] * 4))


def catmull_weights(fraction):
    square = fraction * fraction
    cube = square * fraction
    return (
        (-cube + 2.0 * square - fraction) * 0.5,
        (3.0 * cube - 5.0 * square + 2.0) * 0.5,
        (-3.0 * cube + 4.0 * square + fraction) * 0.5,
        (cube - square) * 0.5,
    )


def spline_matrix(local_base, fraction, cells, refine):
    tiles = cells // lanes
    row = lax.iota(jnp.int32, 2 * lanes)[:, None]
    half = (lax.iota(jnp.int32, local_base.shape[0]) // (refine * (lanes // 2)))[None, :]
    own = half // 2
    other = (own + jnp.where(half % 2 == 1, 1, tiles)) % (tiles + 1)
    lane = jnp.where(row < lanes, own * lanes + row, other * lanes + row - lanes)
    cell = jnp.where(lane < cells + lanes // 2, lane, lane - cells - lanes)
    gap = cell - local_base[None, :]
    matrix = jnp.zeros(gap.shape, jnp.float32)
    for tap, weight in enumerate(catmull_weights(fraction)):
        matrix = jnp.where(gap == tap - 1, weight[None, :], matrix)
    return matrix


def combine_kernel(tiles, main_ref, outer_ref, matrix_ref, gx_ref, gy_ref, gz_ref, base_ref,
                   out_ref, fine_ref, seg_high, seg_low):
    step = pl.program_id(0)
    kinds, rows, cells = main_ref.shape

    @pl.when(step == 0)
    def _():
        for ref, begin, width in ((main_ref, 0, cells), (outer_ref, cells, lanes)):
            high, low = split(ref[...].reshape(kinds * rows, width))
            seg_high[:, begin : begin + width] = high
            seg_low[:, begin : begin + width] = low

    own = step // 2
    other = lax.rem(own + jnp.where(lax.rem(step, 2) == 1, 1, tiles), tiles + 1)

    def pair(ref):
        return jnp.concatenate(
            [ref[:, pl.ds(pl.multiple_of(at * lanes, lanes), lanes)] for at in (own, other)], axis=1
        )

    high, low = pair(seg_high), pair(seg_low)
    weights, rest = split(matrix_ref[...])
    fine = dot(high, weights) + (dot(low, weights) + dot(high, rest))
    vertical = fine[2 * rows :]
    out_ref[...] = base_ref[...] + (
        fine[:rows] * gx_ref[...] + fine[rows : 2 * rows] * gy_ref[...] + vertical * gz_ref[...]
    )
    fine_ref[...] = vertical


def combine_call(main, outer, matrix, gx, gy, gz, base):
    kinds, rows, cells = main.shape
    points = matrix.shape[1]
    steps = 2 * (cells // lanes)
    width = points // steps
    tile = pl.BlockSpec((rows, width), lambda t: (0, t))
    weight = pl.BlockSpec((2 * lanes, width), lambda t: (0, t))
    flat = jax.ShapeDtypeStruct((rows, points), jnp.float32)
    return pl.pallas_call(
        functools.partial(combine_kernel, cells // lanes),
        grid=(steps,),
        in_specs=[
            pl.BlockSpec((kinds, rows, cells), lambda t: (0, 0, 0)),
            pl.BlockSpec((kinds, rows, lanes), lambda t: (0, 0, 0)),
            weight,
            tile,
            tile,
            tile,
            tile,
        ],
        out_specs=[tile, tile],
        out_shape=[flat, flat],
        scratch_shapes=[
            pltpu.VMEM((kinds * rows, cells + lanes), jnp.bfloat16),
            pltpu.VMEM((kinds * rows, cells + lanes), jnp.bfloat16),
        ],
        compiler_params=pltpu.CompilerParams(vmem_limit_bytes=vmem_bytes),
        cost_estimate=pl.CostEstimate(
            flops=12 * kinds * rows * lanes * points, bytes_accessed=16 * 2**20, transcendentals=0
        ),
        name="combine",
    )(main, outer, matrix, gx, gy, gz, base)


def inner_kernel(steps, mid_ref, left_ref, right_ref, before_ref, after_ref, rows_ref,
                 gx_ref, gy_ref, gz_ref, base_ref):
    step = pl.program_id(0)
    depth, rows, width = mid_ref.shape
    at_first, at_last = step == 0, step == steps - 1
    place = lax.broadcasted_iota(jnp.int32, (rows, lanes), 1)
    for z in range(depth):
        mid = mid_ref[z]
        left = jnp.where(at_first, before_ref[z], left_ref[z])
        right = jnp.where(at_last, after_ref[z], right_ref[z])
        curve = centre_weight * mid

        ringed = jnp.concatenate([mid, jnp.where(place < lanes // 2, right, left)], axis=1)
        grade = None
        for m in range(1, reach + 1):
            ahead = pltpu.roll(ringed, width + lanes - m, 1)[:, :width]
            behind = pltpu.roll(ringed, m, 1)[:, :width]
            term = slope[m - 1] * (ahead - behind)
            grade = term if grade is None else grade + term
            curve += bend[m - 1] * (ahead + behind)
        gx_ref[z] = grade

        ringed = jnp.concatenate([mid, rows_ref[z]], axis=0)
        grade = None
        for m in range(1, reach + 1):
            ahead = pltpu.roll(ringed, rows + 2 * reach - m, 0)[:rows]
            behind = pltpu.roll(ringed, m, 0)[:rows]
            term = slope[m - 1] * (ahead - behind)
            grade = term if grade is None else grade + term
            curve += bend[m - 1] * (ahead + behind)
        gy_ref[z] = grade

        grade = None
        for m in range(1, reach + 1):
            for sign in (1, -1):
                if 0 <= z + sign * m < depth:
                    near = mid_ref[z + sign * m]
                    term = (sign * slope[m - 1]) * near
                    grade = term if grade is None else grade + term
                    curve += bend[m - 1] * near
        gz_ref[z] = grade
        base_ref[z] = curve


def inner_call(scalar, before, after, outer_rows):
    depth, rows, points = scalar.shape
    width = min(512, points)
    steps = points // width
    tiles = width // lanes
    last = points // lanes - 1
    tile = pl.BlockSpec((depth, rows, width), lambda t: (0, 0, t))
    edge = (depth, rows, lanes)
    shape = jax.ShapeDtypeStruct(scalar.shape, jnp.float32)
    return pl.pallas_call(
        functools.partial(inner_kernel, steps),
        grid=(steps,),
        in_specs=[
            tile,
            pl.BlockSpec(edge, lambda t: (0, 0, jnp.maximum(t * tiles - 1, 0))),
            pl.BlockSpec(edge, lambda t: (0, 0, jnp.minimum((t + 1) * tiles, last))),
            pl.BlockSpec(edge, lambda t: (0, 0, 0)),
            pl.BlockSpec(edge, lambda t: (0, 0, 0)),
            pl.BlockSpec((depth, 2 * reach, width), lambda t: (0, 0, t)),
        ],
        out_specs=[tile] * 4,
        out_shape=[shape] * 4,
        compiler_params=pltpu.CompilerParams(vmem_limit_bytes=vmem_bytes),
        cost_estimate=pl.CostEstimate(
            flops=100 * scalar.size, bytes_accessed=24 * scalar.size, transcendentals=0
        ),
        name="inner",
    )(scalar, scalar, scalar, before, after, outer_rows)


def outer_kernel(above, part_ref, fine_ref, halo_ref, out_ref):
    for p in range(reach):
        grade = curve = None
        for h in range(reach):
            m = reach + h - p if above else h - reach - p
            if 1 <= abs(m) <= reach:
                near = halo_ref[h]
                first = (slope[m - 1] if m > 0 else -slope[-m - 1]) * near
                second = bend[abs(m) - 1] * near
                grade = first if grade is None else grade + first
                curve = second if curve is None else curve + second
        out_ref[p] = part_ref[p] + (fine_ref[p] * grade + curve)


def outer_call(above, part, fine, halo):
    depth, rows, points = part.shape
    half = depth // reach - 1 if above else 0
    steps = 4
    width = points // steps if points % (steps * lanes) == 0 else points
    block = pl.BlockSpec((reach, rows, width), lambda t: (half, 0, t))
    return pl.pallas_call(
        functools.partial(outer_kernel, above),
        grid=(points // width,),
        in_specs=[block, block, pl.BlockSpec((reach, rows, width), lambda t: (0, 0, t))],
        out_specs=block,
        out_shape=jax.ShapeDtypeStruct(part.shape, jnp.float32),
        input_output_aliases={0: 0},
        compiler_params=pltpu.CompilerParams(vmem_limit_bytes=vmem_bytes),
        cost_estimate=pl.CostEstimate(
            flops=50 * halo.size, bytes_accessed=16 * halo.size, transcendentals=0
        ),
        name="outer",
    )(part, fine, halo)


def general_segment(rows_of_x, block, length):
    cells = rows_of_x.shape[2]
    high, low = circulant_tables(length, cells)
    table = jnp.asarray(high.astype(np.float32)) + jnp.asarray(low.astype(np.float32))
    everyone = lax.all_gather(rows_of_x, "blk", axis=0)
    count = everyone.shape[0]
    order = (block - lax.iota(jnp.int32, count)) % count
    total = jnp.einsum(
        "bcrx,bxk->crk", everyone, jnp.take(table, order, axis=0), precision=lax.Precision.HIGHEST
    )
    mean = jnp.sum(everyone, axis=(0, 3))[..., None] / length
    before = jnp.take(everyone, (block - 1) % count, axis=0)[..., -2:]
    after = jnp.take(everyone, (block + 1) % count, axis=0)[..., :2]

    def sides(start):
        return (total[..., start + lanes - 2 : start + lanes], total[..., start : start + 2])

    low_first, high_first = sides(2 * cells)
    low_second, high_second = sides(2 * cells + lanes)
    first = jnp.concatenate([low_first, total[..., :cells], high_first], axis=2)
    second = jnp.concatenate([low_second, total[..., cells : 2 * cells], high_second], axis=2)
    own = jnp.concatenate([before, rows_of_x, after], axis=2)
    return own - mean + (second - own[0:1] * first)


def general_fine(wide, local_base, fraction):
    slots = lax.iota(jnp.int32, wide.shape[2])[:, None]
    matrix = jnp.zeros((wide.shape[2], local_base.shape[0]), jnp.float32)
    for tap, weight in enumerate(catmull_weights(fraction)):
        matrix = matrix + jnp.where(slots == (local_base + (tap + 1))[None, :], weight[None, :], 0.0)
    return jnp.einsum("crx,xi->cri", wide, matrix, precision=lax.Precision.HIGHEST)


def per_device(velocity, scalar, spline_base, spline_frac):
    kinds, cells, depth, height = velocity.shape
    points = scalar.shape[2]
    rows = depth * height
    count = lax.axis_size("blk")
    length = cells * count
    block = lax.axis_index("blk")

    lower = lax.ppermute(scalar[-reach:], "dep", ring("dep", 1))
    upper = lax.ppermute(scalar[:reach], "dep", ring("dep", -1))
    rows_of_x = jnp.transpose(velocity, (0, 2, 3, 1)).reshape(kinds, rows, cells)

    fast = count == 4 and cells % lanes == 0
    if fast:
        chip = lax.ppermute(rows_of_x, "blk", exclusive("blk", 2))
        core = lax.ppermute(rows_of_x, "blk", exclusive("blk", 1))
    if lax.axis_size("grp") == 2:
        edges = jnp.concatenate([scalar[:, :reach], scalar[:, -reach:]], axis=1)
        outer_rows = lax.ppermute(edges, "grp", ring("grp", 1))
    else:
        outer_rows = jnp.concatenate(
            [
                lax.ppermute(scalar[:, :reach], "grp", ring("grp", -1)),
                lax.ppermute(scalar[:, -reach:], "grp", ring("grp", 1)),
            ],
            axis=1,
        )
    before = lax.ppermute(scalar[:, :, -lanes:], "blk", ring("blk", 1))
    after = lax.ppermute(scalar[:, :, :lanes], "blk", ring("blk", -1))

    gx, gy, gz, base = inner_call(scalar, before, after, outer_rows)
    local_base = spline_base - block * cells
    flat = (rows, points)
    if fast:
        matrix = spline_matrix(local_base, spline_frac, cells, points // cells)
        diagonal = lax.ppermute(chip, "blk", exclusive("blk", 1))
        info = jnp.stack([(block - (block ^ j)) % count for j in range(4)] + [block % 2])
        main, outer = segment_call([rows_of_x, core, chip, diagonal], info.astype(jnp.int32), length)
        part, vertical = combine_call(
            main, outer, matrix, gx.reshape(flat), gy.reshape(flat), gz.reshape(flat), base.reshape(flat)
        )
    else:
        wide = general_segment(rows_of_x, block, length)
        main = wide[..., 2:-2]
        fine = general_fine(wide, local_base, spline_frac)
        vertical = fine[2]
        part = base.reshape(flat) + (
            fine[0] * gx.reshape(flat) + fine[1] * gy.reshape(flat) + vertical * gz.reshape(flat)
        )
    part, vertical = part.reshape(scalar.shape), vertical.reshape(scalar.shape)
    part = outer_call(False, part, vertical, lower)
    result = outer_call(True, part, vertical, upper)
    segment = jnp.transpose(main.reshape(kinds, depth, height, cells), (0, 3, 1, 2))
    return segment, result


def solution(mesh):
    in_specs = (P(None, "blk", "dep", "grp"), P("dep", "grp", "blk"), P("blk"), P("blk"))
    out_specs = (P(None, "blk", "dep", "grp"), P("dep", "grp", "blk"))
    return jax.shard_map(
        per_device, mesh=mesh, in_specs=in_specs, out_specs=out_specs, check_vma=False
    )
```

```python
import functools
import math

import jax
import jax.numpy as jnp
import ml_dtypes
import numpy as np
from jax import lax
from jax.experimental import pallas as pl
from jax.experimental.pallas import tpu as pltpu
from jax.sharding import PartitionSpec as P

velocity_step = 0.002
viscosity = 0.00125
advect_rate = 0.2
diffuse_rate = 0.05
first_side = (0.8, -0.2, 4.0 / 105.0, -1.0 / 280.0)
second_side = (1.6, -0.2, 8.0 / 315.0, -1.0 / 560.0)
second_centre = -205.0 / 72.0
slope = tuple(-advect_rate * a for a in first_side)
bend = tuple(diffuse_rate * b for b in second_side)
centre_weight = 1.0 + 3.0 * diffuse_rate * second_centre
reach = 4
lanes = 128
vmem_bytes = 60 * 1024 * 1024
light = pl.CostEstimate(flops=1024, bytes_accessed=1024, transcendentals=0)


def ring(axis, step):
    count = lax.axis_size(axis)
    return [(i, (i + step) % count) for i in range(count)]


def exclusive(axis, mask):
    return [(i, i ^ mask) for i in range(lax.axis_size(axis))]


def split_table(values):
    high = values.astype(np.float32).astype(ml_dtypes.bfloat16)
    low = (values - high.astype(np.float64)).astype(np.float32).astype(ml_dtypes.bfloat16)
    return high, low


def circulant_tables(length, cells):
    s = np.arange(length)
    signed = np.where(s > length // 2, s - length, s)
    angle = signed * (np.pi / length)
    sine = np.where(s == 0, 1.0, np.sin(angle))
    parity = 1.0 - 2.0 * (s % 2)
    first = np.where(s == 0, 0.0, 0.5 * parity * np.cos(angle) / sine) * velocity_step
    second = np.where(s == 0, -(length * length) / 12.0 - 1.0 / 6.0, -0.5 * parity / (sine * sine))
    second = second * (velocity_step * viscosity)
    own = np.arange(cells)
    outer = np.zeros(lanes, np.int64)
    used = np.zeros(lanes)
    for lane, cell in ((0, cells), (1, cells + 1), (lanes - 2, -2), (lanes - 1, -1)):
        outer[lane] = cell
        used[lane] = 1.0
    blocks = []
    for distance in range(length // cells):
        main = (distance * cells + own[None, :] - own[:, None]) % length
        side = (distance * cells + outer[None, :] - own[:, None]) % length
        blocks.append(
            np.concatenate([first[main], second[main], first[side] * used, second[side] * used], axis=1)
        )
    return split_table(np.stack(blocks))


def dot(a, b):
    return jnp.dot(a, b, preferred_element_type=jnp.float32)


def split(value):
    high = value.astype(jnp.bfloat16)
    return high, (value - high.astype(jnp.float32)).astype(jnp.bfloat16)


def segment_kernel(length, shares, info, own_ref, *refs):
    sent, (high_refs, low_refs) = refs[: 3 * shares], (refs[3 * shares :][:4], refs[3 * shares :][4:8])
    main_ref, outer_ref = refs[-2:]
    kinds, rows, cells = own_ref.shape
    part = rows // shares
    lines = kinds * part
    even = info[4] == 0
    for h in range(shares):
        span = slice(h * part, (h + 1) * part)
        blocks = [own_ref[:, span].reshape(lines, cells)]
        blocks += [sent[j * shares + h][:lines] for j in range(3)]
        total = jnp.zeros((lines, 2 * cells + 2 * lanes), jnp.float32)
        sums = jnp.zeros((lines, 1), jnp.float32)
        for block, high_ref, low_ref in zip(blocks, high_refs, low_refs):
            high, low = split(block)
            total += dot(high, high_ref[0]) + (dot(low, high_ref[0]) + dot(high, low_ref[0]))
            sums += jnp.sum(block, axis=1, keepdims=True)
        mean = sums * (1.0 / length)
        after = jnp.where(even, blocks[1][:, :lanes], blocks[3][:, :lanes])
        before = jnp.where(even, blocks[3][:, cells - lanes :], blocks[1][:, cells - lanes :])
        place = lax.broadcasted_iota(jnp.int32, after.shape, 1)
        outer = jnp.where(place < lanes // 2, after, before)

        def advance(own, first, second):
            lead = jnp.concatenate([own[:part]] * kinds, axis=0)
            return own - mean + (second - lead * first)

        main = advance(blocks[0], total[:, :cells], total[:, cells : 2 * cells])
        side = advance(outer, total[:, 2 * cells : 2 * cells + lanes], total[:, 2 * cells + lanes :])
        main_ref[:, span] = main.reshape(kinds, part, cells)
        outer_ref[:, span] = side.reshape(kinds, part, lanes)


def segment_call(own, core, chip, diagonal, info, length):
    kinds, rows, cells = own.shape
    shares = len(core)
    high, low = circulant_tables(length, cells)
    width = high.shape[2]
    whole = pl.BlockSpec(own.shape, lambda g, info: (0, 0, 0))
    sent = pl.BlockSpec(core[0].shape, lambda g, info: (0, 0))
    tables = [
        pl.BlockSpec((1, cells, width), functools.partial(lambda j, g, info: (info[j], 0, 0), j))
        for j in range(4)
    ]
    return pl.pallas_call(
        functools.partial(segment_kernel, length, shares),
        grid_spec=pltpu.PrefetchScalarGridSpec(
            num_scalar_prefetch=1,
            grid=(1,),
            in_specs=[whole] + [sent] * (3 * shares) + tables + tables,
            out_specs=[whole, pl.BlockSpec((kinds, rows, lanes), lambda g, info: (0, 0, 0))],
        ),
        out_shape=[
            jax.ShapeDtypeStruct((kinds, rows, cells), jnp.float32),
            jax.ShapeDtypeStruct((kinds, rows, lanes), jnp.float32),
        ],
        compiler_params=pltpu.CompilerParams(vmem_limit_bytes=vmem_bytes),
        cost_estimate=light,
        name="segment",
    )(info, own, *core, *chip, *diagonal, *([jnp.asarray(high)] * 4), *([jnp.asarray(low)] * 4))


def catmull_weights(fraction):
    square = fraction * fraction
    cube = square * fraction
    return (
        (-cube + 2.0 * square - fraction) * 0.5,
        (3.0 * cube - 5.0 * square + 2.0) * 0.5,
        (-3.0 * cube + 4.0 * square + fraction) * 0.5,
        (cube - square) * 0.5,
    )


def spline_matrix(local_base, fraction, cells, refine):
    tiles = cells // lanes
    row = lax.iota(jnp.int32, 2 * lanes)[:, None]
    half = (lax.iota(jnp.int32, local_base.shape[0]) // (refine * (lanes // 2)))[None, :]
    own = half // 2
    other = (own + jnp.where(half % 2 == 1, 1, tiles)) % (tiles + 1)
    lane = jnp.where(row < lanes, own * lanes + row, other * lanes + row - lanes)
    cell = jnp.where(lane < cells + lanes // 2, lane, lane - cells - lanes)
    gap = cell - local_base[None, :]
    matrix = jnp.zeros(gap.shape, jnp.float32)
    for tap, weight in enumerate(catmull_weights(fraction)):
        matrix = jnp.where(gap == tap - 1, weight[None, :], matrix)
    return matrix


def end_terms(halo, sign):
    grade = curve = None
    place = lax.broadcasted_iota(jnp.int32, halo.shape, 1)
    halo = jnp.where(place >= lanes // 2 if sign < 0 else place < lanes // 2, halo, 0.0)
    for m in range(1, reach + 1):
        near = pltpu.roll(halo, (-sign * m) % lanes, 1)
        first, second = (sign * slope[m - 1]) * near, bend[m - 1] * near
        grade = first if grade is None else grade + first
        curve = second if curve is None else curve + second
    near = place < reach if sign < 0 else place >= lanes - reach
    return jnp.where(near, grade, 0.0), jnp.where(near, curve, 0.0)


def combine_kernel(tiles, shares, parity, main_ref, outer_ref, matrix_ref, gx_ref, gy_ref, gz_ref, base_ref, *refs):
    core_refs, far_refs = refs[:shares], refs[shares : 2 * shares]
    out_ref, fine_ref, seg_high, seg_low, halo_ref = refs[2 * shares :]
    step, steps = pl.program_id(0), pl.num_programs(0)
    kinds, rows, cells = main_ref.shape
    part = rows // shares

    @pl.when(step == 0)
    def _():
        for ref, begin, width in ((main_ref, 0, cells), (outer_ref, cells, lanes)):
            high, low = split(ref[...].reshape(kinds * rows, width))
            seg_high[:, begin : begin + width] = high
            seg_low[:, begin : begin + width] = low
        core = jnp.concatenate([ref[:, :part] for ref in core_refs], axis=1)
        far = jnp.concatenate([ref[:, :part] for ref in far_refs], axis=1)
        even = parity[0] == 0
        after = jnp.where(even, core, far)[:reach]
        before = jnp.where(even, far, core)[reach:]
        gap = jnp.zeros((lanes - 2 * reach, rows), jnp.float32)
        halo_ref[...] = jnp.concatenate([after, gap, before], axis=0).T

    own = step // 2
    other = lax.rem(own + jnp.where(lax.rem(step, 2) == 1, 1, tiles), tiles + 1)

    def pair(ref):
        return jnp.concatenate(
            [ref[:, pl.ds(pl.multiple_of(at * lanes, lanes), lanes)] for at in (own, other)], axis=1
        )

    high, low = pair(seg_high), pair(seg_low)
    weights, rest = split(matrix_ref[...])
    fine = dot(high, weights) + (dot(low, weights) + dot(high, rest))
    vertical = fine[2 * rows :]
    out_ref[...] = base_ref[...] + (
        fine[:rows] * gx_ref[...] + fine[rows : 2 * rows] * gy_ref[...] + vertical * gz_ref[...]
    )
    fine_ref[...] = vertical
    width = out_ref.shape[1]
    for at, sign, begin in ((0, -1, 0), (steps - 1, 1, width - lanes)):

        @pl.when(step == at)
        def _():
            grade, curve = end_terms(halo_ref[...], sign)
            span = slice(begin, begin + lanes)
            out_ref[:, span] += fine[:rows, span] * grade + curve


def combine_call(main, outer, matrix, gx, gy, gz, base, core, diagonal, parity):
    kinds, rows, cells = main.shape
    points = matrix.shape[1]
    shares = len(core)
    steps = 2 * (cells // lanes)
    width = points // steps
    tile = pl.BlockSpec((rows, width), lambda t, parity: (0, t))
    ends = pl.BlockSpec((2 * reach, cells), lambda t, parity: (core[0].shape[0] // (2 * reach) - 1, 0))
    flat = jax.ShapeDtypeStruct((rows, points), jnp.float32)
    return pl.pallas_call(
        functools.partial(combine_kernel, cells // lanes, shares),
        grid_spec=pltpu.PrefetchScalarGridSpec(
            num_scalar_prefetch=1,
            grid=(steps,),
            in_specs=[
                pl.BlockSpec((kinds, rows, cells), lambda t, parity: (0, 0, 0)),
                pl.BlockSpec((kinds, rows, lanes), lambda t, parity: (0, 0, 0)),
                pl.BlockSpec((2 * lanes, width), lambda t, parity: (0, t)),
                tile,
                tile,
                tile,
                tile,
            ]
            + [ends] * (2 * shares),
            out_specs=[tile, tile],
            scratch_shapes=[
                pltpu.VMEM((kinds * rows, cells + lanes), jnp.bfloat16),
                pltpu.VMEM((kinds * rows, cells + lanes), jnp.bfloat16),
                pltpu.VMEM((rows, lanes), jnp.float32),
            ],
        ),
        out_shape=[flat, flat],
        compiler_params=pltpu.CompilerParams(vmem_limit_bytes=vmem_bytes),
        cost_estimate=light,
        name="combine",
    )(parity, main, outer, matrix, gx, gy, gz, base, *core, *diagonal)


def inner_kernel(steps, mid_ref, left_ref, right_ref, top_ref, bottom_ref,
                 gx_ref, gy_ref, gz_ref, base_ref):
    step = pl.program_id(0)
    depth, rows, width = mid_ref.shape
    at_first, at_last = step == 0, step == steps - 1
    place = lax.broadcasted_iota(jnp.int32, (rows, lanes), 1)
    for z in range(depth):
        mid = mid_ref[z]
        left = jnp.where(at_first, 0.0, left_ref[z])
        right = jnp.where(at_last, 0.0, right_ref[z])
        curve = centre_weight * mid

        ringed = jnp.concatenate([mid, jnp.where(place < lanes // 2, right, left)], axis=1)
        grade = None
        for m in range(1, reach + 1):
            ahead = pltpu.roll(ringed, width + lanes - m, 1)[:, :width]
            behind = pltpu.roll(ringed, m, 1)[:, :width]
            term = slope[m - 1] * (ahead - behind)
            grade = term if grade is None else grade + term
            curve += bend[m - 1] * (ahead + behind)
        gx_ref[z] = grade

        ringed = jnp.concatenate([mid, top_ref[z], bottom_ref[z]], axis=0)
        grade = None
        for m in range(1, reach + 1):
            ahead = pltpu.roll(ringed, rows + 2 * reach - m, 0)[:rows]
            behind = pltpu.roll(ringed, m, 0)[:rows]
            term = slope[m - 1] * (ahead - behind)
            grade = term if grade is None else grade + term
            curve += bend[m - 1] * (ahead + behind)
        gy_ref[z] = grade

        grade = None
        for m in range(1, reach + 1):
            for sign in (1, -1):
                if 0 <= z + sign * m < depth:
                    near = mid_ref[z + sign * m]
                    term = (sign * slope[m - 1]) * near
                    grade = term if grade is None else grade + term
                    curve += bend[m - 1] * near
        gz_ref[z] = grade
        base_ref[z] = curve


def inner_call(scalar, top, bottom):
    depth, rows, points = scalar.shape
    width = min(512, points)
    steps = points // width
    tiles = width // lanes
    last = points // lanes - 1
    tile = pl.BlockSpec((depth, rows, width), lambda t: (0, 0, t))
    edge = (depth, rows, lanes)
    shape = jax.ShapeDtypeStruct(scalar.shape, jnp.float32)
    return pl.pallas_call(
        functools.partial(inner_kernel, steps),
        grid=(steps,),
        in_specs=[
            tile,
            pl.BlockSpec(edge, lambda t: (0, 0, jnp.maximum(t * tiles - 1, 0))),
            pl.BlockSpec(edge, lambda t: (0, 0, jnp.minimum((t + 1) * tiles, last))),
            pl.BlockSpec((depth, reach, width), lambda t: (0, 0, t)),
            pl.BlockSpec((depth, reach, width), lambda t: (0, 0, t)),
        ],
        out_specs=[tile] * 4,
        out_shape=[shape] * 4,
        compiler_params=pltpu.CompilerParams(vmem_limit_bytes=vmem_bytes),
        cost_estimate=light,
        name="inner",
    )(scalar, scalar, scalar, top, bottom)


def outer_kernel(above, part_ref, fine_ref, halo_ref, out_ref):
    for p in range(reach):
        grade = curve = None
        for h in range(reach):
            m = reach + h - p if above else h - reach - p
            if 1 <= abs(m) <= reach:
                near = halo_ref[h]
                first = (slope[m - 1] if m > 0 else -slope[-m - 1]) * near
                second = bend[abs(m) - 1] * near
                grade = first if grade is None else grade + first
                curve = second if curve is None else curve + second
        out_ref[p] = part_ref[p] + (fine_ref[p] * grade + curve)


def outer_call(above, part, fine, halo, begin):
    depth, rows, points = part.shape
    width = halo.shape[2]
    half = depth // reach - 1 if above else 0
    step_width = math.gcd(width, max(begin, width), 512)
    steps = width // step_width
    block = pl.BlockSpec((reach, rows, step_width), lambda t: (half, 0, begin // step_width + t))
    return pl.pallas_call(
        functools.partial(outer_kernel, above),
        grid=(steps,),
        in_specs=[block, block, pl.BlockSpec((reach, rows, step_width), lambda t: (0, 0, t))],
        out_specs=block,
        out_shape=jax.ShapeDtypeStruct(part.shape, jnp.float32),
        input_output_aliases={0: 0},
        compiler_params=pltpu.CompilerParams(vmem_limit_bytes=vmem_bytes),
        cost_estimate=light,
        name="outer",
    )(part, fine, halo)


def tie(value, *gates):
    anywhere = pl.BlockSpec(memory_space=pl.ANY)
    return pl.pallas_call(
        lambda *refs: None,
        in_specs=[anywhere] * (1 + len(gates)),
        out_specs=anywhere,
        out_shape=jax.ShapeDtypeStruct(value.shape, value.dtype),
        input_output_aliases={0: 0},
        cost_estimate=light,
        name="tie",
    )(value, *gates)


def pack_kernel(own_ref, first_ref, last_ref, *refs):
    outs = refs[-len(refs) :]
    kinds, rows, cells = own_ref.shape
    part = rows // len(outs)
    lines = kinds * part
    first = first_ref[...].reshape(rows, lanes).T
    last = last_ref[...].reshape(rows, lanes).T
    for h, out in enumerate(outs):
        span = slice(h * part, (h + 1) * part)
        out[:lines] = own_ref[:, span].reshape(lines, cells)
        ends = jnp.concatenate([first[:reach, span], last[lanes - reach :, span]], axis=0)
        out[lines:, :part] = ends
        if part < cells:
            out[lines:, part:] = jnp.zeros((2 * reach, cells - part), jnp.float32)


def pack_call(own, scalar, shares):
    kinds, rows, cells = own.shape
    depth, height, points = scalar.shape
    end = points // lanes - 1
    shape = jax.ShapeDtypeStruct((kinds * (rows // shares) + 2 * reach, cells), jnp.float32)
    return pl.pallas_call(
        pack_kernel,
        grid=(1,),
        in_specs=[
            pl.BlockSpec(own.shape, lambda t: (0, 0, 0)),
            pl.BlockSpec((depth, height, lanes), lambda t: (0, 0, 0)),
            pl.BlockSpec((depth, height, lanes), lambda t: (0, 0, end)),
        ],
        out_specs=[pl.BlockSpec(shape.shape, lambda t: (0, 0))] * shares,
        out_shape=[shape] * shares,
        cost_estimate=light,
        name="pack",
    )(own, scalar, scalar)


def piece_kernel(source_ref, *refs):
    refs[-1][...] = source_ref[...]


def piece_call(source, begin, size, gates=()):
    points = source.shape[2]
    width = math.gcd(points, 512)
    shape = (size,) + source.shape[1:]
    return pl.pallas_call(
        piece_kernel,
        grid=(points // width,),
        in_specs=[pl.BlockSpec(shape[:2] + (width,), lambda t: (begin // size, 0, t))]
        + [pl.BlockSpec(memory_space=pl.ANY)] * len(gates),
        out_specs=pl.BlockSpec(shape[:2] + (width,), lambda t: (0, 0, t)),
        out_shape=jax.ShapeDtypeStruct(shape, source.dtype),
        cost_estimate=light,
        name="piece",
    )(source, *gates)


def general_segment(rows_of_x, block, length):
    cells = rows_of_x.shape[2]
    high, low = circulant_tables(length, cells)
    table = jnp.asarray(high.astype(np.float32)) + jnp.asarray(low.astype(np.float32))
    everyone = lax.all_gather(rows_of_x, "blk", axis=0)
    count = everyone.shape[0]
    order = (block - lax.iota(jnp.int32, count)) % count
    total = jnp.einsum(
        "bcrx,bxk->crk", everyone, jnp.take(table, order, axis=0), precision=lax.Precision.HIGHEST
    )
    mean = jnp.sum(everyone, axis=(0, 3))[..., None] / length
    before = jnp.take(everyone, (block - 1) % count, axis=0)[..., -2:]
    after = jnp.take(everyone, (block + 1) % count, axis=0)[..., :2]

    def sides(start):
        return (total[..., start + lanes - 2 : start + lanes], total[..., start : start + 2])

    low_first, high_first = sides(2 * cells)
    low_second, high_second = sides(2 * cells + lanes)
    first = jnp.concatenate([low_first, total[..., :cells], high_first], axis=2)
    second = jnp.concatenate([low_second, total[..., cells : 2 * cells], high_second], axis=2)
    own = jnp.concatenate([before, rows_of_x, after], axis=2)
    return own - mean + (second - own[0:1] * first)


def general_fine(wide, local_base, fraction):
    slots = lax.iota(jnp.int32, wide.shape[2])[:, None]
    matrix = jnp.zeros((wide.shape[2], local_base.shape[0]), jnp.float32)
    for tap, weight in enumerate(catmull_weights(fraction)):
        matrix = matrix + jnp.where(slots == (local_base + (tap + 1))[None, :], weight[None, :], 0.0)
    return jnp.einsum("crx,xi->cri", wide, matrix, precision=lax.Precision.HIGHEST)


def per_device(velocity, scalar, spline_base, spline_frac):
    kinds, cells, depth, height = velocity.shape
    points = scalar.shape[2]
    rows = depth * height
    count = lax.axis_size("blk")
    length = cells * count
    block = lax.axis_index("blk")

    lower = lax.ppermute(piece_call(scalar, depth - reach, reach), "dep", ring("dep", 1))
    upper = lax.ppermute(piece_call(scalar, 0, reach), "dep", ring("dep", -1))
    top = lax.ppermute(scalar[:, :reach], "grp", ring("grp", -1))
    bottom = lax.ppermute(scalar[:, -reach:], "grp", ring("grp", 1))
    rows_of_x = jnp.transpose(velocity, (0, 2, 3, 1)).reshape(kinds, rows, cells)
    local_base = spline_base - block * cells
    flat = (rows, points)

    shares = 1
    if count == 4 and cells % lanes == 0 and rows // shares <= cells:
        own = pack_call(rows_of_x, scalar, shares)
        chip = [lax.ppermute(part, "blk", exclusive("blk", 2)) for part in own]
        core = [lax.ppermute(part, "blk", exclusive("blk", 1)) for part in own]
        fields = inner_call(scalar, top, bottom)
        matrix = spline_matrix(local_base, spline_frac, cells, points // cells)
        chip = [tie(part, fields[3]) for part in chip]
        diagonal = [lax.ppermute(part, "blk", exclusive("blk", 1)) for part in chip]
        info = jnp.stack([(block - (block ^ j)) % count for j in range(4)] + [block % 2])
        info = info.astype(jnp.int32)
        main, outer = segment_call(rows_of_x, core, chip, diagonal, info, length)
        part, vertical = combine_call(
            main, outer, matrix, *[field.reshape(flat) for field in fields], core, diagonal, info[4:]
        )
    else:
        before = lax.ppermute(scalar[:, :, -reach:], "blk", ring("blk", 1)).reshape(rows, reach)
        after = lax.ppermute(scalar[:, :, :reach], "blk", ring("blk", -1)).reshape(rows, reach)
        gx, gy, gz, base = [field.reshape(flat) for field in inner_call(scalar, top, bottom)]
        wide = jnp.concatenate([before, jnp.zeros(flat, jnp.float32), after], axis=1)
        for m in range(1, reach + 1):
            ahead = lax.slice_in_dim(wide, reach + m, reach + m + points, axis=1)
            behind = lax.slice_in_dim(wide, reach - m, reach - m + points, axis=1)
            gx = gx + slope[m - 1] * (ahead - behind)
            base = base + bend[m - 1] * (ahead + behind)
        wide = general_segment(rows_of_x, block, length)
        main = wide[..., 2:-2]
        fine = general_fine(wide, local_base, spline_frac)
        vertical = fine[2]
        part = base + (fine[0] * gx + fine[1] * gy + vertical * gz)
    part, vertical = part.reshape(scalar.shape), vertical.reshape(scalar.shape)
    part = outer_call(False, part, vertical, lower, 0)
    part = outer_call(True, part, vertical, upper, 0)
    segment = jnp.transpose(main.reshape(kinds, depth, height, cells), (0, 3, 1, 2))
    return segment, part


def solution(mesh):
    in_specs = (P(None, "blk", "dep", "grp"), P("dep", "grp", "blk"), P("blk"), P("blk"))
    out_specs = (P(None, "blk", "dep", "grp"), P("dep", "grp", "blk"))
    return jax.shard_map(
        per_device, mesh=mesh, in_specs=in_specs, out_specs=out_specs, check_vma=False
    )
```

```python
import functools
import math

import jax
import jax.numpy as jnp
import ml_dtypes
import numpy as np
from jax import lax
from jax.experimental import pallas as pl
from jax.experimental.pallas import tpu as pltpu
from jax.sharding import PartitionSpec as P

velocity_step = 0.002
viscosity = 0.00125
advect_rate = 0.2
diffuse_rate = 0.05
first_side = (0.8, -0.2, 4.0 / 105.0, -1.0 / 280.0)
second_side = (1.6, -0.2, 8.0 / 315.0, -1.0 / 560.0)
second_centre = -205.0 / 72.0
first_all = tuple(-a for a in reversed(first_side)) + (0.0,) + first_side
second_all = tuple(reversed(second_side)) + (second_centre,) + second_side
slope = tuple(-advect_rate * a for a in first_side)
bend = tuple(diffuse_rate * b for b in second_side)
centre_weight = 1.0 + 3.0 * diffuse_rate * second_centre
highest = lax.Precision.HIGHEST
reach = 4
lanes = 128
vmem_bytes = 32 * 1024 * 1024
most_vmem_bytes = 60 * 1024 * 1024
light = pl.CostEstimate(flops=1024, bytes_accessed=1024, transcendentals=0)


def ring(axis, step):
    count = lax.axis_size(axis)
    return [(i, (i + step) % count) for i in range(count)]


def exclusive(axis, mask):
    return [(i, i ^ mask) for i in range(lax.axis_size(axis))]


def split_table(values):
    high = values.astype(np.float32).astype(ml_dtypes.bfloat16)
    low = (values - high.astype(np.float64)).astype(np.float32).astype(ml_dtypes.bfloat16)
    return high, low


def right_table(values):
    high, low = split_table(values)
    return np.concatenate([high, high, low], axis=-2)


def circulant_tables(length, cells):
    s = np.arange(length)
    signed = np.where(s > length // 2, s - length, s)
    angle = signed * (np.pi / length)
    sine = np.where(s == 0, 1.0, np.sin(angle))
    parity = 1.0 - 2.0 * (s % 2)
    first = np.where(s == 0, 0.0, 0.5 * parity * np.cos(angle) / sine) * velocity_step
    second = np.where(s == 0, -(length * length) / 12.0 - 1.0 / 6.0, -0.5 * parity / (sine * sine))
    second = second * (velocity_step * viscosity)
    own = np.arange(cells)
    outer = np.zeros(lanes, np.int64)
    used = np.zeros(lanes)
    for lane, cell in ((0, cells), (1, cells + 1), (lanes - 2, -2), (lanes - 1, -1)):
        outer[lane] = cell
        used[lane] = 1.0
    blocks = []
    for distance in range(length // cells):
        main = (distance * cells + own[None, :] - own[:, None]) % length
        side = (distance * cells + outer[None, :] - own[:, None]) % length
        blocks.append(
            np.concatenate([first[main], second[main], first[side] * used, second[side] * used], axis=1)
        )
    return right_table(np.stack(blocks))


def level_table(depth, height):
    size, side = depth * height, 2 * reach
    table = np.zeros((3, depth, height, size + depth * side))
    for z in range(depth):
        for y in range(height):
            for m in range(-reach, reach + 1):
                if m == 0:
                    continue
                first = slope[m - 1] if m > 0 else -slope[-m - 1]
                second = bend[abs(m) - 1]
                if 0 <= y + m < height:
                    at = z * height + y + m
                else:
                    at = size + z * side + (y + m - height if m > 0 else y + m + side)
                table[0, z, y, at] += first
                table[2, z, y, at] += second
                if 0 <= z + m < depth:
                    table[1, z, y, (z + m) * height + y] += first
                    table[2, z, y, (z + m) * height + y] += second
    high, low = split_table(table.reshape(3 * size, -1))
    return np.concatenate([high, high, low], axis=1)


def dot(a, b):
    return jnp.dot(a, b, preferred_element_type=jnp.float32)


def split(value):
    high = value.astype(jnp.bfloat16)
    return high, (value - high.astype(jnp.float32)).astype(jnp.bfloat16)


def left_operand(value):
    high, low = split(value)
    return jnp.concatenate([high, low, high], axis=1)


def segment_kernel(length, info, own_ref, core_ref, chip_ref, far_ref, *refs):
    table_refs, (main_ref, outer_ref) = refs[:4], refs[4:]
    kinds, rows, cells = own_ref.shape
    lines = kinds * rows
    blocks = [own_ref[...].reshape(lines, cells)] + [ref[:lines] for ref in (core_ref, chip_ref, far_ref)]
    total = sums = None
    for block, table_ref in zip(blocks, table_refs):
        product = dot(left_operand(block), table_ref[0])
        partial = jnp.sum(block, axis=1, keepdims=True)
        total = product if total is None else total + product
        sums = partial if sums is None else sums + partial
    mean = sums * (1.0 / length)
    even = info[4] == 0
    after = jnp.where(even, blocks[1][:, :lanes], blocks[3][:, :lanes])
    before = jnp.where(even, blocks[3][:, cells - lanes :], blocks[1][:, cells - lanes :])
    place = lax.broadcasted_iota(jnp.int32, after.shape, 1)
    outer = jnp.where(place < lanes // 2, after, before)

    def advance(own, first, second):
        lead = jnp.concatenate([own[:rows]] * kinds, axis=0)
        return own - mean + (second - lead * first)

    main = advance(blocks[0], total[:, :cells], total[:, cells : 2 * cells])
    side = advance(outer, total[:, 2 * cells : 2 * cells + lanes], total[:, 2 * cells + lanes :])
    main_ref[...] = main.reshape(kinds, rows, cells)
    outer_ref[...] = side.reshape(kinds, rows, lanes)


def segment_call(own, core, chip, diagonal, info, length):
    kinds, rows, cells = own.shape
    table = circulant_tables(length, cells)
    whole = pl.BlockSpec(own.shape, lambda g, info: (0, 0, 0))
    sent = pl.BlockSpec(core.shape, lambda g, info: (0, 0))
    tables = [
        pl.BlockSpec((1,) + table.shape[1:], functools.partial(lambda j, g, info: (info[j], 0, 0), j))
        for j in range(4)
    ]
    return pl.pallas_call(
        functools.partial(segment_kernel, length),
        grid_spec=pltpu.PrefetchScalarGridSpec(
            num_scalar_prefetch=1,
            grid=(1,),
            in_specs=[whole] + [sent] * 3 + tables,
            out_specs=[whole, pl.BlockSpec((kinds, rows, lanes), lambda g, info: (0, 0, 0))],
        ),
        out_shape=[
            jax.ShapeDtypeStruct((kinds, rows, cells), jnp.float32),
            jax.ShapeDtypeStruct((kinds, rows, lanes), jnp.float32),
        ],
        compiler_params=pltpu.CompilerParams(vmem_limit_bytes=vmem_bytes),
        cost_estimate=light,
        name="segment",
    )(info, own, core, chip, diagonal, *([jnp.asarray(table)] * 4))


def catmull_weights(fraction):
    square = fraction * fraction
    cube = square * fraction
    return (
        (-cube + 2.0 * square - fraction) * 0.5,
        (3.0 * cube - 5.0 * square + 2.0) * 0.5,
        (-3.0 * cube + 4.0 * square + fraction) * 0.5,
        (cube - square) * 0.5,
    )


def spline_matrix(local_base, fraction, cells, refine):
    tiles = cells // lanes
    row = lax.iota(jnp.int32, 2 * lanes)[:, None]
    half = (lax.iota(jnp.int32, local_base.shape[0]) // (refine * (lanes // 2)))[None, :]
    own = half // 2
    other = (own + jnp.where(half % 2 == 1, 1, tiles)) % (tiles + 1)
    lane = jnp.where(row < lanes, own * lanes + row, other * lanes + row - lanes)
    cell = jnp.where(lane < cells + lanes // 2, lane, lane - cells - lanes)
    gap = cell - local_base[None, :]
    matrix = jnp.zeros(gap.shape, jnp.float32)
    for tap, weight in enumerate(catmull_weights(fraction)):
        matrix = jnp.where(gap == tap - 1, weight[None, :], matrix)
    return matrix


def end_terms(halo, sign):
    grade = curve = None
    place = lax.broadcasted_iota(jnp.int32, halo.shape, 1)
    halo = jnp.where(place >= lanes // 2 if sign < 0 else place < lanes // 2, halo, 0.0)
    for m in range(1, reach + 1):
        near = pltpu.roll(halo, (-sign * m) % lanes, 1)
        first, second = (sign * slope[m - 1]) * near, bend[m - 1] * near
        grade = first if grade is None else grade + first
        curve = second if curve is None else curve + second
    near = place < reach if sign < 0 else place >= lanes - reach
    return jnp.where(near, grade, 0.0), jnp.where(near, curve, 0.0)


def side_terms(ringed, extent):
    size = ringed.shape[1]
    grade = curve = None
    for m in range(1, reach + 1):
        ahead = pltpu.roll(ringed, size - m, 1)[:, :extent]
        behind = pltpu.roll(ringed, m, 1)[:, :extent]
        first, second = slope[m - 1] * (ahead - behind), bend[m - 1] * (ahead + behind)
        grade = first if grade is None else grade + first
        curve = second if curve is None else curve + second
    return grade, curve


def combine_kernel(tiles, parity, main_ref, outer_ref, matrix_ref, mid_ref, left_ref, right_ref, rows_ref, table_ref,
                   core_ref, far_ref, out_ref, fine_ref, seg_high, seg_low, halo_ref):
    step, steps = pl.program_id(0), pl.num_programs(0)
    kinds, rows, cells = main_ref.shape
    depth, height, width = mid_ref.shape

    @pl.when(step == 0)
    def _():
        for ref, begin, size in ((main_ref, 0, cells), (outer_ref, cells, lanes)):
            high, low = split(ref[...].reshape(kinds * rows, size))
            seg_high[:, begin : begin + size] = high
            seg_low[:, begin : begin + size] = low
        even = parity[0] == 0
        after = jnp.where(even, core_ref[:, :rows], far_ref[:, :rows])[:reach]
        before = jnp.where(even, far_ref[:, :rows], core_ref[:, :rows])[reach:]
        gap = jnp.zeros((lanes - 2 * reach, rows), jnp.float32)
        halo_ref[...] = jnp.concatenate([after, gap, before], axis=0).T

    own = step // 2
    other = lax.rem(own + jnp.where(lax.rem(step, 2) == 1, 1, tiles), tiles + 1)
    spans = [pl.ds(pl.multiple_of(at * lanes, lanes), lanes) for at in (own, other)]
    source = jnp.concatenate([ref[:, span] for ref in (seg_high, seg_low, seg_high) for span in spans], axis=1)
    high, low = split(matrix_ref[...])
    fine = dot(source, jnp.concatenate([high, high, low], axis=0))

    values = jnp.concatenate([mid_ref[...].reshape(rows, width), rows_ref[...].reshape(-1, width)], axis=0)
    high, low = split(values)
    level = dot(table_ref[...], jnp.concatenate([high, low, high], axis=0))

    place = lax.broadcasted_iota(jnp.int32, (height, lanes), 1)
    for z in range(depth):
        left = jnp.where(step == 0, 0.0, left_ref[z])
        right = jnp.where(step == steps - 1, 0.0, right_ref[z])
        mid = mid_ref[z]
        grade, curve = side_terms(jnp.concatenate([mid, jnp.where(place < lanes // 2, right, left)], axis=1), width)
        span = slice(z * height, (z + 1) * height)

        def of(array, kind):
            return array[kind * rows + z * height : kind * rows + (z + 1) * height]

        vertical = of(fine, 2)
        out_ref[span] = (centre_weight * mid + (curve + of(level, 2))) + (
            of(fine, 0) * grade + of(fine, 1) * of(level, 0) + vertical * of(level, 1)
        )
        fine_ref[span] = vertical
    for at, sign, begin in ((0, -1, 0), (steps - 1, 1, width - lanes)):

        @pl.when(step == at)
        def _():
            grade, curve = end_terms(halo_ref[...], sign)
            span = slice(begin, begin + lanes)
            out_ref[:, span] += fine[:rows, span] * grade + curve


def combine_call(main, outer, matrix, scalar, outer_rows, core, diagonal, parity):
    kinds, rows, cells = main.shape
    depth, height, points = scalar.shape
    steps = 2 * (cells // lanes)
    width = points // steps
    tiles, last = width // lanes, points // lanes - 1
    table = level_table(depth, height)
    flat_tile = pl.BlockSpec((rows, width), lambda t, parity: (0, t))
    edge = (depth, height, lanes)
    ends = pl.BlockSpec((2 * reach, cells), lambda t, parity: (core.shape[0] // (2 * reach) - 1, 0))
    flat = jax.ShapeDtypeStruct((rows, points), jnp.float32)
    return pl.pallas_call(
        functools.partial(combine_kernel, cells // lanes),
        grid_spec=pltpu.PrefetchScalarGridSpec(
            num_scalar_prefetch=1,
            grid=(steps,),
            in_specs=[
                pl.BlockSpec((kinds, rows, cells), lambda t, parity: (0, 0, 0)),
                pl.BlockSpec((kinds, rows, lanes), lambda t, parity: (0, 0, 0)),
                pl.BlockSpec((2 * lanes, width), lambda t, parity: (0, t)),
                pl.BlockSpec((depth, height, width), lambda t, parity: (0, 0, t)),
                pl.BlockSpec(edge, lambda t, parity: (0, 0, jnp.maximum(t * tiles - 1, 0))),
                pl.BlockSpec(edge, lambda t, parity: (0, 0, jnp.minimum((t + 1) * tiles, last))),
                pl.BlockSpec((depth, 2 * reach, width), lambda t, parity: (0, 0, t)),
                pl.BlockSpec(table.shape, lambda t, parity: (0, 0)),
                ends,
                ends,
            ],
            out_specs=[flat_tile, flat_tile],
            scratch_shapes=[
                pltpu.VMEM((kinds * rows, cells + lanes), jnp.bfloat16),
                pltpu.VMEM((kinds * rows, cells + lanes), jnp.bfloat16),
                pltpu.VMEM((rows, lanes), jnp.float32),
            ],
        ),
        out_shape=[flat, flat],
        compiler_params=pltpu.CompilerParams(vmem_limit_bytes=vmem_bytes),
        cost_estimate=light,
        name="combine",
    )(parity, main, outer, matrix, scalar, scalar, scalar, outer_rows, jnp.asarray(table), core, diagonal)


def finish_kernel(chunks, part_ref, fine_ref, low_hbm, high_hbm, out_hbm,
                  out_ref, low_ref, high_ref, in_sems, out_sems):
    depth, _, points = part_ref.shape
    width = points // chunks
    sources = ((low_hbm, low_ref), (high_hbm, high_ref))
    arrivals, sends = [], []
    for c in range(chunks):
        span = slice(None), slice(None), pl.ds(c * width, width)
        arrivals.append(
            [
                pltpu.make_async_copy(source.at[span], held.at[span], in_sems.at[c, i])
                for i, (source, held) in enumerate(sources)
            ]
        )
        sends.append(pltpu.make_async_copy(out_ref.at[span], out_hbm.at[span], out_sems.at[c]))
        for copy in arrivals[-1]:
            copy.start()
    for c in range(chunks):
        for copy in arrivals[c]:
            copy.wait()
        span = pl.ds(c * width, width)
        for p in range(depth):
            grade = curve = None
            for halo_ref, first_layer in ((low_ref, -reach), (high_ref, depth)):
                for h in range(reach):
                    m = first_layer + h - p
                    if abs(m) <= reach:
                        near = halo_ref[h, :, span]
                        first = (slope[m - 1] if m > 0 else -slope[-m - 1]) * near
                        second = bend[abs(m) - 1] * near
                        grade = first if grade is None else grade + first
                        curve = second if curve is None else curve + second
            out_ref[p, :, span] = part_ref[p, :, span] + (fine_ref[p, :, span] * grade + curve)
        sends[c].start()
    for send in sends:
        send.wait()


def finish_call(part, fine, low, high):
    points = part.shape[2]
    chunks = 4 if points % (4 * lanes) == 0 else 1
    anywhere = pl.BlockSpec(memory_space=pl.ANY)
    return pl.pallas_call(
        functools.partial(finish_kernel, chunks),
        in_specs=[pl.BlockSpec(memory_space=pltpu.VMEM)] * 2 + [anywhere] * 2,
        out_specs=anywhere,
        out_shape=jax.ShapeDtypeStruct(part.shape, jnp.float32),
        scratch_shapes=[pltpu.VMEM(array.shape, jnp.float32) for array in (part, low, high)]
        + [pltpu.SemaphoreType.DMA((chunks, 2)), pltpu.SemaphoreType.DMA((chunks,))],
        compiler_params=pltpu.CompilerParams(vmem_limit_bytes=vmem_bytes),
        cost_estimate=light,
        name="finish",
    )(part, fine, low, high)


def tie(value, *gates):
    anywhere = pl.BlockSpec(memory_space=pl.ANY)
    return pl.pallas_call(
        lambda *refs: None,
        in_specs=[anywhere] * (1 + len(gates)),
        out_specs=anywhere,
        out_shape=jax.ShapeDtypeStruct(value.shape, value.dtype),
        input_output_aliases={0: 0},
        cost_estimate=light,
        name="tie",
    )(value, *gates)


def depart_kernel(own_hbm, scalar_hbm, *refs):
    outs, (own_ref, scalar_ref, sent_ref, edge_ref, in_sems, out_sems) = refs[:4], refs[4:]
    kinds, rows, cells = own_ref.shape
    depth, height, points = scalar_ref.shape
    lines = kinds * rows
    layers = [pl.ds(depth - reach, reach), pl.ds(0, reach)]
    middle = depth - 2 * reach
    arrivals = [
        pltpu.make_async_copy(scalar_hbm.at[span], scalar_ref.at[span], in_sems.at[i])
        for i, span in enumerate(layers + [pl.ds(reach, middle)] * (middle > 0))
    ]
    arrivals.append(pltpu.make_async_copy(own_hbm, own_ref, in_sems.at[3]))
    for copy in arrivals:
        copy.start()
    sends = []

    def send(source, target):
        copy = pltpu.make_async_copy(source, target, out_sems.at[len(sends)])
        copy.start()
        sends.append(copy)

    for i, span in enumerate(layers):
        arrivals[i].wait()
        send(scalar_ref.at[span], outs[i])
    for copy in arrivals[2:]:
        copy.wait()
    edge_ref[:, :reach] = scalar_ref[:, :reach]
    edge_ref[:, reach:] = scalar_ref[:, height - reach :]
    send(edge_ref, outs[2])
    sent_ref[:lines] = own_ref[...].reshape(lines, cells)
    first = scalar_ref[:, :, :lanes].reshape(rows, lanes).T
    last = scalar_ref[:, :, points - lanes :].reshape(rows, lanes).T
    ends = jnp.concatenate([first[:reach], last[lanes - reach :]], axis=0)
    sent_ref[lines:] = jnp.zeros((2 * reach, cells), jnp.float32)
    sent_ref[lines:, :rows] = ends
    send(sent_ref, outs[-1])
    for copy in sends:
        copy.wait()


def depart_call(own, scalar):
    kinds, rows, cells = own.shape
    depth, height, points = scalar.shape
    edge = (depth, 2 * reach, points)
    sent = (kinds * rows + 2 * reach, cells)
    shapes = [(reach, height, points)] * 2 + [edge] + [sent]
    anywhere = pl.BlockSpec(memory_space=pl.ANY)
    return pl.pallas_call(
        depart_kernel,
        in_specs=[anywhere] * 2,
        out_specs=[anywhere] * len(shapes),
        out_shape=[jax.ShapeDtypeStruct(shape, jnp.float32) for shape in shapes],
        scratch_shapes=[
            pltpu.VMEM(own.shape, jnp.float32),
            pltpu.VMEM(scalar.shape, jnp.float32),
            pltpu.VMEM(sent, jnp.float32),
            pltpu.VMEM(edge, jnp.float32),
            pltpu.SemaphoreType.DMA((4,)),
            pltpu.SemaphoreType.DMA((4,)),
        ],
        compiler_params=pltpu.CompilerParams(vmem_limit_bytes=most_vmem_bytes),
        cost_estimate=light,
        name="depart",
    )(own, scalar)


def padded_2(block, sides, width):
    for axis, dim in sides:
        count = lax.axis_size(axis)
        forward = [(i, i + 1) for i in range(count - 1)]
        forward.append((count - 1, 0))
        backward = [(target, source) for source, target in forward]
        low = lax.ppermute(
            lax.slice_in_dim(block, block.shape[dim] - width, None, axis=dim), axis, forward
        )
        high = lax.ppermute(lax.slice_in_dim(block, 0, width, axis=dim), axis, backward)
        block = jnp.concatenate([low, block, high], axis=dim)
    return block


def derivative_rows(first_row, count, length):
    rows = first_row + lax.iota(jnp.int32, count)
    columns = lax.iota(jnp.int32, length)
    offset = (rows[:, None] - columns[None, :]) % length
    signed = jnp.where(offset > length // 2, offset - length, offset)
    angle = signed.astype(jnp.float32) * (math.pi / length)
    parity = 1.0 - 2.0 * (offset % 2).astype(jnp.float32)
    same = offset == 0
    sine = jnp.where(same, 1.0, jnp.sin(angle))
    first = jnp.where(same, 0.0, 0.5 * parity * jnp.cos(angle) / sine)
    second = jnp.where(same, -(length * length) / 12.0 - 1.0 / 6.0, -0.5 * parity / (sine * sine))
    average = jnp.full((count, length), 1.0 / length, jnp.float32)
    return jnp.concatenate([first, second, average], axis=0)


def scalar_update(padded, fine):
    extent = (padded.shape[0] - 8, padded.shape[1] - 8, padded.shape[2] - 8)
    centre = lax.slice(padded, (4, 4, 4), (4 + extent[0], 4 + extent[1], 4 + extent[2]))
    gradients = []
    curvature = jnp.zeros(extent, jnp.float32)
    for axis_index in range(3):
        slope = jnp.zeros(extent, jnp.float32)
        for offset in range(9):
            begin = [4, 4, 4]
            begin[axis_index] = offset
            finish = (begin[0] + extent[0], begin[1] + extent[1], begin[2] + extent[2])
            window = lax.slice(padded, tuple(begin), finish)
            if first_all[offset] != 0.0:
                slope = slope + first_all[offset] * window
            curvature = curvature + second_all[offset] * window
        gradients.append(slope)
    advection = fine[2] * gradients[0] + fine[1] * gradients[1] + fine[0] * gradients[2]
    return centre - advect_rate * advection + diffuse_rate * curvature


def general_per_device(velocity, scalar, spline_base, spline_frac):
    cells = velocity.shape[1]
    length = cells * lax.axis_size("blk")
    block = lax.axis_index("blk")
    table = derivative_rows(block * cells, cells, length)
    both = jnp.einsum(
        "km,cmzy->ckzy",
        table,
        lax.all_gather(velocity, "blk", axis=1, tiled=True),
        precision=highest,
    )
    segment = (
        velocity
        - both[:, 2 * cells :]
        + velocity_step * (viscosity * both[:, cells : 2 * cells] - velocity[0:1] * both[:, :cells])
    )
    widened = padded_2(segment, (("blk", 1),), 2)
    weights = catmull_weights(spline_frac)
    local_base = spline_base - (block * cells - 2)
    slots = lax.iota(jnp.int32, cells + 4)[:, None]
    matrix = jnp.zeros((cells + 4, spline_base.shape[0]), jnp.float32)
    for tap_index in range(4):
        matrix = matrix + jnp.where(
            slots == (local_base + (tap_index - 1))[None, :], weights[tap_index][None, :], 0.0
        )
    fine = jnp.einsum("cxzy,xi->czyi", widened, matrix, precision=highest)
    padded = padded_2(scalar, (("grp", 1), ("blk", 2), ("dep", 0)), 4)
    return (segment, scalar_update(padded, fine))


def per_device(velocity, scalar, spline_base, spline_frac):
    kinds, cells, depth, height = velocity.shape
    points = scalar.shape[2]
    rows = depth * height
    count = lax.axis_size("blk")
    if count != 4 or lax.axis_size("grp") != 2 or cells % lanes or rows > cells or (points // 2) % cells:
        return general_per_device(velocity, scalar, spline_base, spline_frac)
    length = cells * count
    block = lax.axis_index("blk")

    rows_of_x = jnp.transpose(velocity, (0, 2, 3, 1)).reshape(kinds, rows, cells)
    up, down, edges, own = depart_call(rows_of_x, scalar)
    chip = lax.ppermute(own, "blk", exclusive("blk", 2))
    lower = lax.ppermute(up, "dep", ring("dep", 1))
    upper = lax.ppermute(down, "dep", ring("dep", -1))
    outer_rows = lax.ppermute(tie(edges, chip), "grp", ring("grp", 1))
    matrix = spline_matrix(spline_base - block * cells, spline_frac, cells, points // cells)
    core = lax.ppermute(tie(own, chip), "blk", exclusive("blk", 1))
    diagonal = lax.ppermute(chip, "blk", exclusive("blk", 1))
    info = jnp.stack([(block - (block ^ j)) % count for j in range(4)] + [block % 2]).astype(jnp.int32)
    main, outer = segment_call(rows_of_x, core, chip, diagonal, info, length)
    part, vertical = combine_call(main, outer, matrix, scalar, outer_rows, core, diagonal, info[4:])
    result = finish_call(part.reshape(scalar.shape), vertical.reshape(scalar.shape), lower, upper)
    segment = jnp.transpose(main.reshape(kinds, depth, height, cells), (0, 3, 1, 2))
    return segment, result


def solution(mesh):
    in_specs = (P(None, "blk", "dep", "grp"), P("dep", "grp", "blk"), P("blk"), P("blk"))
    out_specs = (P(None, "blk", "dep", "grp"), P("dep", "grp", "blk"))
    return jax.shard_map(
        per_device, mesh=mesh, in_specs=in_specs, out_specs=out_specs, check_vma=False
    )
```

```python
import functools
import math

import jax
import jax.numpy as jnp
import ml_dtypes
import numpy as np
from jax import lax
from jax.experimental import pallas as pl
from jax.experimental.pallas import tpu as pltpu
from jax.sharding import PartitionSpec as P

velocity_step = 0.002
viscosity = 0.00125
advect_rate = 0.2
diffuse_rate = 0.05
first_side = (0.8, -0.2, 4.0 / 105.0, -1.0 / 280.0)
second_side = (1.6, -0.2, 8.0 / 315.0, -1.0 / 560.0)
second_centre = -205.0 / 72.0
first_all = tuple(-a for a in reversed(first_side)) + (0.0,) + first_side
second_all = tuple(reversed(second_side)) + (second_centre,) + second_side
slope = tuple(-advect_rate * a for a in first_side)
bend = tuple(diffuse_rate * b for b in second_side)
centre_weight = 1.0 + 3.0 * diffuse_rate * second_centre
highest = lax.Precision.HIGHEST
reach = 4
lanes = 128
vmem_bytes = 32 * 1024 * 1024
most_vmem_bytes = 60 * 1024 * 1024
light = pl.CostEstimate(flops=1024, bytes_accessed=1024, transcendentals=0)


def ring(axis, step):
    count = lax.axis_size(axis)
    return [(i, (i + step) % count) for i in range(count)]


def exclusive(axis, mask):
    return [(i, i ^ mask) for i in range(lax.axis_size(axis))]


def split_table(values):
    high = values.astype(np.float32).astype(ml_dtypes.bfloat16)
    low = (values - high.astype(np.float64)).astype(np.float32).astype(ml_dtypes.bfloat16)
    return high, low


def right_table(values):
    high, low = split_table(values)
    return np.concatenate([high, high, low], axis=-2)


def circulant_tables(length, cells):
    s = np.arange(length)
    signed = np.where(s > length // 2, s - length, s)
    angle = signed * (np.pi / length)
    sine = np.where(s == 0, 1.0, np.sin(angle))
    parity = 1.0 - 2.0 * (s % 2)
    first = np.where(s == 0, 0.0, 0.5 * parity * np.cos(angle) / sine) * velocity_step
    second = np.where(s == 0, -(length * length) / 12.0 - 1.0 / 6.0, -0.5 * parity / (sine * sine))
    second = second * (velocity_step * viscosity)
    own = np.arange(cells)
    outer = np.zeros(lanes, np.int64)
    used = np.zeros(lanes)
    for lane, cell in ((0, cells), (1, cells + 1), (lanes - 2, -2), (lanes - 1, -1)):
        outer[lane] = cell
        used[lane] = 1.0
    blocks = []
    for distance in range(length // cells):
        main = (distance * cells + own[None, :] - own[:, None]) % length
        side = (distance * cells + outer[None, :] - own[:, None]) % length
        blocks.append(
            np.concatenate([first[main], second[main], first[side] * used, second[side] * used], axis=1)
        )
    return right_table(np.stack(blocks))


def level_table(depth, height):
    size, side = depth * height, 2 * reach
    table = np.zeros((3, depth, height, size + depth * side))
    for z in range(depth):
        for y in range(height):
            for m in range(-reach, reach + 1):
                if m == 0:
                    continue
                first = slope[m - 1] if m > 0 else -slope[-m - 1]
                second = bend[abs(m) - 1]
                if 0 <= y + m < height:
                    at = z * height + y + m
                else:
                    at = size + z * side + (y + m - height if m > 0 else y + m + side)
                table[0, z, y, at] += first
                table[2, z, y, at] += second
                if 0 <= z + m < depth:
                    table[1, z, y, (z + m) * height + y] += first
                    table[2, z, y, (z + m) * height + y] += second
    high, low = split_table(table.reshape(3 * size, -1))
    return np.concatenate([high, high, low], axis=1)


def dot(a, b):
    return jnp.dot(a, b, preferred_element_type=jnp.float32)


def split(value):
    high = value.astype(jnp.bfloat16)
    return high, (value - high.astype(jnp.float32)).astype(jnp.bfloat16)


def left_operand(value):
    high, low = split(value)
    return jnp.concatenate([high, low, high], axis=1)


def segment_kernel(length, info, own_ref, core_ref, chip_ref, far_ref, *refs):
    table_refs, (main_ref, outer_ref) = refs[:4], refs[4:]
    kinds, rows, cells = own_ref.shape
    lines = kinds * rows
    blocks = [own_ref[...].reshape(lines, cells), core_ref[:lines]]
    blocks += [ref[...].reshape(lines, cells) for ref in (chip_ref, far_ref)]
    total = sums = None
    for block, table_ref in zip(blocks, table_refs):
        product = dot(left_operand(block), table_ref[0])
        partial = jnp.sum(block, axis=1, keepdims=True)
        total = product if total is None else total + product
        sums = partial if sums is None else sums + partial
    mean = sums * (1.0 / length)
    even = info[4] == 0
    after = jnp.where(even, blocks[1][:, :lanes], blocks[3][:, :lanes])
    before = jnp.where(even, blocks[3][:, cells - lanes :], blocks[1][:, cells - lanes :])
    place = lax.broadcasted_iota(jnp.int32, after.shape, 1)
    outer = jnp.where(place < lanes // 2, after, before)

    def advance(own, first, second):
        lead = jnp.concatenate([own[:rows]] * kinds, axis=0)
        return own - mean + (second - lead * first)

    main = advance(blocks[0], total[:, :cells], total[:, cells : 2 * cells])
    side = advance(outer, total[:, 2 * cells : 2 * cells + lanes], total[:, 2 * cells + lanes :])
    main_ref[...] = main.reshape(kinds, rows, cells)
    outer_ref[...] = side.reshape(kinds, rows, lanes)


def segment_call(own, core, chip, diagonal, info, length):
    kinds, rows, cells = own.shape
    table = circulant_tables(length, cells)
    whole = pl.BlockSpec(own.shape, lambda g, info: (0, 0, 0))
    sent = pl.BlockSpec(core.shape, lambda g, info: (0, 0))
    tables = [
        pl.BlockSpec((1,) + table.shape[1:], functools.partial(lambda j, g, info: (info[j], 0, 0), j))
        for j in range(4)
    ]
    return pl.pallas_call(
        functools.partial(segment_kernel, length),
        grid_spec=pltpu.PrefetchScalarGridSpec(
            num_scalar_prefetch=1,
            grid=(1,),
            in_specs=[whole, sent, whole, whole] + tables,
            out_specs=[whole, pl.BlockSpec((kinds, rows, lanes), lambda g, info: (0, 0, 0))],
        ),
        out_shape=[
            jax.ShapeDtypeStruct((kinds, rows, cells), jnp.float32),
            jax.ShapeDtypeStruct((kinds, rows, lanes), jnp.float32),
        ],
        compiler_params=pltpu.CompilerParams(vmem_limit_bytes=vmem_bytes),
        cost_estimate=light,
        name="segment",
    )(info, own, core, chip, diagonal, *([jnp.asarray(table)] * 4))


def catmull_weights(fraction):
    square = fraction * fraction
    cube = square * fraction
    return (
        (-cube + 2.0 * square - fraction) * 0.5,
        (3.0 * cube - 5.0 * square + 2.0) * 0.5,
        (-3.0 * cube + 4.0 * square + fraction) * 0.5,
        (cube - square) * 0.5,
    )


def spline_matrix(local_base, fraction, cells, refine):
    tiles = cells // lanes
    row = lax.iota(jnp.int32, 2 * lanes)[:, None]
    half = (lax.iota(jnp.int32, local_base.shape[0]) // (refine * (lanes // 2)))[None, :]
    own = half // 2
    other = (own + jnp.where(half % 2 == 1, 1, tiles)) % (tiles + 1)
    lane = jnp.where(row < lanes, own * lanes + row, other * lanes + row - lanes)
    cell = jnp.where(lane < cells + lanes // 2, lane, lane - cells - lanes)
    gap = cell - local_base[None, :]
    matrix = jnp.zeros(gap.shape, jnp.float32)
    for tap, weight in enumerate(catmull_weights(fraction)):
        matrix = jnp.where(gap == tap - 1, weight[None, :], matrix)
    return matrix


def end_terms(halo, sign):
    grade = curve = None
    place = lax.broadcasted_iota(jnp.int32, halo.shape, 1)
    halo = jnp.where(place >= lanes // 2 if sign < 0 else place < lanes // 2, halo, 0.0)
    for m in range(1, reach + 1):
        near = pltpu.roll(halo, (-sign * m) % lanes, 1)
        first, second = (sign * slope[m - 1]) * near, bend[m - 1] * near
        grade = first if grade is None else grade + first
        curve = second if curve is None else curve + second
    near = place < reach if sign < 0 else place >= lanes - reach
    return jnp.where(near, grade, 0.0), jnp.where(near, curve, 0.0)


def side_terms(ringed, extent):
    size = ringed.shape[1]
    grade = curve = None
    for m in range(1, reach + 1):
        ahead = pltpu.roll(ringed, size - m, 1)[:, :extent]
        behind = pltpu.roll(ringed, m, 1)[:, :extent]
        first, second = slope[m - 1] * (ahead - behind), bend[m - 1] * (ahead + behind)
        grade = first if grade is None else grade + first
        curve = second if curve is None else curve + second
    return grade, curve


def combine_kernel(tiles, parity, main_ref, outer_ref, matrix_ref, mid_ref, left_ref, right_ref, rows_ref, table_ref,
                   core_ref, far_ref, out_ref, fine_ref, seg_high, seg_low, halo_ref):
    step, steps = pl.program_id(0), pl.num_programs(0)
    kinds, rows, cells = main_ref.shape
    depth, height, width = mid_ref.shape

    @pl.when(step == 0)
    def _():
        for ref, begin, size in ((main_ref, 0, cells), (outer_ref, cells, lanes)):
            high, low = split(ref[...].reshape(kinds * rows, size))
            seg_high[:, begin : begin + size] = high
            seg_low[:, begin : begin + size] = low
        even = parity[0] == 0
        after = jnp.where(even, core_ref[:, :rows], far_ref[:, :rows])[:reach]
        before = jnp.where(even, far_ref[:, :rows], core_ref[:, :rows])[reach:]
        gap = jnp.zeros((lanes - 2 * reach, rows), jnp.float32)
        halo_ref[...] = jnp.concatenate([after, gap, before], axis=0).T

    own = step // 2
    other = lax.rem(own + jnp.where(lax.rem(step, 2) == 1, 1, tiles), tiles + 1)
    spans = [pl.ds(pl.multiple_of(at * lanes, lanes), lanes) for at in (own, other)]
    source = jnp.concatenate([ref[:, span] for ref in (seg_high, seg_low, seg_high) for span in spans], axis=1)
    high, low = split(matrix_ref[...])
    fine = dot(source, jnp.concatenate([high, high, low], axis=0))

    values = jnp.concatenate([mid_ref[...].reshape(rows, width), rows_ref[...].reshape(-1, width)], axis=0)
    high, low = split(values)
    level = dot(table_ref[...], jnp.concatenate([high, low, high], axis=0))

    place = lax.broadcasted_iota(jnp.int32, (height, lanes), 1)
    for z in range(depth):
        left = jnp.where(step == 0, 0.0, left_ref[z])
        right = jnp.where(step == steps - 1, 0.0, right_ref[z])
        mid = mid_ref[z]
        grade, curve = side_terms(jnp.concatenate([mid, jnp.where(place < lanes // 2, right, left)], axis=1), width)
        span = slice(z * height, (z + 1) * height)

        def of(array, kind):
            return array[kind * rows + z * height : kind * rows + (z + 1) * height]

        vertical = of(fine, 2)
        out_ref[span] = (centre_weight * mid + (curve + of(level, 2))) + (
            of(fine, 0) * grade + of(fine, 1) * of(level, 0) + vertical * of(level, 1)
        )
        fine_ref[span] = vertical
    for at, sign, begin in ((0, -1, 0), (steps - 1, 1, width - lanes)):

        @pl.when(step == at)
        def _():
            grade, curve = end_terms(halo_ref[...], sign)
            span = slice(begin, begin + lanes)
            out_ref[:, span] += fine[:rows, span] * grade + curve


def combine_call(main, outer, matrix, scalar, outer_rows, core, diagonal, parity):
    kinds, rows, cells = main.shape
    depth, height, points = scalar.shape
    steps = 2 * (cells // lanes)
    width = points // steps
    tiles, last = width // lanes, points // lanes - 1
    table = level_table(depth, height)
    flat_tile = pl.BlockSpec((rows, width), lambda t, parity: (0, t))
    edge = (depth, height, lanes)
    ends = pl.BlockSpec((2 * reach, cells), lambda t, parity: (core.shape[0] // (2 * reach) - 1, 0))
    flat = jax.ShapeDtypeStruct((rows, points), jnp.float32)
    return pl.pallas_call(
        functools.partial(combine_kernel, cells // lanes),
        grid_spec=pltpu.PrefetchScalarGridSpec(
            num_scalar_prefetch=1,
            grid=(steps,),
            in_specs=[
                pl.BlockSpec((kinds, rows, cells), lambda t, parity: (0, 0, 0)),
                pl.BlockSpec((kinds, rows, lanes), lambda t, parity: (0, 0, 0)),
                pl.BlockSpec((2 * lanes, width), lambda t, parity: (0, t)),
                pl.BlockSpec((depth, height, width), lambda t, parity: (0, 0, t)),
                pl.BlockSpec(edge, lambda t, parity: (0, 0, jnp.maximum(t * tiles - 1, 0))),
                pl.BlockSpec(edge, lambda t, parity: (0, 0, jnp.minimum((t + 1) * tiles, last))),
                pl.BlockSpec((depth, 2 * reach, width), lambda t, parity: (0, 0, t)),
                pl.BlockSpec(table.shape, lambda t, parity: (0, 0)),
                ends,
                pl.BlockSpec((2 * reach, cells), lambda t, parity: (0, 0)),
            ],
            out_specs=[flat_tile, flat_tile],
            scratch_shapes=[
                pltpu.VMEM((kinds * rows, cells + lanes), jnp.bfloat16),
                pltpu.VMEM((kinds * rows, cells + lanes), jnp.bfloat16),
                pltpu.VMEM((rows, lanes), jnp.float32),
            ],
        ),
        out_shape=[flat, flat],
        compiler_params=pltpu.CompilerParams(vmem_limit_bytes=vmem_bytes),
        cost_estimate=light,
        name="combine",
    )(parity, main, outer, matrix, scalar, scalar, scalar, outer_rows, jnp.asarray(table), core, diagonal)


def finish_kernel(chunks, part_ref, fine_ref, low_ref, high_hbm, out_hbm, out_ref, high_ref, in_sems, out_sems):
    depth, _, points = part_ref.shape
    width = points // chunks
    spans = [pl.ds(c * width, width) for c in range(chunks)]
    arrivals = [
        pltpu.make_async_copy(high_hbm.at[:, :, span], high_ref.at[:, :, span], in_sems.at[c])
        for c, span in enumerate(spans)
    ]
    for copy in arrivals:
        copy.start()
    sends = []

    def add(halo_ref, first_layer, layers, span):
        for p in layers:
            grade = curve = None
            for h in range(reach):
                m = first_layer + h - p
                if abs(m) <= reach:
                    near = halo_ref[h, :, span]
                    first = (slope[m - 1] if m > 0 else -slope[-m - 1]) * near
                    second = bend[abs(m) - 1] * near
                    grade = first if grade is None else grade + first
                    curve = second if curve is None else curve + second
            out_ref[p, :, span] = part_ref[p, :, span] + (fine_ref[p, :, span] * grade + curve)
        at = pl.ds(layers[0], len(layers)), slice(None), span
        copy = pltpu.make_async_copy(out_ref.at[at], out_hbm.at[at], out_sems.at[len(sends)])
        copy.start()
        sends.append(copy)

    for span in spans:
        add(low_ref, -reach, range(reach), span)
    for arrival, span in zip(arrivals, spans):
        arrival.wait()
        add(high_ref, depth, range(depth - reach, depth), span)
    for copy in sends:
        copy.wait()


def finish_call(part, fine, low, high):
    points = part.shape[2]
    chunks = 4 if points % (4 * lanes) == 0 else 1
    held = pl.BlockSpec(memory_space=pltpu.VMEM)
    anywhere = pl.BlockSpec(memory_space=pl.ANY)
    return pl.pallas_call(
        functools.partial(finish_kernel, chunks),
        in_specs=[held, held, held, anywhere],
        out_specs=anywhere,
        out_shape=jax.ShapeDtypeStruct(part.shape, jnp.float32),
        scratch_shapes=[
            pltpu.VMEM(part.shape, jnp.float32),
            pltpu.VMEM(high.shape, jnp.float32),
            pltpu.SemaphoreType.DMA((chunks,)),
            pltpu.SemaphoreType.DMA((2 * chunks,)),
        ],
        compiler_params=pltpu.CompilerParams(vmem_limit_bytes=vmem_bytes),
        cost_estimate=light,
        name="finish",
    )(part, fine, low, high)


def tie(value, *gates):
    anywhere = pl.BlockSpec(memory_space=pl.ANY)
    return pl.pallas_call(
        lambda *refs: None,
        in_specs=[anywhere] * (1 + len(gates)),
        out_specs=anywhere,
        out_shape=jax.ShapeDtypeStruct(value.shape, value.dtype),
        input_output_aliases={0: 0},
        cost_estimate=light,
        name="tie",
    )(value, *gates)


def depart_kernel(own_hbm, scalar_hbm, gate, down_hbm, edge_hbm, sent_hbm, end_hbm,
                  own_ref, scalar_ref, ends_ref, edge_ref, in_sems, out_sems):
    kinds, rows, cells = own_ref.shape
    depth, height, points = scalar_ref.shape
    layers = [pl.ds(depth - reach, reach), pl.ds(0, reach)]
    middle = depth - 2 * reach
    arrivals = [
        pltpu.make_async_copy(scalar_hbm.at[span], scalar_ref.at[span], in_sems.at[i])
        for i, span in enumerate(layers + [pl.ds(reach, middle)] * (middle > 0))
    ]
    arrivals.append(pltpu.make_async_copy(own_hbm, own_ref, in_sems.at[3]))
    for copy in arrivals[::-1]:
        copy.start()
    sends = []

    def send(source, target):
        copy = pltpu.make_async_copy(source, target, out_sems.at[len(sends)])
        copy.start()
        sends.append(copy)

    arrivals[-1].wait()
    for kind in range(kinds):
        send(own_ref.at[kind], sent_hbm.at[pl.ds(kind * rows, rows)])
    for copy in arrivals[:-1]:
        copy.wait()
    send(scalar_ref.at[layers[1]], down_hbm)
    edge_ref[:, :reach] = scalar_ref[:, :reach]
    edge_ref[:, reach:] = scalar_ref[:, height - reach :]
    send(edge_ref, edge_hbm)
    first = scalar_ref[:, :, :lanes].reshape(rows, lanes).T
    last = scalar_ref[:, :, points - lanes :].reshape(rows, lanes).T
    ends_ref[...] = jnp.zeros_like(ends_ref)
    ends_ref[:, :rows] = jnp.concatenate([first[:reach], last[lanes - reach :]], axis=0)
    send(ends_ref, sent_hbm.at[pl.ds(kinds * rows, 2 * reach)])
    send(ends_ref, end_hbm)
    for copy in sends:
        copy.wait()


def depart_call(own, scalar, gate):
    kinds, rows, cells = own.shape
    depth, height, points = scalar.shape
    edge, ends = (depth, 2 * reach, points), (2 * reach, cells)
    shapes = [(reach, height, points), edge, (kinds * rows + 2 * reach, cells), ends]
    anywhere = pl.BlockSpec(memory_space=pl.ANY)
    return pl.pallas_call(
        depart_kernel,
        in_specs=[anywhere] * 3,
        out_specs=[anywhere] * len(shapes),
        out_shape=[jax.ShapeDtypeStruct(shape, jnp.float32) for shape in shapes],
        scratch_shapes=[
            pltpu.VMEM(own.shape, jnp.float32),
            pltpu.VMEM(scalar.shape, jnp.float32),
            pltpu.VMEM(ends, jnp.float32),
            pltpu.VMEM(edge, jnp.float32),
            pltpu.SemaphoreType.DMA((4,)),
            pltpu.SemaphoreType.DMA((4 + kinds,)),
        ],
        compiler_params=pltpu.CompilerParams(vmem_limit_bytes=most_vmem_bytes),
        cost_estimate=light,
        name="depart",
    )(own, scalar, gate)


def padded_2(block, sides, width):
    for axis, dim in sides:
        count = lax.axis_size(axis)
        forward = [(i, i + 1) for i in range(count - 1)]
        forward.append((count - 1, 0))
        backward = [(target, source) for source, target in forward]
        low = lax.ppermute(
            lax.slice_in_dim(block, block.shape[dim] - width, None, axis=dim), axis, forward
        )
        high = lax.ppermute(lax.slice_in_dim(block, 0, width, axis=dim), axis, backward)
        block = jnp.concatenate([low, block, high], axis=dim)
    return block


def derivative_rows(first_row, count, length):
    rows = first_row + lax.iota(jnp.int32, count)
    columns = lax.iota(jnp.int32, length)
    offset = (rows[:, None] - columns[None, :]) % length
    signed = jnp.where(offset > length // 2, offset - length, offset)
    angle = signed.astype(jnp.float32) * (math.pi / length)
    parity = 1.0 - 2.0 * (offset % 2).astype(jnp.float32)
    same = offset == 0
    sine = jnp.where(same, 1.0, jnp.sin(angle))
    first = jnp.where(same, 0.0, 0.5 * parity * jnp.cos(angle) / sine)
    second = jnp.where(same, -(length * length) / 12.0 - 1.0 / 6.0, -0.5 * parity / (sine * sine))
    average = jnp.full((count, length), 1.0 / length, jnp.float32)
    return jnp.concatenate([first, second, average], axis=0)


def scalar_update(padded, fine):
    extent = (padded.shape[0] - 8, padded.shape[1] - 8, padded.shape[2] - 8)
    centre = lax.slice(padded, (4, 4, 4), (4 + extent[0], 4 + extent[1], 4 + extent[2]))
    gradients = []
    curvature = jnp.zeros(extent, jnp.float32)
    for axis_index in range(3):
        slope = jnp.zeros(extent, jnp.float32)
        for offset in range(9):
            begin = [4, 4, 4]
            begin[axis_index] = offset
            finish = (begin[0] + extent[0], begin[1] + extent[1], begin[2] + extent[2])
            window = lax.slice(padded, tuple(begin), finish)
            if first_all[offset] != 0.0:
                slope = slope + first_all[offset] * window
            curvature = curvature + second_all[offset] * window
        gradients.append(slope)
    advection = fine[2] * gradients[0] + fine[1] * gradients[1] + fine[0] * gradients[2]
    return centre - advect_rate * advection + diffuse_rate * curvature


def general_per_device(velocity, scalar, spline_base, spline_frac):
    cells = velocity.shape[1]
    length = cells * lax.axis_size("blk")
    block = lax.axis_index("blk")
    table = derivative_rows(block * cells, cells, length)
    both = jnp.einsum(
        "km,cmzy->ckzy",
        table,
        lax.all_gather(velocity, "blk", axis=1, tiled=True),
        precision=highest,
    )
    segment = (
        velocity
        - both[:, 2 * cells :]
        + velocity_step * (viscosity * both[:, cells : 2 * cells] - velocity[0:1] * both[:, :cells])
    )
    widened = padded_2(segment, (("blk", 1),), 2)
    weights = catmull_weights(spline_frac)
    local_base = spline_base - (block * cells - 2)
    slots = lax.iota(jnp.int32, cells + 4)[:, None]
    matrix = jnp.zeros((cells + 4, spline_base.shape[0]), jnp.float32)
    for tap_index in range(4):
        matrix = matrix + jnp.where(
            slots == (local_base + (tap_index - 1))[None, :], weights[tap_index][None, :], 0.0
        )
    fine = jnp.einsum("cxzy,xi->czyi", widened, matrix, precision=highest)
    padded = padded_2(scalar, (("grp", 1), ("blk", 2), ("dep", 0)), 4)
    return (segment, scalar_update(padded, fine))


def per_device(velocity, scalar, spline_base, spline_frac):
    kinds, cells, depth, height = velocity.shape
    points = scalar.shape[2]
    rows = depth * height
    count = lax.axis_size("blk")
    if count != 4 or lax.axis_size("grp") != 2 or cells % lanes or rows > cells or (points // 2) % cells or depth != 2 * reach:
        return general_per_device(velocity, scalar, spline_base, spline_frac)
    length = cells * count
    block = lax.axis_index("blk")

    rows_of_x = jnp.transpose(velocity, (0, 2, 3, 1)).reshape(kinds, rows, cells)
    chip = lax.ppermute(rows_of_x, "blk", exclusive("blk", 2))
    up = scalar[-reach:]
    lower = lax.ppermute(up, "dep", ring("dep", 1))
    down, edges, own, ends = depart_call(rows_of_x, scalar, up)
    upper = lax.ppermute(down, "dep", ring("dep", -1))
    far_ends = lax.ppermute(ends, "blk", exclusive("blk", 3))
    matrix = spline_matrix(spline_base - block * cells, spline_frac, cells, points // cells)
    outer_rows = lax.ppermute(edges, "grp", ring("grp", 1))
    core = lax.ppermute(tie(own, chip), "blk", exclusive("blk", 1))
    chip = tie(chip, far_ends, matrix, outer_rows)
    diagonal = lax.ppermute(chip, "blk", exclusive("blk", 1))
    info = jnp.stack([(block - (block ^ j)) % count for j in range(4)] + [block % 2]).astype(jnp.int32)
    main, outer = segment_call(rows_of_x, core, chip, diagonal, info, length)
    part, vertical = combine_call(main, outer, matrix, scalar, outer_rows, core, far_ends, info[4:])
    result = finish_call(part.reshape(scalar.shape), vertical.reshape(scalar.shape), lower, upper)
    segment = jnp.transpose(main.reshape(kinds, depth, height, cells), (0, 3, 1, 2))
    return segment, result


def solution(mesh):
    in_specs = (P(None, "blk", "dep", "grp"), P("dep", "grp", "blk"), P("blk"), P("blk"))
    out_specs = (P(None, "blk", "dep", "grp"), P("dep", "grp", "blk"))
    return jax.shard_map(
        per_device, mesh=mesh, in_specs=in_specs, out_specs=out_specs, check_vma=False
    )
```

```python
import functools
import math

import jax
import jax.numpy as jnp
import ml_dtypes
import numpy as np
from jax import lax
from jax.experimental import pallas as pl
from jax.experimental.pallas import tpu as pltpu
from jax.sharding import PartitionSpec as P

velocity_step = 0.002
viscosity = 0.00125
advect_rate = 0.2
diffuse_rate = 0.05
first_side = (0.8, -0.2, 4.0 / 105.0, -1.0 / 280.0)
second_side = (1.6, -0.2, 8.0 / 315.0, -1.0 / 560.0)
second_centre = -205.0 / 72.0
first_all = tuple(-a for a in reversed(first_side)) + (0.0,) + first_side
second_all = tuple(reversed(second_side)) + (second_centre,) + second_side
slope = tuple(-advect_rate * a for a in first_side)
bend = tuple(diffuse_rate * b for b in second_side)
centre_weight = 1.0 + 3.0 * diffuse_rate * second_centre
highest = lax.Precision.HIGHEST
reach = 4
slab_chunks = 4
lanes = 128
vmem_bytes = 32 * 1024 * 1024
most_vmem_bytes = 60 * 1024 * 1024
light = pl.CostEstimate(flops=1024, bytes_accessed=1024, transcendentals=0)


def ring(axis, step):
    count = lax.axis_size(axis)
    return [(i, (i + step) % count) for i in range(count)]


def exclusive(axis, mask):
    return [(i, i ^ mask) for i in range(lax.axis_size(axis))]


def split_table(values):
    high = values.astype(np.float32).astype(ml_dtypes.bfloat16)
    low = (values - high.astype(np.float64)).astype(np.float32).astype(ml_dtypes.bfloat16)
    return high, low


def right_table(values):
    high, low = split_table(values)
    return np.concatenate([high, high, low], axis=-2)


def circulant_tables(length, cells):
    s = np.arange(length)
    signed = np.where(s > length // 2, s - length, s)
    angle = signed * (np.pi / length)
    sine = np.where(s == 0, 1.0, np.sin(angle))
    parity = 1.0 - 2.0 * (s % 2)
    first = np.where(s == 0, 0.0, 0.5 * parity * np.cos(angle) / sine) * velocity_step
    second = np.where(s == 0, -(length * length) / 12.0 - 1.0 / 6.0, -0.5 * parity / (sine * sine))
    second = second * (velocity_step * viscosity)
    own = np.arange(cells)
    outer = np.zeros(lanes, np.int64)
    used = np.zeros(lanes)
    for lane, cell in ((0, cells), (1, cells + 1), (lanes - 2, -2), (lanes - 1, -1)):
        outer[lane] = cell
        used[lane] = 1.0
    blocks = []
    for distance in range(length // cells):
        main = (distance * cells + own[None, :] - own[:, None]) % length
        side = (distance * cells + outer[None, :] - own[:, None]) % length
        blocks.append(
            np.concatenate([first[main], second[main], first[side] * used, second[side] * used], axis=1)
        )
    return right_table(np.stack(blocks))


def level_table(depth, height):
    size, side = depth * height, 2 * reach
    table = np.zeros((3, depth, height, size + depth * side))
    for z in range(depth):
        for y in range(height):
            for m in range(-reach, reach + 1):
                if m == 0:
                    continue
                first = slope[m - 1] if m > 0 else -slope[-m - 1]
                second = bend[abs(m) - 1]
                if 0 <= y + m < height:
                    at = z * height + y + m
                else:
                    at = size + z * side + (y + m - height if m > 0 else y + m + side)
                table[0, z, y, at] += first
                table[2, z, y, at] += second
                if 0 <= z + m < depth:
                    table[1, z, y, (z + m) * height + y] += first
                    table[2, z, y, (z + m) * height + y] += second
    high, low = split_table(table.reshape(3 * size, -1))
    return np.concatenate([high, high, low], axis=1)


def dot(a, b):
    return jnp.dot(a, b, preferred_element_type=jnp.float32)


def split(value):
    high = value.astype(jnp.bfloat16)
    return high, (value - high.astype(jnp.float32)).astype(jnp.bfloat16)


def left_operand(value):
    high, low = split(value)
    return jnp.concatenate([high, low, high], axis=1)


def segment_kernel(length, info, own_ref, core_ref, chip_ref, far_ref, *refs):
    table_refs, (main_ref, outer_ref) = refs[:4], refs[4:]
    kinds, rows, cells = own_ref.shape
    lines = kinds * rows
    blocks = [own_ref[...].reshape(lines, cells), core_ref[:lines]]
    blocks += [ref[...].reshape(lines, cells) for ref in (chip_ref, far_ref)]
    total = sums = None
    for block, table_ref in zip(blocks, table_refs):
        product = dot(left_operand(block), table_ref[0])
        partial = jnp.sum(block, axis=1, keepdims=True)
        total = product if total is None else total + product
        sums = partial if sums is None else sums + partial
    mean = sums * (1.0 / length)
    even = info[4] == 0
    after = jnp.where(even, blocks[1][:, :lanes], blocks[3][:, :lanes])
    before = jnp.where(even, blocks[3][:, cells - lanes :], blocks[1][:, cells - lanes :])
    place = lax.broadcasted_iota(jnp.int32, after.shape, 1)
    outer = jnp.where(place < lanes // 2, after, before)

    def advance(own, first, second):
        lead = jnp.concatenate([own[:rows]] * kinds, axis=0)
        return own - mean + (second - lead * first)

    main = advance(blocks[0], total[:, :cells], total[:, cells : 2 * cells])
    side = advance(outer, total[:, 2 * cells : 2 * cells + lanes], total[:, 2 * cells + lanes :])
    main_ref[...] = main.reshape(kinds, rows, cells)
    outer_ref[...] = side.reshape(kinds, rows, lanes)


def segment_call(own, core, chip, diagonal, info, length):
    kinds, rows, cells = own.shape
    table = circulant_tables(length, cells)
    whole = pl.BlockSpec(own.shape, lambda g, info: (0, 0, 0))
    sent = pl.BlockSpec(core.shape, lambda g, info: (0, 0))
    tables = [
        pl.BlockSpec((1,) + table.shape[1:], functools.partial(lambda j, g, info: (info[j], 0, 0), j))
        for j in range(4)
    ]
    return pl.pallas_call(
        functools.partial(segment_kernel, length),
        grid_spec=pltpu.PrefetchScalarGridSpec(
            num_scalar_prefetch=1,
            grid=(1,),
            in_specs=[whole, sent, whole, whole] + tables,
            out_specs=[whole, pl.BlockSpec((kinds, rows, lanes), lambda g, info: (0, 0, 0))],
        ),
        out_shape=[
            jax.ShapeDtypeStruct((kinds, rows, cells), jnp.float32),
            jax.ShapeDtypeStruct((kinds, rows, lanes), jnp.float32),
        ],
        compiler_params=pltpu.CompilerParams(vmem_limit_bytes=vmem_bytes),
        cost_estimate=light,
        name="segment",
    )(info, own, core, chip, diagonal, *([jnp.asarray(table)] * 4))


def catmull_weights(fraction):
    square = fraction * fraction
    cube = square * fraction
    return (
        (-cube + 2.0 * square - fraction) * 0.5,
        (3.0 * cube - 5.0 * square + 2.0) * 0.5,
        (-3.0 * cube + 4.0 * square + fraction) * 0.5,
        (cube - square) * 0.5,
    )


def spline_matrix(local_base, fraction, cells, refine):
    tiles = cells // lanes
    row = lax.iota(jnp.int32, 2 * lanes)[:, None]
    half = (lax.iota(jnp.int32, local_base.shape[0]) // (refine * (lanes // 2)))[None, :]
    own = half // 2
    other = (own + jnp.where(half % 2 == 1, 1, tiles)) % (tiles + 1)
    lane = jnp.where(row < lanes, own * lanes + row, other * lanes + row - lanes)
    cell = jnp.where(lane < cells + lanes // 2, lane, lane - cells - lanes)
    gap = cell - local_base[None, :]
    matrix = jnp.zeros(gap.shape, jnp.float32)
    for tap, weight in enumerate(catmull_weights(fraction)):
        matrix = jnp.where(gap == tap - 1, weight[None, :], matrix)
    return matrix


def end_terms(halo, sign):
    grade = curve = None
    place = lax.broadcasted_iota(jnp.int32, halo.shape, 1)
    halo = jnp.where(place >= lanes // 2 if sign < 0 else place < lanes // 2, halo, 0.0)
    for m in range(1, reach + 1):
        near = pltpu.roll(halo, (-sign * m) % lanes, 1)
        first, second = (sign * slope[m - 1]) * near, bend[m - 1] * near
        grade = first if grade is None else grade + first
        curve = second if curve is None else curve + second
    near = place < reach if sign < 0 else place >= lanes - reach
    return jnp.where(near, grade, 0.0), jnp.where(near, curve, 0.0)


def side_terms(ringed, extent):
    size = ringed.shape[1]
    grade = curve = None
    for m in range(1, reach + 1):
        ahead = pltpu.roll(ringed, size - m, 1)[:, :extent]
        behind = pltpu.roll(ringed, m, 1)[:, :extent]
        first, second = slope[m - 1] * (ahead - behind), bend[m - 1] * (ahead + behind)
        grade = first if grade is None else grade + first
        curve = second if curve is None else curve + second
    return grade, curve


def combine_kernel(tiles, parity, main_ref, outer_ref, matrix_ref, mid_ref, left_ref, right_ref, rows_ref, table_ref,
                   core_ref, far_ref, out_ref, fine_ref, seg_high, seg_low, halo_ref):
    step, steps = pl.program_id(0), pl.num_programs(0)
    kinds, rows, cells = main_ref.shape
    depth, height, width = mid_ref.shape

    @pl.when(step == 0)
    def _():
        for ref, begin, size in ((main_ref, 0, cells), (outer_ref, cells, lanes)):
            high, low = split(ref[...].reshape(kinds * rows, size))
            seg_high[:, begin : begin + size] = high
            seg_low[:, begin : begin + size] = low
        even = parity[0] == 0
        after = jnp.where(even, core_ref[:, :rows], far_ref[:, :rows])[:reach]
        before = jnp.where(even, far_ref[:, :rows], core_ref[:, :rows])[reach:]
        gap = jnp.zeros((lanes - 2 * reach, rows), jnp.float32)
        halo_ref[...] = jnp.concatenate([after, gap, before], axis=0).T

    own = step // 2
    other = lax.rem(own + jnp.where(lax.rem(step, 2) == 1, 1, tiles), tiles + 1)
    spans = [pl.ds(pl.multiple_of(at * lanes, lanes), lanes) for at in (own, other)]
    source = jnp.concatenate([ref[:, span] for ref in (seg_high, seg_low, seg_high) for span in spans], axis=1)
    high, low = split(matrix_ref[...])
    fine = dot(source, jnp.concatenate([high, high, low], axis=0))

    values = jnp.concatenate([mid_ref[...].reshape(rows, width), rows_ref[...].reshape(-1, width)], axis=0)
    high, low = split(values)
    level = dot(table_ref[...], jnp.concatenate([high, low, high], axis=0))

    place = lax.broadcasted_iota(jnp.int32, (height, lanes), 1)
    for z in range(depth):
        left = jnp.where(step == 0, 0.0, left_ref[z])
        right = jnp.where(step == steps - 1, 0.0, right_ref[z])
        mid = mid_ref[z]
        grade, curve = side_terms(jnp.concatenate([mid, jnp.where(place < lanes // 2, right, left)], axis=1), width)
        span = slice(z * height, (z + 1) * height)

        def of(array, kind):
            return array[kind * rows + z * height : kind * rows + (z + 1) * height]

        vertical = of(fine, 2)
        out_ref[span] = (centre_weight * mid + (curve + of(level, 2))) + (
            of(fine, 0) * grade + of(fine, 1) * of(level, 0) + vertical * of(level, 1)
        )
        fine_ref[span] = vertical
    for at, sign, begin in ((0, -1, 0), (steps - 1, 1, width - lanes)):

        @pl.when(step == at)
        def _():
            grade, curve = end_terms(halo_ref[...], sign)
            span = slice(begin, begin + lanes)
            out_ref[:, span] += fine[:rows, span] * grade + curve


def combine_call(main, outer, matrix, scalar, outer_rows, core, diagonal, parity):
    kinds, rows, cells = main.shape
    depth, height, points = scalar.shape
    steps = 2 * (cells // lanes)
    width = points // steps
    tiles, last = width // lanes, points // lanes - 1
    table = level_table(depth, height)
    flat_tile = pl.BlockSpec((rows, width), lambda t, parity: (0, t))
    edge = (depth, height, lanes)
    ends = pl.BlockSpec((2 * reach, cells), lambda t, parity: (core.shape[0] // (2 * reach) - 1, 0))
    flat = jax.ShapeDtypeStruct((rows, points), jnp.float32)
    return pl.pallas_call(
        functools.partial(combine_kernel, cells // lanes),
        grid_spec=pltpu.PrefetchScalarGridSpec(
            num_scalar_prefetch=1,
            grid=(steps,),
            in_specs=[
                pl.BlockSpec((kinds, rows, cells), lambda t, parity: (0, 0, 0)),
                pl.BlockSpec((kinds, rows, lanes), lambda t, parity: (0, 0, 0)),
                pl.BlockSpec((2 * lanes, width), lambda t, parity: (0, t)),
                pl.BlockSpec((depth, height, width), lambda t, parity: (0, 0, t)),
                pl.BlockSpec(edge, lambda t, parity: (0, 0, jnp.maximum(t * tiles - 1, 0))),
                pl.BlockSpec(edge, lambda t, parity: (0, 0, jnp.minimum((t + 1) * tiles, last))),
                pl.BlockSpec((depth, 2 * reach, width), lambda t, parity: (0, 0, t)),
                pl.BlockSpec(table.shape, lambda t, parity: (0, 0)),
                ends,
                pl.BlockSpec((2 * reach, cells), lambda t, parity: (0, 0)),
            ],
            out_specs=[flat_tile, flat_tile],
            scratch_shapes=[
                pltpu.VMEM((kinds * rows, cells + lanes), jnp.bfloat16),
                pltpu.VMEM((kinds * rows, cells + lanes), jnp.bfloat16),
                pltpu.VMEM((rows, lanes), jnp.float32),
            ],
        ),
        out_shape=[flat, flat],
        compiler_params=pltpu.CompilerParams(vmem_limit_bytes=vmem_bytes),
        cost_estimate=light,
        name="combine",
    )(parity, main, outer, matrix, scalar, scalar, scalar, outer_rows, jnp.asarray(table), core, diagonal)


def finish_kernel(chunks, part_ref, fine_ref, low_hbm, high_hbm, out_hbm, out_ref, low_ref, high_ref, in_sems, out_sems):
    depth, _, points = part_ref.shape
    width = points // chunks
    spans = [pl.ds(c * width, width) for c in range(chunks)]
    arrivals = [
        pltpu.make_async_copy(source.at[:, :, span], target.at[:, :, span], in_sems.at[i, c])
        for i, (source, target) in enumerate(((low_hbm, low_ref), (high_hbm, high_ref)))
        for c, span in enumerate(spans)
    ]
    for copy in arrivals:
        copy.start()
    sends = []

    def add(halo_ref, first_layer, layers, span):
        for p in layers:
            grade = curve = None
            for h in range(reach):
                m = first_layer + h - p
                if abs(m) <= reach:
                    near = halo_ref[h, :, span]
                    first = (slope[m - 1] if m > 0 else -slope[-m - 1]) * near
                    second = bend[abs(m) - 1] * near
                    grade = first if grade is None else grade + first
                    curve = second if curve is None else curve + second
            out_ref[p, :, span] = part_ref[p, :, span] + (fine_ref[p, :, span] * grade + curve)
        at = pl.ds(layers[0], len(layers)), slice(None), span
        copy = pltpu.make_async_copy(out_ref.at[at], out_hbm.at[at], out_sems.at[len(sends)])
        copy.start()
        sends.append(copy)

    for arrival, span in zip(arrivals, spans):
        arrival.wait()
        add(low_ref, -reach, range(reach), span)
    for arrival, span in zip(arrivals[chunks:], spans):
        arrival.wait()
        add(high_ref, depth, range(depth - reach, depth), span)
    for copy in sends:
        copy.wait()


def finish_call(part, fine, low, high):
    points = part.shape[2]
    chunks = 4 if points % (4 * lanes) == 0 else 1
    held = pl.BlockSpec(memory_space=pltpu.VMEM)
    anywhere = pl.BlockSpec(memory_space=pl.ANY)
    return pl.pallas_call(
        functools.partial(finish_kernel, chunks),
        in_specs=[held, held, anywhere, anywhere],
        out_specs=anywhere,
        out_shape=jax.ShapeDtypeStruct(part.shape, jnp.float32),
        scratch_shapes=[
            pltpu.VMEM(part.shape, jnp.float32),
            pltpu.VMEM(low.shape, jnp.float32),
            pltpu.VMEM(high.shape, jnp.float32),
            pltpu.SemaphoreType.DMA((2, chunks)),
            pltpu.SemaphoreType.DMA((2 * chunks,)),
        ],
        compiler_params=pltpu.CompilerParams(vmem_limit_bytes=vmem_bytes),
        cost_estimate=light,
        name="finish",
    )(part, fine, low, high)


def tie(value, *gates):
    anywhere = pl.BlockSpec(memory_space=pl.ANY)
    return pl.pallas_call(
        lambda *refs: None,
        in_specs=[anywhere] * (1 + len(gates)),
        out_specs=anywhere,
        out_shape=jax.ShapeDtypeStruct(value.shape, value.dtype),
        input_output_aliases={0: 0},
        cost_estimate=light,
        name="tie",
    )(value, *gates)


def slab_kernel(begin, source_hbm, out_ref, held_ref, in_sems, out_sems):
    layers, _, points = held_ref.shape
    width = points // slab_chunks
    spans = [pl.ds(c * width, width) for c in range(slab_chunks)]
    arrivals = [
        pltpu.make_async_copy(
            source_hbm.at[pl.ds(begin, layers), :, span], held_ref.at[:, :, span], in_sems.at[c]
        )
        for c, span in enumerate(spans)
    ]
    sends = [
        pltpu.make_async_copy(held_ref.at[:, :, span], out_ref.at[:, :, span], out_sems.at[c])
        for c, span in enumerate(spans)
    ]
    for copy in arrivals:
        copy.start()
    for copy, send in zip(arrivals, sends):
        copy.wait()
        send.start()
    for send in sends:
        send.wait()


def slab_call(scalar, width):
    depth, height, _ = scalar.shape
    shape = (reach, height, width)
    anywhere = pl.BlockSpec(memory_space=pl.ANY)
    return pl.pallas_call(
        functools.partial(slab_kernel, depth - reach),
        in_specs=[anywhere],
        out_specs=anywhere,
        out_shape=jax.ShapeDtypeStruct(shape, jnp.float32),
        scratch_shapes=[pltpu.VMEM(shape, jnp.float32)] + [pltpu.SemaphoreType.DMA((slab_chunks,))] * 2,
        compiler_params=pltpu.CompilerParams(vmem_limit_bytes=52 * 1024 * 1024),
        cost_estimate=light,
        name="slab",
    )(scalar)


def depart_kernel(own_hbm, scalar_hbm, gate, down_hbm, edge_hbm, sent_hbm, end_hbm,
                  own_ref, scalar_ref, ends_ref, edge_ref, in_sems, out_sems):
    kinds, rows, cells = own_ref.shape
    depth, height, points = scalar_ref.shape
    layers = [pl.ds(depth - reach, reach), pl.ds(0, reach)]
    middle = depth - 2 * reach
    arrivals = [
        pltpu.make_async_copy(scalar_hbm.at[span], scalar_ref.at[span], in_sems.at[i])
        for i, span in enumerate(layers + [pl.ds(reach, middle)] * (middle > 0))
    ]
    arrivals.append(pltpu.make_async_copy(own_hbm, own_ref, in_sems.at[3]))
    for copy in arrivals[::-1]:
        copy.start()
    sends = []

    def send(source, target):
        copy = pltpu.make_async_copy(source, target, out_sems.at[len(sends)])
        copy.start()
        sends.append(copy)

    arrivals[-1].wait()
    for kind in range(kinds):
        send(own_ref.at[kind], sent_hbm.at[pl.ds(kind * rows, rows)])
    for copy in arrivals[:-1]:
        copy.wait()
    send(scalar_ref.at[layers[1]], down_hbm)
    edge_ref[:, :reach] = scalar_ref[:, :reach]
    edge_ref[:, reach:] = scalar_ref[:, height - reach :]
    send(edge_ref, edge_hbm)
    first = scalar_ref[:, :, :lanes].reshape(rows, lanes).T
    last = scalar_ref[:, :, points - lanes :].reshape(rows, lanes).T
    ends_ref[...] = jnp.zeros_like(ends_ref)
    ends_ref[:, :rows] = jnp.concatenate([first[:reach], last[lanes - reach :]], axis=0)
    send(ends_ref, sent_hbm.at[pl.ds(kinds * rows, 2 * reach)])
    send(ends_ref, end_hbm)
    for copy in sends:
        copy.wait()


def depart_call(own, scalar, gate):
    kinds, rows, cells = own.shape
    depth, height, points = scalar.shape
    edge, ends = (depth, 2 * reach, points), (2 * reach, cells)
    shapes = [(reach, height, points), edge, (kinds * rows + 2 * reach, cells), ends]
    anywhere = pl.BlockSpec(memory_space=pl.ANY)
    return pl.pallas_call(
        depart_kernel,
        in_specs=[anywhere] * 3,
        out_specs=[anywhere] * len(shapes),
        out_shape=[jax.ShapeDtypeStruct(shape, jnp.float32) for shape in shapes],
        scratch_shapes=[
            pltpu.VMEM(own.shape, jnp.float32),
            pltpu.VMEM(scalar.shape, jnp.float32),
            pltpu.VMEM(ends, jnp.float32),
            pltpu.VMEM(edge, jnp.float32),
            pltpu.SemaphoreType.DMA((4,)),
            pltpu.SemaphoreType.DMA((4 + kinds,)),
        ],
        compiler_params=pltpu.CompilerParams(vmem_limit_bytes=most_vmem_bytes),
        cost_estimate=light,
        name="depart",
    )(own, scalar, gate)


def padded_2(block, sides, width):
    for axis, dim in sides:
        count = lax.axis_size(axis)
        forward = [(i, i + 1) for i in range(count - 1)]
        forward.append((count - 1, 0))
        backward = [(target, source) for source, target in forward]
        low = lax.ppermute(
            lax.slice_in_dim(block, block.shape[dim] - width, None, axis=dim), axis, forward
        )
        high = lax.ppermute(lax.slice_in_dim(block, 0, width, axis=dim), axis, backward)
        block = jnp.concatenate([low, block, high], axis=dim)
    return block


def derivative_rows(first_row, count, length):
    rows = first_row + lax.iota(jnp.int32, count)
    columns = lax.iota(jnp.int32, length)
    offset = (rows[:, None] - columns[None, :]) % length
    signed = jnp.where(offset > length // 2, offset - length, offset)
    angle = signed.astype(jnp.float32) * (math.pi / length)
    parity = 1.0 - 2.0 * (offset % 2).astype(jnp.float32)
    same = offset == 0
    sine = jnp.where(same, 1.0, jnp.sin(angle))
    first = jnp.where(same, 0.0, 0.5 * parity * jnp.cos(angle) / sine)
    second = jnp.where(same, -(length * length) / 12.0 - 1.0 / 6.0, -0.5 * parity / (sine * sine))
    average = jnp.full((count, length), 1.0 / length, jnp.float32)
    return jnp.concatenate([first, second, average], axis=0)


def scalar_update(padded, fine):
    extent = (padded.shape[0] - 8, padded.shape[1] - 8, padded.shape[2] - 8)
    centre = lax.slice(padded, (4, 4, 4), (4 + extent[0], 4 + extent[1], 4 + extent[2]))
    gradients = []
    curvature = jnp.zeros(extent, jnp.float32)
    for axis_index in range(3):
        slope = jnp.zeros(extent, jnp.float32)
        for offset in range(9):
            begin = [4, 4, 4]
            begin[axis_index] = offset
            finish = (begin[0] + extent[0], begin[1] + extent[1], begin[2] + extent[2])
            window = lax.slice(padded, tuple(begin), finish)
            if first_all[offset] != 0.0:
                slope = slope + first_all[offset] * window
            curvature = curvature + second_all[offset] * window
        gradients.append(slope)
    advection = fine[2] * gradients[0] + fine[1] * gradients[1] + fine[0] * gradients[2]
    return centre - advect_rate * advection + diffuse_rate * curvature


def general_per_device(velocity, scalar, spline_base, spline_frac):
    cells = velocity.shape[1]
    length = cells * lax.axis_size("blk")
    block = lax.axis_index("blk")
    table = derivative_rows(block * cells, cells, length)
    both = jnp.einsum(
        "km,cmzy->ckzy",
        table,
        lax.all_gather(velocity, "blk", axis=1, tiled=True),
        precision=highest,
    )
    segment = (
        velocity
        - both[:, 2 * cells :]
        + velocity_step * (viscosity * both[:, cells : 2 * cells] - velocity[0:1] * both[:, :cells])
    )
    widened = padded_2(segment, (("blk", 1),), 2)
    weights = catmull_weights(spline_frac)
    local_base = spline_base - (block * cells - 2)
    slots = lax.iota(jnp.int32, cells + 4)[:, None]
    matrix = jnp.zeros((cells + 4, spline_base.shape[0]), jnp.float32)
    for tap_index in range(4):
        matrix = matrix + jnp.where(
            slots == (local_base + (tap_index - 1))[None, :], weights[tap_index][None, :], 0.0
        )
    fine = jnp.einsum("cxzy,xi->czyi", widened, matrix, precision=highest)
    padded = padded_2(scalar, (("grp", 1), ("blk", 2), ("dep", 0)), 4)
    return (segment, scalar_update(padded, fine))


def per_device(velocity, scalar, spline_base, spline_frac):
    kinds, cells, depth, height = velocity.shape
    points = scalar.shape[2]
    rows = depth * height
    count = lax.axis_size("blk")
    if count != 4 or lax.axis_size("grp") != 2 or cells % lanes or rows > cells or (points // 2) % cells or depth != 2 * reach:
        return general_per_device(velocity, scalar, spline_base, spline_frac)
    length = cells * count
    block = lax.axis_index("blk")

    rows_of_x = jnp.transpose(velocity, (0, 2, 3, 1)).reshape(kinds, rows, cells)
    chip = lax.ppermute(rows_of_x, "blk", exclusive("blk", 2))
    up = slab_call(scalar, points)
    lower = lax.ppermute(up, "dep", ring("dep", 1))
    down, edges, own, ends = depart_call(rows_of_x, scalar, up)
    upper = lax.ppermute(down, "dep", ring("dep", -1))
    far_ends = lax.ppermute(ends, "blk", exclusive("blk", 3))
    matrix = spline_matrix(spline_base - block * cells, spline_frac, cells, points // cells)
    outer_rows = lax.ppermute(edges, "grp", ring("grp", 1))
    core = lax.ppermute(tie(own, chip), "blk", exclusive("blk", 1))
    chip = tie(chip, far_ends, matrix, outer_rows)
    diagonal = lax.ppermute(chip, "blk", exclusive("blk", 1))
    info = jnp.stack([(block - (block ^ j)) % count for j in range(4)] + [block % 2]).astype(jnp.int32)
    main, outer = segment_call(rows_of_x, core, chip, diagonal, info, length)
    part, vertical = combine_call(main, outer, matrix, scalar, outer_rows, core, far_ends, info[4:])
    result = finish_call(part.reshape(scalar.shape), vertical.reshape(scalar.shape), lower, upper)
    segment = jnp.transpose(main.reshape(kinds, depth, height, cells), (0, 3, 1, 2))
    return segment, result


def solution(mesh):
    in_specs = (P(None, "blk", "dep", "grp"), P("dep", "grp", "blk"), P("blk"), P("blk"))
    out_specs = (P(None, "blk", "dep", "grp"), P("dep", "grp", "blk"))
    return jax.shard_map(
        per_device, mesh=mesh, in_specs=in_specs, out_specs=out_specs, check_vma=False
    )
```

```python
import functools
import math

import jax
import jax.numpy as jnp
import ml_dtypes
import numpy as np
from jax import lax
from jax.experimental import pallas as pl
from jax.experimental.pallas import tpu as pltpu
from jax.sharding import PartitionSpec as P

velocity_step = 0.002
viscosity = 0.00125
advect_rate = 0.2
diffuse_rate = 0.05
first_side = (0.8, -0.2, 4.0 / 105.0, -1.0 / 280.0)
second_side = (1.6, -0.2, 8.0 / 315.0, -1.0 / 560.0)
second_centre = -205.0 / 72.0
first_all = tuple(-a for a in reversed(first_side)) + (0.0,) + first_side
second_all = tuple(reversed(second_side)) + (second_centre,) + second_side
slope = tuple(-advect_rate * a for a in first_side)
bend = tuple(diffuse_rate * b for b in second_side)
centre_weight = 1.0 + 3.0 * diffuse_rate * second_centre
highest = lax.Precision.HIGHEST
reach = 4
slab_chunks = 4
lanes = 128
vmem_bytes = 32 * 1024 * 1024
most_vmem_bytes = 60 * 1024 * 1024
light = pl.CostEstimate(flops=1024, bytes_accessed=1024, transcendentals=0)


def ring(axis, step):
    count = lax.axis_size(axis)
    return [(i, (i + step) % count) for i in range(count)]


def exclusive(axis, mask):
    return [(i, i ^ mask) for i in range(lax.axis_size(axis))]


def split_table(values):
    high = values.astype(np.float32).astype(ml_dtypes.bfloat16)
    low = (values - high.astype(np.float64)).astype(np.float32).astype(ml_dtypes.bfloat16)
    return high, low


def right_table(values):
    high, low = split_table(values)
    return np.concatenate([high, high, low], axis=-2)


def circulant_tables(length, cells):
    s = np.arange(length)
    signed = np.where(s > length // 2, s - length, s)
    angle = signed * (np.pi / length)
    sine = np.where(s == 0, 1.0, np.sin(angle))
    parity = 1.0 - 2.0 * (s % 2)
    first = np.where(s == 0, 0.0, 0.5 * parity * np.cos(angle) / sine) * velocity_step
    second = np.where(s == 0, -(length * length) / 12.0 - 1.0 / 6.0, -0.5 * parity / (sine * sine))
    second = second * (velocity_step * viscosity)
    own = np.arange(cells)
    outer = np.zeros(lanes, np.int64)
    used = np.zeros(lanes)
    for lane, cell in ((0, cells), (1, cells + 1), (lanes - 2, -2), (lanes - 1, -1)):
        outer[lane] = cell
        used[lane] = 1.0
    blocks = []
    for distance in range(length // cells):
        main = (distance * cells + own[None, :] - own[:, None]) % length
        side = (distance * cells + outer[None, :] - own[:, None]) % length
        blocks.append(
            np.concatenate([first[main], second[main], first[side] * used, second[side] * used], axis=1)
        )
    return right_table(np.stack(blocks))


def level_table(depth, height):
    size, side = depth * height, 2 * reach
    table = np.zeros((3, depth, height, size + depth * side))
    for z in range(depth):
        for y in range(height):
            for m in range(-reach, reach + 1):
                if m == 0:
                    continue
                first = slope[m - 1] if m > 0 else -slope[-m - 1]
                second = bend[abs(m) - 1]
                if 0 <= y + m < height:
                    at = z * height + y + m
                else:
                    at = size + z * side + (y + m - height if m > 0 else y + m + side)
                table[0, z, y, at] += first
                table[2, z, y, at] += second
                if 0 <= z + m < depth:
                    table[1, z, y, (z + m) * height + y] += first
                    table[2, z, y, (z + m) * height + y] += second
    high, low = split_table(table.reshape(3 * size, -1))
    return np.concatenate([high, high, low], axis=1)


def dot(a, b):
    return jnp.dot(a, b, preferred_element_type=jnp.float32)


def split(value):
    high = value.astype(jnp.bfloat16)
    return high, (value - high.astype(jnp.float32)).astype(jnp.bfloat16)


def left_operand(value):
    high, low = split(value)
    return jnp.concatenate([high, low, high], axis=1)


def segment_kernel(length, info, own_ref, core_ref, chip_ref, far_ref, *refs):
    table_refs, (main_ref, outer_ref) = refs[:4], refs[4:]
    kinds, rows, cells = own_ref.shape
    lines = kinds * rows
    blocks = [own_ref[...].reshape(lines, cells), core_ref[:lines]]
    blocks += [ref[...].reshape(lines, cells) for ref in (chip_ref, far_ref)]
    total = sums = None
    for block, table_ref in zip(blocks, table_refs):
        product = dot(left_operand(block), table_ref[0])
        partial = jnp.sum(block, axis=1, keepdims=True)
        total = product if total is None else total + product
        sums = partial if sums is None else sums + partial
    mean = sums * (1.0 / length)
    even = info[4] == 0
    after = jnp.where(even, blocks[1][:, :lanes], blocks[3][:, :lanes])
    before = jnp.where(even, blocks[3][:, cells - lanes :], blocks[1][:, cells - lanes :])
    place = lax.broadcasted_iota(jnp.int32, after.shape, 1)
    outer = jnp.where(place < lanes // 2, after, before)

    def advance(own, first, second):
        lead = jnp.concatenate([own[:rows]] * kinds, axis=0)
        return own - mean + (second - lead * first)

    main = advance(blocks[0], total[:, :cells], total[:, cells : 2 * cells])
    side = advance(outer, total[:, 2 * cells : 2 * cells + lanes], total[:, 2 * cells + lanes :])
    main_ref[...] = main.reshape(kinds, rows, cells)
    outer_ref[...] = side.reshape(kinds, rows, lanes)


def segment_call(own, core, chip, diagonal, info, length):
    kinds, rows, cells = own.shape
    table = circulant_tables(length, cells)
    whole = pl.BlockSpec(own.shape, lambda g, info: (0, 0, 0))
    sent = pl.BlockSpec(core.shape, lambda g, info: (0, 0))
    tables = [
        pl.BlockSpec((1,) + table.shape[1:], functools.partial(lambda j, g, info: (info[j], 0, 0), j))
        for j in range(4)
    ]
    return pl.pallas_call(
        functools.partial(segment_kernel, length),
        grid_spec=pltpu.PrefetchScalarGridSpec(
            num_scalar_prefetch=1,
            grid=(1,),
            in_specs=[whole, sent, whole, whole] + tables,
            out_specs=[whole, pl.BlockSpec((kinds, rows, lanes), lambda g, info: (0, 0, 0))],
        ),
        out_shape=[
            jax.ShapeDtypeStruct((kinds, rows, cells), jnp.float32),
            jax.ShapeDtypeStruct((kinds, rows, lanes), jnp.float32),
        ],
        compiler_params=pltpu.CompilerParams(vmem_limit_bytes=vmem_bytes),
        cost_estimate=light,
        name="segment",
    )(info, own, core, chip, diagonal, *([jnp.asarray(table)] * 4))


def catmull_weights(fraction):
    square = fraction * fraction
    cube = square * fraction
    return (
        (-cube + 2.0 * square - fraction) * 0.5,
        (3.0 * cube - 5.0 * square + 2.0) * 0.5,
        (-3.0 * cube + 4.0 * square + fraction) * 0.5,
        (cube - square) * 0.5,
    )


def spline_matrix(local_base, fraction, cells, refine):
    tiles = cells // lanes
    row = lax.iota(jnp.int32, 2 * lanes)[:, None]
    half = (lax.iota(jnp.int32, local_base.shape[0]) // (refine * (lanes // 2)))[None, :]
    own = half // 2
    other = (own + jnp.where(half % 2 == 1, 1, tiles)) % (tiles + 1)
    lane = jnp.where(row < lanes, own * lanes + row, other * lanes + row - lanes)
    cell = jnp.where(lane < cells + lanes // 2, lane, lane - cells - lanes)
    gap = cell - local_base[None, :]
    matrix = jnp.zeros(gap.shape, jnp.float32)
    for tap, weight in enumerate(catmull_weights(fraction)):
        matrix = jnp.where(gap == tap - 1, weight[None, :], matrix)
    return matrix


def end_terms(halo, sign):
    grade = curve = None
    place = lax.broadcasted_iota(jnp.int32, halo.shape, 1)
    halo = jnp.where(place >= lanes // 2 if sign < 0 else place < lanes // 2, halo, 0.0)
    for m in range(1, reach + 1):
        near = pltpu.roll(halo, (-sign * m) % lanes, 1)
        first, second = (sign * slope[m - 1]) * near, bend[m - 1] * near
        grade = first if grade is None else grade + first
        curve = second if curve is None else curve + second
    near = place < reach if sign < 0 else place >= lanes - reach
    return jnp.where(near, grade, 0.0), jnp.where(near, curve, 0.0)


def side_terms(ringed, extent):
    size = ringed.shape[1]
    grade = curve = None
    for m in range(1, reach + 1):
        ahead = pltpu.roll(ringed, size - m, 1)[:, :extent]
        behind = pltpu.roll(ringed, m, 1)[:, :extent]
        first, second = slope[m - 1] * (ahead - behind), bend[m - 1] * (ahead + behind)
        grade = first if grade is None else grade + first
        curve = second if curve is None else curve + second
    return grade, curve


def combine_kernel(tiles, parity, main_ref, outer_ref, matrix_ref, mid_ref, left_ref, right_ref, rows_ref, table_ref,
                   core_ref, far_ref, out_ref, fine_ref, seg_high, seg_low, halo_ref):
    step, steps = pl.program_id(0), pl.num_programs(0)
    kinds, rows, cells = main_ref.shape
    depth, height, width = mid_ref.shape

    @pl.when(step == 0)
    def _():
        for ref, begin, size in ((main_ref, 0, cells), (outer_ref, cells, lanes)):
            high, low = split(ref[...].reshape(kinds * rows, size))
            seg_high[:, begin : begin + size] = high
            seg_low[:, begin : begin + size] = low
        even = parity[0] == 0
        after = jnp.where(even, core_ref[:, :rows], far_ref[:, :rows])[:reach]
        before = jnp.where(even, far_ref[:, :rows], core_ref[:, :rows])[reach:]
        gap = jnp.zeros((lanes - 2 * reach, rows), jnp.float32)
        halo_ref[...] = jnp.concatenate([after, gap, before], axis=0).T

    own = step // 2
    other = lax.rem(own + jnp.where(lax.rem(step, 2) == 1, 1, tiles), tiles + 1)
    spans = [pl.ds(pl.multiple_of(at * lanes, lanes), lanes) for at in (own, other)]
    source = jnp.concatenate([ref[:, span] for ref in (seg_high, seg_low, seg_high) for span in spans], axis=1)
    high, low = split(matrix_ref[...])
    fine = dot(source, jnp.concatenate([high, high, low], axis=0))

    values = jnp.concatenate([mid_ref[...].reshape(rows, width), rows_ref[...].reshape(-1, width)], axis=0)
    high, low = split(values)
    level = dot(table_ref[...], jnp.concatenate([high, low, high], axis=0))

    place = lax.broadcasted_iota(jnp.int32, (height, lanes), 1)
    for z in range(depth):
        left = jnp.where(step == 0, 0.0, left_ref[z])
        right = jnp.where(step == steps - 1, 0.0, right_ref[z])
        mid = mid_ref[z]
        grade, curve = side_terms(jnp.concatenate([mid, jnp.where(place < lanes // 2, right, left)], axis=1), width)
        span = slice(z * height, (z + 1) * height)

        def of(array, kind):
            return array[kind * rows + z * height : kind * rows + (z + 1) * height]

        vertical = of(fine, 2)
        out_ref[span] = (centre_weight * mid + (curve + of(level, 2))) + (
            of(fine, 0) * grade + of(fine, 1) * of(level, 0) + vertical * of(level, 1)
        )
        fine_ref[span] = vertical
    for at, sign, begin in ((0, -1, 0), (steps - 1, 1, width - lanes)):

        @pl.when(step == at)
        def _():
            grade, curve = end_terms(halo_ref[...], sign)
            span = slice(begin, begin + lanes)
            out_ref[:, span] += fine[:rows, span] * grade + curve


def combine_call(main, outer, matrix, scalar, outer_rows, core, diagonal, parity):
    kinds, rows, cells = main.shape
    depth, height, points = scalar.shape
    steps = 2 * (cells // lanes)
    width = points // steps
    tiles, last = width // lanes, points // lanes - 1
    table = level_table(depth, height)
    flat_tile = pl.BlockSpec((rows, width), lambda t, parity: (0, t))
    edge = (depth, height, lanes)
    ends = pl.BlockSpec((2 * reach, cells), lambda t, parity: (core.shape[0] // (2 * reach) - 1, 0))
    flat = jax.ShapeDtypeStruct((rows, points), jnp.float32)
    return pl.pallas_call(
        functools.partial(combine_kernel, cells // lanes),
        grid_spec=pltpu.PrefetchScalarGridSpec(
            num_scalar_prefetch=1,
            grid=(steps,),
            in_specs=[
                pl.BlockSpec((kinds, rows, cells), lambda t, parity: (0, 0, 0)),
                pl.BlockSpec((kinds, rows, lanes), lambda t, parity: (0, 0, 0)),
                pl.BlockSpec((2 * lanes, width), lambda t, parity: (0, t)),
                pl.BlockSpec((depth, height, width), lambda t, parity: (0, 0, t)),
                pl.BlockSpec(edge, lambda t, parity: (0, 0, jnp.maximum(t * tiles - 1, 0))),
                pl.BlockSpec(edge, lambda t, parity: (0, 0, jnp.minimum((t + 1) * tiles, last))),
                pl.BlockSpec((depth, 2 * reach, width), lambda t, parity: (0, 0, t)),
                pl.BlockSpec(table.shape, lambda t, parity: (0, 0)),
                ends,
                pl.BlockSpec((2 * reach, cells), lambda t, parity: (0, 0)),
            ],
            out_specs=[flat_tile, flat_tile],
            scratch_shapes=[
                pltpu.VMEM((kinds * rows, cells + lanes), jnp.bfloat16),
                pltpu.VMEM((kinds * rows, cells + lanes), jnp.bfloat16),
                pltpu.VMEM((rows, lanes), jnp.float32),
            ],
        ),
        out_shape=[flat, flat],
        compiler_params=pltpu.CompilerParams(vmem_limit_bytes=vmem_bytes),
        cost_estimate=light,
        name="combine",
    )(parity, main, outer, matrix, scalar, scalar, scalar, outer_rows, jnp.asarray(table), core, diagonal)


def finish_kernel(parts, aliased, part_ref, fine_ref, *refs):
    halos, (out_hbm, out_ref, held_ref, in_sems, out_sems) = refs[: len(parts)], refs[len(parts) + aliased :]
    work, arrivals, sends = [], [], []
    for i, (halo, (first_layer, begin, start, size, chunk)) in enumerate(zip(halos, parts)):
        for x in range(0, size, chunk):
            held = held_ref.at[i, :, :, pl.ds(x, chunk)]
            copy = pltpu.make_async_copy(halo.at[:, :, pl.ds(x, chunk)], held, in_sems.at[len(arrivals)])
            copy.start()
            arrivals.append(copy)
            work.append((i, first_layer, begin, pl.ds(x, chunk), pl.ds(start + x, chunk)))
    for (i, first_layer, begin, held, span), arrival in zip(work, arrivals):
        arrival.wait()
        for p in range(begin, begin + reach):
            grade = curve = None
            for h in range(reach):
                m = first_layer + h - p
                if abs(m) <= reach:
                    near = held_ref[i, h, :, held]
                    first = (slope[m - 1] if m > 0 else -slope[-m - 1]) * near
                    second = bend[abs(m) - 1] * near
                    grade = first if grade is None else grade + first
                    curve = second if curve is None else curve + second
            out_ref[p, :, span] = part_ref[p, :, span] + (fine_ref[p, :, span] * grade + curve)
        at = pl.ds(begin, reach), slice(None), span
        copy = pltpu.make_async_copy(out_ref.at[at], out_hbm.at[at], out_sems.at[len(sends)])
        copy.start()
        sends.append(copy)
    for copy in sends:
        copy.wait()


def finish_call(part, fine, halos, started=None):
    depth = part.shape[0]
    parts, count = [], 0
    for above, start, halo in halos:
        size = halo.shape[2]
        chunk = math.gcd(size, 512)
        half = (depth, depth - reach) if above else (-reach, 0)
        parts.append(half + (start, size, chunk))
        count += size // chunk
    aliased = started is not None
    held = pl.BlockSpec(memory_space=pltpu.VMEM)
    anywhere = pl.BlockSpec(memory_space=pl.ANY)
    widest = max(halo.shape[2] for _, _, halo in halos)
    return pl.pallas_call(
        functools.partial(finish_kernel, parts, aliased),
        in_specs=[held, held] + [anywhere] * (len(halos) + aliased),
        out_specs=anywhere,
        out_shape=jax.ShapeDtypeStruct(part.shape, jnp.float32),
        input_output_aliases={2 + len(halos): 0} if aliased else {},
        scratch_shapes=[
            pltpu.VMEM(part.shape, jnp.float32),
            pltpu.VMEM((len(halos), reach, part.shape[1], widest), jnp.float32),
            pltpu.SemaphoreType.DMA((count,)),
            pltpu.SemaphoreType.DMA((count,)),
        ],
        compiler_params=pltpu.CompilerParams(vmem_limit_bytes=vmem_bytes),
        cost_estimate=light,
        name="finish",
    )(part, fine, *[halo for _, _, halo in halos], *([started] if aliased else []))


def tie(value, *gates):
    anywhere = pl.BlockSpec(memory_space=pl.ANY)
    return pl.pallas_call(
        lambda *refs: None,
        in_specs=[anywhere] * (1 + len(gates)),
        out_specs=anywhere,
        out_shape=jax.ShapeDtypeStruct(value.shape, value.dtype),
        input_output_aliases={0: 0},
        cost_estimate=light,
        name="tie",
    )(value, *gates)


def slab_kernel(begin, source_hbm, out_ref, held_ref, in_sems, out_sems):
    layers, _, points = held_ref.shape
    width = points // slab_chunks
    spans = [pl.ds(c * width, width) for c in range(slab_chunks)]
    arrivals = [
        pltpu.make_async_copy(
            source_hbm.at[pl.ds(begin, layers), :, span], held_ref.at[:, :, span], in_sems.at[c]
        )
        for c, span in enumerate(spans)
    ]
    sends = [
        pltpu.make_async_copy(held_ref.at[:, :, span], out_ref.at[:, :, span], out_sems.at[c])
        for c, span in enumerate(spans)
    ]
    for copy in arrivals:
        copy.start()
    for copy, send in zip(arrivals, sends):
        copy.wait()
        send.start()
    for send in sends:
        send.wait()


def slab_call(scalar, width):
    depth, height, _ = scalar.shape
    shape = (reach, height, width)
    anywhere = pl.BlockSpec(memory_space=pl.ANY)
    return pl.pallas_call(
        functools.partial(slab_kernel, depth - reach),
        in_specs=[anywhere],
        out_specs=anywhere,
        out_shape=jax.ShapeDtypeStruct(shape, jnp.float32),
        scratch_shapes=[pltpu.VMEM(shape, jnp.float32)] + [pltpu.SemaphoreType.DMA((slab_chunks,))] * 2,
        compiler_params=pltpu.CompilerParams(vmem_limit_bytes=52 * 1024 * 1024),
        cost_estimate=light,
        name="slab",
    )(scalar)


def depart_kernel(own_hbm, scalar_hbm, gate, down_hbm, late_hbm, edge_hbm, sent_hbm, end_hbm,
                  own_ref, scalar_ref, ends_ref, edge_ref, in_sems, out_sems):
    kinds, rows, cells = own_ref.shape
    depth, height, points = scalar_ref.shape
    layers = [pl.ds(depth - reach, reach), pl.ds(0, reach)]
    middle = depth - 2 * reach
    arrivals = [
        pltpu.make_async_copy(scalar_hbm.at[span], scalar_ref.at[span], in_sems.at[i])
        for i, span in enumerate(layers + [pl.ds(reach, middle)] * (middle > 0))
    ]
    arrivals.append(pltpu.make_async_copy(own_hbm, own_ref, in_sems.at[3]))
    for copy in arrivals[::-1]:
        copy.start()
    sends = []

    def send(source, target):
        copy = pltpu.make_async_copy(source, target, out_sems.at[len(sends)])
        copy.start()
        sends.append(copy)

    arrivals[-1].wait()
    for kind in range(kinds):
        send(own_ref.at[kind], sent_hbm.at[pl.ds(kind * rows, rows)])
    for copy in arrivals[:-1]:
        copy.wait()
    cut = down_hbm.shape[2]
    send(scalar_ref.at[layers[1], :, pl.ds(0, cut)], down_hbm)
    send(scalar_ref.at[layers[1], :, pl.ds(cut, points - cut)], late_hbm)
    edge_ref[:, :reach] = scalar_ref[:, :reach]
    edge_ref[:, reach:] = scalar_ref[:, height - reach :]
    send(edge_ref, edge_hbm)
    first = scalar_ref[:, :, :lanes].reshape(rows, lanes).T
    last = scalar_ref[:, :, points - lanes :].reshape(rows, lanes).T
    ends_ref[...] = jnp.zeros_like(ends_ref)
    ends_ref[:, :rows] = jnp.concatenate([first[:reach], last[lanes - reach :]], axis=0)
    send(ends_ref, sent_hbm.at[pl.ds(kinds * rows, 2 * reach)])
    send(ends_ref, end_hbm)
    for copy in sends:
        copy.wait()


def depart_call(own, scalar, cut, gate):
    kinds, rows, cells = own.shape
    depth, height, points = scalar.shape
    edge, ends = (depth, 2 * reach, points), (2 * reach, cells)
    shapes = [(reach, height, cut), (reach, height, points - cut), edge, (kinds * rows + 2 * reach, cells), ends]
    anywhere = pl.BlockSpec(memory_space=pl.ANY)
    return pl.pallas_call(
        depart_kernel,
        in_specs=[anywhere] * 3,
        out_specs=[anywhere] * len(shapes),
        out_shape=[jax.ShapeDtypeStruct(shape, jnp.float32) for shape in shapes],
        scratch_shapes=[
            pltpu.VMEM(own.shape, jnp.float32),
            pltpu.VMEM(scalar.shape, jnp.float32),
            pltpu.VMEM(ends, jnp.float32),
            pltpu.VMEM(edge, jnp.float32),
            pltpu.SemaphoreType.DMA((4,)),
            pltpu.SemaphoreType.DMA((5 + kinds,)),
        ],
        compiler_params=pltpu.CompilerParams(vmem_limit_bytes=most_vmem_bytes),
        cost_estimate=light,
        name="depart",
    )(own, scalar, gate)


def padded_2(block, sides, width):
    for axis, dim in sides:
        count = lax.axis_size(axis)
        forward = [(i, i + 1) for i in range(count - 1)]
        forward.append((count - 1, 0))
        backward = [(target, source) for source, target in forward]
        low = lax.ppermute(
            lax.slice_in_dim(block, block.shape[dim] - width, None, axis=dim), axis, forward
        )
        high = lax.ppermute(lax.slice_in_dim(block, 0, width, axis=dim), axis, backward)
        block = jnp.concatenate([low, block, high], axis=dim)
    return block


def derivative_rows(first_row, count, length):
    rows = first_row + lax.iota(jnp.int32, count)
    columns = lax.iota(jnp.int32, length)
    offset = (rows[:, None] - columns[None, :]) % length
    signed = jnp.where(offset > length // 2, offset - length, offset)
    angle = signed.astype(jnp.float32) * (math.pi / length)
    parity = 1.0 - 2.0 * (offset % 2).astype(jnp.float32)
    same = offset == 0
    sine = jnp.where(same, 1.0, jnp.sin(angle))
    first = jnp.where(same, 0.0, 0.5 * parity * jnp.cos(angle) / sine)
    second = jnp.where(same, -(length * length) / 12.0 - 1.0 / 6.0, -0.5 * parity / (sine * sine))
    average = jnp.full((count, length), 1.0 / length, jnp.float32)
    return jnp.concatenate([first, second, average], axis=0)


def scalar_update(padded, fine):
    extent = (padded.shape[0] - 8, padded.shape[1] - 8, padded.shape[2] - 8)
    centre = lax.slice(padded, (4, 4, 4), (4 + extent[0], 4 + extent[1], 4 + extent[2]))
    gradients = []
    curvature = jnp.zeros(extent, jnp.float32)
    for axis_index in range(3):
        slope = jnp.zeros(extent, jnp.float32)
        for offset in range(9):
            begin = [4, 4, 4]
            begin[axis_index] = offset
            finish = (begin[0] + extent[0], begin[1] + extent[1], begin[2] + extent[2])
            window = lax.slice(padded, tuple(begin), finish)
            if first_all[offset] != 0.0:
                slope = slope + first_all[offset] * window
            curvature = curvature + second_all[offset] * window
        gradients.append(slope)
    advection = fine[2] * gradients[0] + fine[1] * gradients[1] + fine[0] * gradients[2]
    return centre - advect_rate * advection + diffuse_rate * curvature


def general_per_device(velocity, scalar, spline_base, spline_frac):
    cells = velocity.shape[1]
    length = cells * lax.axis_size("blk")
    block = lax.axis_index("blk")
    table = derivative_rows(block * cells, cells, length)
    both = jnp.einsum(
        "km,cmzy->ckzy",
        table,
        lax.all_gather(velocity, "blk", axis=1, tiled=True),
        precision=highest,
    )
    segment = (
        velocity
        - both[:, 2 * cells :]
        + velocity_step * (viscosity * both[:, cells : 2 * cells] - velocity[0:1] * both[:, :cells])
    )
    widened = padded_2(segment, (("blk", 1),), 2)
    weights = catmull_weights(spline_frac)
    local_base = spline_base - (block * cells - 2)
    slots = lax.iota(jnp.int32, cells + 4)[:, None]
    matrix = jnp.zeros((cells + 4, spline_base.shape[0]), jnp.float32)
    for tap_index in range(4):
        matrix = matrix + jnp.where(
            slots == (local_base + (tap_index - 1))[None, :], weights[tap_index][None, :], 0.0
        )
    fine = jnp.einsum("cxzy,xi->czyi", widened, matrix, precision=highest)
    padded = padded_2(scalar, (("grp", 1), ("blk", 2), ("dep", 0)), 4)
    return (segment, scalar_update(padded, fine))


def per_device(velocity, scalar, spline_base, spline_frac):
    kinds, cells, depth, height = velocity.shape
    points = scalar.shape[2]
    rows = depth * height
    count = lax.axis_size("blk")
    if count != 4 or lax.axis_size("grp") != 2 or cells % lanes or rows > cells or (points // 2) % cells or depth != 2 * reach or points % (8 * lanes):
        return general_per_device(velocity, scalar, spline_base, spline_frac)
    length = cells * count
    block = lax.axis_index("blk")

    rows_of_x = jnp.transpose(velocity, (0, 2, 3, 1)).reshape(kinds, rows, cells)
    chip = lax.ppermute(rows_of_x, "blk", exclusive("blk", 2))
    up = slab_call(scalar, points)
    lower = lax.ppermute(up, "dep", ring("dep", 1))
    cut = points - points // 8
    down, late, edges, own, ends = depart_call(rows_of_x, scalar, cut, up)
    upper = lax.ppermute(down, "dep", ring("dep", -1))
    late = lax.ppermute(late, "dep", ring("dep", -1))
    far_ends = lax.ppermute(ends, "blk", exclusive("blk", 3))
    matrix = spline_matrix(spline_base - block * cells, spline_frac, cells, points // cells)
    outer_rows = lax.ppermute(edges, "grp", ring("grp", 1))
    core = lax.ppermute(tie(own, chip), "blk", exclusive("blk", 1))
    chip = tie(chip, far_ends, matrix, outer_rows)
    diagonal = lax.ppermute(chip, "blk", exclusive("blk", 1))
    info = jnp.stack([(block - (block ^ j)) % count for j in range(4)] + [block % 2]).astype(jnp.int32)
    main, outer = segment_call(rows_of_x, core, chip, diagonal, info, length)
    part, vertical = combine_call(main, outer, matrix, scalar, outer_rows, core, far_ends, info[4:])
    part, vertical = part.reshape(scalar.shape), vertical.reshape(scalar.shape)
    result = finish_call(part, vertical, [(False, 0, lower), (True, 0, upper)])
    result = finish_call(part, vertical, [(True, cut, late)], result)
    segment = jnp.transpose(main.reshape(kinds, depth, height, cells), (0, 3, 1, 2))
    return segment, result


def solution(mesh):
    in_specs = (P(None, "blk", "dep", "grp"), P("dep", "grp", "blk"), P("blk"), P("blk"))
    out_specs = (P(None, "blk", "dep", "grp"), P("dep", "grp", "blk"))
    return jax.shard_map(
        per_device, mesh=mesh, in_specs=in_specs, out_specs=out_specs, check_vma=False
    )
```

```python
import functools
import math

import jax
import jax.numpy as jnp
import ml_dtypes
import numpy as np
from jax import lax
from jax.experimental import pallas as pl
from jax.experimental.pallas import tpu as pltpu
from jax.sharding import PartitionSpec as P

velocity_step = 0.002
viscosity = 0.00125
advect_rate = 0.2
diffuse_rate = 0.05
first_side = (0.8, -0.2, 4.0 / 105.0, -1.0 / 280.0)
second_side = (1.6, -0.2, 8.0 / 315.0, -1.0 / 560.0)
second_centre = -205.0 / 72.0
first_all = tuple(-a for a in reversed(first_side)) + (0.0,) + first_side
second_all = tuple(reversed(second_side)) + (second_centre,) + second_side
slope = tuple(-advect_rate * a for a in first_side)
bend = tuple(diffuse_rate * b for b in second_side)
centre_weight = 1.0 + 3.0 * diffuse_rate * second_centre
highest = lax.Precision.HIGHEST
reach = 4
slab_chunks = 2
lanes = 128
vmem_bytes = 32 * 1024 * 1024
most_vmem_bytes = 60 * 1024 * 1024
light = pl.CostEstimate(flops=1024, bytes_accessed=1024, transcendentals=0)


def ring(axis, step):
    count = lax.axis_size(axis)
    return [(i, (i + step) % count) for i in range(count)]


def exclusive(axis, mask):
    return [(i, i ^ mask) for i in range(lax.axis_size(axis))]


def split_table(values):
    high = values.astype(np.float32).astype(ml_dtypes.bfloat16)
    low = (values - high.astype(np.float64)).astype(np.float32).astype(ml_dtypes.bfloat16)
    return high, low


def right_table(values):
    high, low = split_table(values)
    return np.concatenate([high, high, low], axis=-2)


def circulant_tables(length, cells):
    s = np.arange(length)
    signed = np.where(s > length // 2, s - length, s)
    angle = signed * (np.pi / length)
    sine = np.where(s == 0, 1.0, np.sin(angle))
    parity = 1.0 - 2.0 * (s % 2)
    first = np.where(s == 0, 0.0, 0.5 * parity * np.cos(angle) / sine) * velocity_step
    second = np.where(s == 0, -(length * length) / 12.0 - 1.0 / 6.0, -0.5 * parity / (sine * sine))
    second = second * (velocity_step * viscosity)
    own = np.arange(cells)
    outer = np.zeros(lanes, np.int64)
    used = np.zeros(lanes)
    for lane, cell in ((0, cells), (1, cells + 1), (lanes - 2, -2), (lanes - 1, -1)):
        outer[lane] = cell
        used[lane] = 1.0
    blocks = []
    for distance in range(length // cells):
        main = (distance * cells + own[None, :] - own[:, None]) % length
        side = (distance * cells + outer[None, :] - own[:, None]) % length
        blocks.append(
            np.concatenate([first[main], second[main], first[side] * used, second[side] * used], axis=1)
        )
    return right_table(np.stack(blocks))


def level_table(depth, height):
    size, side = depth * height, 2 * reach
    table = np.zeros((3, depth, height, size + depth * side))
    for z in range(depth):
        for y in range(height):
            for m in range(-reach, reach + 1):
                if m == 0:
                    continue
                first = slope[m - 1] if m > 0 else -slope[-m - 1]
                second = bend[abs(m) - 1]
                if 0 <= y + m < height:
                    at = z * height + y + m
                else:
                    at = size + z * side + (y + m - height if m > 0 else y + m + side)
                table[0, z, y, at] += first
                table[2, z, y, at] += second
                if 0 <= z + m < depth:
                    table[1, z, y, (z + m) * height + y] += first
                    table[2, z, y, (z + m) * height + y] += second
    high, low = split_table(table.reshape(3 * size, -1))
    return np.concatenate([high, high, low], axis=1)


def dot(a, b):
    return jnp.dot(a, b, preferred_element_type=jnp.float32)


def split(value):
    high = value.astype(jnp.bfloat16)
    return high, (value - high.astype(jnp.float32)).astype(jnp.bfloat16)


def left_operand(value):
    high, low = split(value)
    return jnp.concatenate([high, low, high], axis=1)


def segment_kernel(length, info, own_ref, core_ref, chip_ref, far_ref, *refs):
    table_refs, (main_ref, outer_ref) = refs[:4], refs[4:]
    kinds, rows, cells = own_ref.shape
    lines = kinds * rows
    blocks = [own_ref[...].reshape(lines, cells), core_ref[:lines]]
    blocks += [ref[...].reshape(lines, cells) for ref in (chip_ref, far_ref)]
    total = sums = None
    for block, table_ref in zip(blocks, table_refs):
        product = dot(left_operand(block), table_ref[0])
        partial = jnp.sum(block, axis=1, keepdims=True)
        total = product if total is None else total + product
        sums = partial if sums is None else sums + partial
    mean = sums * (1.0 / length)
    even = info[4] == 0
    after = jnp.where(even, blocks[1][:, :lanes], blocks[3][:, :lanes])
    before = jnp.where(even, blocks[3][:, cells - lanes :], blocks[1][:, cells - lanes :])
    place = lax.broadcasted_iota(jnp.int32, after.shape, 1)
    outer = jnp.where(place < lanes // 2, after, before)

    def advance(own, first, second):
        lead = jnp.concatenate([own[:rows]] * kinds, axis=0)
        return own - mean + (second - lead * first)

    main = advance(blocks[0], total[:, :cells], total[:, cells : 2 * cells])
    side = advance(outer, total[:, 2 * cells : 2 * cells + lanes], total[:, 2 * cells + lanes :])
    main_ref[...] = main.reshape(kinds, rows, cells)
    outer_ref[...] = side.reshape(kinds, rows, lanes)


def segment_call(own, core, chip, diagonal, info, length):
    kinds, rows, cells = own.shape
    table = circulant_tables(length, cells)
    whole = pl.BlockSpec(own.shape, lambda g, info: (0, 0, 0))
    sent = pl.BlockSpec(core.shape, lambda g, info: (0, 0))
    tables = [
        pl.BlockSpec((1,) + table.shape[1:], functools.partial(lambda j, g, info: (info[j], 0, 0), j))
        for j in range(4)
    ]
    return pl.pallas_call(
        functools.partial(segment_kernel, length),
        grid_spec=pltpu.PrefetchScalarGridSpec(
            num_scalar_prefetch=1,
            grid=(1,),
            in_specs=[whole, sent, whole, whole] + tables,
            out_specs=[whole, pl.BlockSpec((kinds, rows, lanes), lambda g, info: (0, 0, 0))],
        ),
        out_shape=[
            jax.ShapeDtypeStruct((kinds, rows, cells), jnp.float32),
            jax.ShapeDtypeStruct((kinds, rows, lanes), jnp.float32),
        ],
        compiler_params=pltpu.CompilerParams(vmem_limit_bytes=vmem_bytes),
        cost_estimate=light,
        name="segment",
    )(info, own, core, chip, diagonal, *([jnp.asarray(table)] * 4))


def catmull_weights(fraction):
    square = fraction * fraction
    cube = square * fraction
    return (
        (-cube + 2.0 * square - fraction) * 0.5,
        (3.0 * cube - 5.0 * square + 2.0) * 0.5,
        (-3.0 * cube + 4.0 * square + fraction) * 0.5,
        (cube - square) * 0.5,
    )


def spline_matrix(local_base, fraction, cells, refine):
    tiles = cells // lanes
    row = lax.iota(jnp.int32, 2 * lanes)[:, None]
    half = (lax.iota(jnp.int32, local_base.shape[0]) // (refine * (lanes // 2)))[None, :]
    own = half // 2
    other = (own + jnp.where(half % 2 == 1, 1, tiles)) % (tiles + 1)
    lane = jnp.where(row < lanes, own * lanes + row, other * lanes + row - lanes)
    cell = jnp.where(lane < cells + lanes // 2, lane, lane - cells - lanes)
    gap = cell - local_base[None, :]
    matrix = jnp.zeros(gap.shape, jnp.float32)
    for tap, weight in enumerate(catmull_weights(fraction)):
        matrix = jnp.where(gap == tap - 1, weight[None, :], matrix)
    return matrix


def end_terms(halo, sign):
    grade = curve = None
    place = lax.broadcasted_iota(jnp.int32, halo.shape, 1)
    halo = jnp.where(place >= lanes // 2 if sign < 0 else place < lanes // 2, halo, 0.0)
    for m in range(1, reach + 1):
        near = pltpu.roll(halo, (-sign * m) % lanes, 1)
        first, second = (sign * slope[m - 1]) * near, bend[m - 1] * near
        grade = first if grade is None else grade + first
        curve = second if curve is None else curve + second
    near = place < reach if sign < 0 else place >= lanes - reach
    return jnp.where(near, grade, 0.0), jnp.where(near, curve, 0.0)


def side_terms(ringed, extent):
    size = ringed.shape[1]
    grade = curve = None
    for m in range(1, reach + 1):
        ahead = pltpu.roll(ringed, size - m, 1)[:, :extent]
        behind = pltpu.roll(ringed, m, 1)[:, :extent]
        first, second = slope[m - 1] * (ahead - behind), bend[m - 1] * (ahead + behind)
        grade = first if grade is None else grade + first
        curve = second if curve is None else curve + second
    return grade, curve


def combine_kernel(tiles, parity, main_ref, outer_ref, matrix_ref, mid_ref, left_ref, right_ref, rows_ref, table_ref,
                   core_ref, far_ref, out_ref, fine_ref, seg_high, seg_low, halo_ref):
    step, steps = pl.program_id(0), pl.num_programs(0)
    kinds, rows, cells = main_ref.shape
    depth, height, width = mid_ref.shape

    @pl.when(step == 0)
    def _():
        for ref, begin, size in ((main_ref, 0, cells), (outer_ref, cells, lanes)):
            high, low = split(ref[...].reshape(kinds * rows, size))
            seg_high[:, begin : begin + size] = high
            seg_low[:, begin : begin + size] = low
        even = parity[0] == 0
        after = jnp.where(even, core_ref[:, :rows], far_ref[:, :rows])[:reach]
        before = jnp.where(even, far_ref[:, :rows], core_ref[:, :rows])[reach:]
        gap = jnp.zeros((lanes - 2 * reach, rows), jnp.float32)
        halo_ref[...] = jnp.concatenate([after, gap, before], axis=0).T

    own = step // 2
    other = lax.rem(own + jnp.where(lax.rem(step, 2) == 1, 1, tiles), tiles + 1)
    spans = [pl.ds(pl.multiple_of(at * lanes, lanes), lanes) for at in (own, other)]
    source = jnp.concatenate([ref[:, span] for ref in (seg_high, seg_low, seg_high) for span in spans], axis=1)
    high, low = split(matrix_ref[...])
    fine = dot(source, jnp.concatenate([high, high, low], axis=0))

    values = jnp.concatenate([mid_ref[...].reshape(rows, width), rows_ref[...].reshape(-1, width)], axis=0)
    high, low = split(values)
    level = dot(table_ref[...], jnp.concatenate([high, low, high], axis=0))

    place = lax.broadcasted_iota(jnp.int32, (height, lanes), 1)
    for z in range(depth):
        left = jnp.where(step == 0, 0.0, left_ref[z])
        right = jnp.where(step == steps - 1, 0.0, right_ref[z])
        mid = mid_ref[z]
        grade, curve = side_terms(jnp.concatenate([mid, jnp.where(place < lanes // 2, right, left)], axis=1), width)
        span = slice(z * height, (z + 1) * height)

        def of(array, kind):
            return array[kind * rows + z * height : kind * rows + (z + 1) * height]

        vertical = of(fine, 2)
        out_ref[span] = (centre_weight * mid + (curve + of(level, 2))) + (
            of(fine, 0) * grade + of(fine, 1) * of(level, 0) + vertical * of(level, 1)
        )
        fine_ref[span] = vertical
    for at, sign, begin in ((0, -1, 0), (steps - 1, 1, width - lanes)):

        @pl.when(step == at)
        def _():
            grade, curve = end_terms(halo_ref[...], sign)
            span = slice(begin, begin + lanes)
            out_ref[:, span] += fine[:rows, span] * grade + curve


def combine_call(main, outer, matrix, scalar, outer_rows, core, diagonal, parity):
    kinds, rows, cells = main.shape
    depth, height, points = scalar.shape
    steps = 2 * (cells // lanes)
    width = points // steps
    tiles, last = width // lanes, points // lanes - 1
    table = level_table(depth, height)
    flat_tile = pl.BlockSpec((rows, width), lambda t, parity: (0, t))
    edge = (depth, height, lanes)
    ends = pl.BlockSpec((2 * reach, cells), lambda t, parity: (core.shape[0] // (2 * reach) - 1, 0))
    flat = jax.ShapeDtypeStruct((rows, points), jnp.float32)
    return pl.pallas_call(
        functools.partial(combine_kernel, cells // lanes),
        grid_spec=pltpu.PrefetchScalarGridSpec(
            num_scalar_prefetch=1,
            grid=(steps,),
            in_specs=[
                pl.BlockSpec((kinds, rows, cells), lambda t, parity: (0, 0, 0)),
                pl.BlockSpec((kinds, rows, lanes), lambda t, parity: (0, 0, 0)),
                pl.BlockSpec((2 * lanes, width), lambda t, parity: (0, t)),
                pl.BlockSpec((depth, height, width), lambda t, parity: (0, 0, t)),
                pl.BlockSpec(edge, lambda t, parity: (0, 0, jnp.maximum(t * tiles - 1, 0))),
                pl.BlockSpec(edge, lambda t, parity: (0, 0, jnp.minimum((t + 1) * tiles, last))),
                pl.BlockSpec((depth, 2 * reach, width), lambda t, parity: (0, 0, t)),
                pl.BlockSpec(table.shape, lambda t, parity: (0, 0)),
                ends,
                pl.BlockSpec((2 * reach, cells), lambda t, parity: (0, 0)),
            ],
            out_specs=[flat_tile, flat_tile],
            scratch_shapes=[
                pltpu.VMEM((kinds * rows, cells + lanes), jnp.bfloat16),
                pltpu.VMEM((kinds * rows, cells + lanes), jnp.bfloat16),
                pltpu.VMEM((rows, lanes), jnp.float32),
            ],
        ),
        out_shape=[flat, flat],
        compiler_params=pltpu.CompilerParams(vmem_limit_bytes=vmem_bytes),
        cost_estimate=light,
        name="combine",
    )(parity, main, outer, matrix, scalar, scalar, scalar, outer_rows, jnp.asarray(table), core, diagonal)


def finish_kernel(parts, aliased, direct, part_ref, fine_ref, *refs):
    halos, (out_hbm, out_ref, held_ref, in_sems, out_sems) = refs[: len(parts)], refs[len(parts) + aliased :]
    work, arrivals, sends = [], [], []
    for i, (halo, (first_layer, begin, start, size, chunk)) in enumerate(zip(halos, parts)):
        for x in range(0, size, chunk):
            span, place = pl.ds(x, chunk), pl.ds(start + x, chunk)
            if direct:
                work.append((halo, first_layer, begin, span, place))
                continue
            copy = pltpu.make_async_copy(
                halo.at[:, :, span], held_ref.at[i, :, :, span], in_sems.at[len(arrivals)]
            )
            copy.start()
            arrivals.append(copy)
            work.append((held_ref.at[i], first_layer, begin, span, place))
    for c, (near_ref, first_layer, begin, held, span) in enumerate(work):
        if not direct:
            arrivals[c].wait()
        for p in range(begin, begin + reach):
            grade = curve = None
            for h in range(reach):
                m = first_layer + h - p
                if abs(m) <= reach:
                    near = near_ref[h, :, held]
                    first = (slope[m - 1] if m > 0 else -slope[-m - 1]) * near
                    second = bend[abs(m) - 1] * near
                    grade = first if grade is None else grade + first
                    curve = second if curve is None else curve + second
            out_ref[p, :, span] = part_ref[p, :, span] + (fine_ref[p, :, span] * grade + curve)
        at = pl.ds(begin, reach), slice(None), span
        copy = pltpu.make_async_copy(out_ref.at[at], out_hbm.at[at], out_sems.at[len(sends)])
        copy.start()
        sends.append(copy)
    for copy in sends:
        copy.wait()


def finish_call(part, fine, halos, started=None):
    depth = part.shape[0]
    parts, count = [], 0
    for above, start, halo in halos:
        size = halo.shape[2]
        chunk = math.gcd(size, 512)
        half = (depth, depth - reach) if above else (-reach, 0)
        parts.append(half + (start, size, chunk))
        count += size // chunk
    aliased = started is not None
    held = pl.BlockSpec(memory_space=pltpu.VMEM)
    anywhere = pl.BlockSpec(memory_space=pl.ANY)
    widest = max(halo.shape[2] for _, _, halo in halos)
    return pl.pallas_call(
        functools.partial(finish_kernel, parts, aliased, aliased),
        in_specs=[held, held] + [held if aliased else anywhere] * len(halos) + [anywhere] * aliased,
        out_specs=anywhere,
        out_shape=jax.ShapeDtypeStruct(part.shape, jnp.float32),
        input_output_aliases={2 + len(halos): 0} if aliased else {},
        scratch_shapes=[
            pltpu.VMEM(part.shape, jnp.float32),
            pltpu.VMEM((len(halos), reach, part.shape[1], widest), jnp.float32),
            pltpu.SemaphoreType.DMA((count,)),
            pltpu.SemaphoreType.DMA((count,)),
        ],
        compiler_params=pltpu.CompilerParams(vmem_limit_bytes=vmem_bytes),
        cost_estimate=light,
        name="finish",
    )(part, fine, *[halo for _, _, halo in halos], *([started] if aliased else []))


def tie(value, *gates):
    anywhere = pl.BlockSpec(memory_space=pl.ANY)
    return pl.pallas_call(
        lambda *refs: None,
        in_specs=[anywhere] * (1 + len(gates)),
        out_specs=anywhere,
        out_shape=jax.ShapeDtypeStruct(value.shape, value.dtype),
        input_output_aliases={0: 0},
        cost_estimate=light,
        name="tie",
    )(value, *gates)


def slab_kernel(begin, source_hbm, out_ref, held_ref, in_sems, out_sems):
    layers, _, points = held_ref.shape
    share = points // slab_chunks
    spans = [pl.ds(c * share, share) for c in range(slab_chunks)]
    arrivals = [
        pltpu.make_async_copy(
            source_hbm.at[pl.ds(begin, layers), :, span], held_ref.at[:, :, span], in_sems.at[c]
        )
        for c, span in enumerate(spans)
    ]
    sends = [
        pltpu.make_async_copy(held_ref.at[:, :, span], out_ref.at[:, :, span], out_sems.at[c])
        for c, span in enumerate(spans)
    ]
    for copy in arrivals:
        copy.start()
    for copy, send in zip(arrivals, sends):
        copy.wait()
        send.start()
    for send in sends:
        send.wait()


def slab_call(scalar, width):
    depth, height, _ = scalar.shape
    shape = (reach, height, width)
    anywhere = pl.BlockSpec(memory_space=pl.ANY)
    return pl.pallas_call(
        functools.partial(slab_kernel, depth - reach),
        in_specs=[anywhere],
        out_specs=anywhere,
        out_shape=jax.ShapeDtypeStruct(shape, jnp.float32),
        scratch_shapes=[pltpu.VMEM(shape, jnp.float32)] + [pltpu.SemaphoreType.DMA((slab_chunks,))] * 2,
        compiler_params=pltpu.CompilerParams(vmem_limit_bytes=52 * 1024 * 1024),
        cost_estimate=light,
        name="slab",
    )(scalar)


def depart_kernel(own_hbm, scalar_hbm, gate, down_hbm, late_down_hbm, late_up_hbm, edge_hbm, sent_hbm, end_hbm,
                  own_ref, scalar_ref, ends_ref, edge_ref, in_sems, out_sems):
    kinds, rows, cells = own_ref.shape
    depth, height, points = scalar_ref.shape
    layers = [pl.ds(depth - reach, reach), pl.ds(0, reach)]
    middle = depth - 2 * reach
    arrivals = [
        pltpu.make_async_copy(scalar_hbm.at[span], scalar_ref.at[span], in_sems.at[i])
        for i, span in enumerate(layers + [pl.ds(reach, middle)] * (middle > 0))
    ]
    arrivals.append(pltpu.make_async_copy(own_hbm, own_ref, in_sems.at[3]))
    for copy in arrivals[::-1]:
        copy.start()
    sends = []

    def send(source, target):
        copy = pltpu.make_async_copy(source, target, out_sems.at[len(sends)])
        copy.start()
        sends.append(copy)

    arrivals[-1].wait()
    for kind in range(kinds):
        send(own_ref.at[kind], sent_hbm.at[pl.ds(kind * rows, rows)])
    for copy in arrivals[:-1]:
        copy.wait()
    cut = down_hbm.shape[2]
    send(scalar_ref.at[layers[1], :, pl.ds(0, cut)], down_hbm)
    send(scalar_ref.at[layers[1], :, pl.ds(cut, points - cut)], late_down_hbm)
    send(scalar_ref.at[layers[0], :, pl.ds(cut, points - cut)], late_up_hbm)
    edge_ref[:, :reach] = scalar_ref[:, :reach]
    edge_ref[:, reach:] = scalar_ref[:, height - reach :]
    send(edge_ref, edge_hbm)
    first = scalar_ref[:, :, :lanes].reshape(rows, lanes).T
    last = scalar_ref[:, :, points - lanes :].reshape(rows, lanes).T
    ends_ref[...] = jnp.zeros_like(ends_ref)
    ends_ref[:, :rows] = jnp.concatenate([first[:reach], last[lanes - reach :]], axis=0)
    send(ends_ref, sent_hbm.at[pl.ds(kinds * rows, 2 * reach)])
    send(ends_ref, end_hbm)
    for copy in sends:
        copy.wait()


def depart_call(own, scalar, cut, gate):
    kinds, rows, cells = own.shape
    depth, height, points = scalar.shape
    edge, ends = (depth, 2 * reach, points), (2 * reach, cells)
    shapes = [(reach, height, cut)] + [(reach, height, points - cut)] * 2 + [edge, (kinds * rows + 2 * reach, cells), ends]
    anywhere = pl.BlockSpec(memory_space=pl.ANY)
    return pl.pallas_call(
        depart_kernel,
        in_specs=[anywhere] * 3,
        out_specs=[anywhere] * len(shapes),
        out_shape=[jax.ShapeDtypeStruct(shape, jnp.float32) for shape in shapes],
        scratch_shapes=[
            pltpu.VMEM(own.shape, jnp.float32),
            pltpu.VMEM(scalar.shape, jnp.float32),
            pltpu.VMEM(ends, jnp.float32),
            pltpu.VMEM(edge, jnp.float32),
            pltpu.SemaphoreType.DMA((4,)),
            pltpu.SemaphoreType.DMA((6 + kinds,)),
        ],
        compiler_params=pltpu.CompilerParams(vmem_limit_bytes=most_vmem_bytes),
        cost_estimate=light,
        name="depart",
    )(own, scalar, gate)


def padded_2(block, sides, width):
    for axis, dim in sides:
        count = lax.axis_size(axis)
        forward = [(i, i + 1) for i in range(count - 1)]
        forward.append((count - 1, 0))
        backward = [(target, source) for source, target in forward]
        low = lax.ppermute(
            lax.slice_in_dim(block, block.shape[dim] - width, None, axis=dim), axis, forward
        )
        high = lax.ppermute(lax.slice_in_dim(block, 0, width, axis=dim), axis, backward)
        block = jnp.concatenate([low, block, high], axis=dim)
    return block


def derivative_rows(first_row, count, length):
    rows = first_row + lax.iota(jnp.int32, count)
    columns = lax.iota(jnp.int32, length)
    offset = (rows[:, None] - columns[None, :]) % length
    signed = jnp.where(offset > length // 2, offset - length, offset)
    angle = signed.astype(jnp.float32) * (math.pi / length)
    parity = 1.0 - 2.0 * (offset % 2).astype(jnp.float32)
    same = offset == 0
    sine = jnp.where(same, 1.0, jnp.sin(angle))
    first = jnp.where(same, 0.0, 0.5 * parity * jnp.cos(angle) / sine)
    second = jnp.where(same, -(length * length) / 12.0 - 1.0 / 6.0, -0.5 * parity / (sine * sine))
    average = jnp.full((count, length), 1.0 / length, jnp.float32)
    return jnp.concatenate([first, second, average], axis=0)


def scalar_update(padded, fine):
    extent = (padded.shape[0] - 8, padded.shape[1] - 8, padded.shape[2] - 8)
    centre = lax.slice(padded, (4, 4, 4), (4 + extent[0], 4 + extent[1], 4 + extent[2]))
    gradients = []
    curvature = jnp.zeros(extent, jnp.float32)
    for axis_index in range(3):
        slope = jnp.zeros(extent, jnp.float32)
        for offset in range(9):
            begin = [4, 4, 4]
            begin[axis_index] = offset
            finish = (begin[0] + extent[0], begin[1] + extent[1], begin[2] + extent[2])
            window = lax.slice(padded, tuple(begin), finish)
            if first_all[offset] != 0.0:
                slope = slope + first_all[offset] * window
            curvature = curvature + second_all[offset] * window
        gradients.append(slope)
    advection = fine[2] * gradients[0] + fine[1] * gradients[1] + fine[0] * gradients[2]
    return centre - advect_rate * advection + diffuse_rate * curvature


def general_per_device(velocity, scalar, spline_base, spline_frac):
    cells = velocity.shape[1]
    length = cells * lax.axis_size("blk")
    block = lax.axis_index("blk")
    table = derivative_rows(block * cells, cells, length)
    both = jnp.einsum(
        "km,cmzy->ckzy",
        table,
        lax.all_gather(velocity, "blk", axis=1, tiled=True),
        precision=highest,
    )
    segment = (
        velocity
        - both[:, 2 * cells :]
        + velocity_step * (viscosity * both[:, cells : 2 * cells] - velocity[0:1] * both[:, :cells])
    )
    widened = padded_2(segment, (("blk", 1),), 2)
    weights = catmull_weights(spline_frac)
    local_base = spline_base - (block * cells - 2)
    slots = lax.iota(jnp.int32, cells + 4)[:, None]
    matrix = jnp.zeros((cells + 4, spline_base.shape[0]), jnp.float32)
    for tap_index in range(4):
        matrix = matrix + jnp.where(
            slots == (local_base + (tap_index - 1))[None, :], weights[tap_index][None, :], 0.0
        )
    fine = jnp.einsum("cxzy,xi->czyi", widened, matrix, precision=highest)
    padded = padded_2(scalar, (("grp", 1), ("blk", 2), ("dep", 0)), 4)
    return (segment, scalar_update(padded, fine))


def per_device(velocity, scalar, spline_base, spline_frac):
    kinds, cells, depth, height = velocity.shape
    points = scalar.shape[2]
    rows = depth * height
    count = lax.axis_size("blk")
    if count != 4 or lax.axis_size("grp") != 2 or cells % lanes or rows > cells or (points // 2) % cells or depth != 2 * reach or points % (8 * lanes):
        return general_per_device(velocity, scalar, spline_base, spline_frac)
    length = cells * count
    block = lax.axis_index("blk")

    rows_of_x = jnp.transpose(velocity, (0, 2, 3, 1)).reshape(kinds, rows, cells)
    chip = lax.ppermute(rows_of_x, "blk", exclusive("blk", 2))
    cut = points - points // 8
    up = slab_call(scalar, cut)
    lower = lax.ppermute(up, "dep", ring("dep", 1))
    down, late_down, late_up, edges, own, ends = depart_call(rows_of_x, scalar, cut, up)
    upper = lax.ppermute(down, "dep", ring("dep", -1))
    late_upper = lax.ppermute(late_down, "dep", ring("dep", -1))
    far_ends = lax.ppermute(ends, "blk", exclusive("blk", 3))
    matrix = spline_matrix(spline_base - block * cells, spline_frac, cells, points // cells)
    outer_rows = lax.ppermute(edges, "grp", ring("grp", 1))
    core = lax.ppermute(tie(own, chip), "blk", exclusive("blk", 1))
    chip = tie(chip, far_ends, matrix, outer_rows)
    diagonal = lax.ppermute(chip, "blk", exclusive("blk", 1))
    late_lower = lax.ppermute(tie(late_up, diagonal), "dep", ring("dep", 1))
    info = jnp.stack([(block - (block ^ j)) % count for j in range(4)] + [block % 2]).astype(jnp.int32)
    main, outer = segment_call(rows_of_x, core, chip, diagonal, info, length)
    part, vertical = combine_call(main, outer, matrix, scalar, outer_rows, core, far_ends, info[4:])
    part, vertical = part.reshape(scalar.shape), vertical.reshape(scalar.shape)
    result = finish_call(part, vertical, [(False, 0, lower), (True, 0, upper)])
    result = finish_call(part, vertical, [(False, cut, late_lower), (True, cut, late_upper)], result)
    segment = jnp.transpose(main.reshape(kinds, depth, height, cells), (0, 3, 1, 2))
    return segment, result


def solution(mesh):
    in_specs = (P(None, "blk", "dep", "grp"), P("dep", "grp", "blk"), P("blk"), P("blk"))
    out_specs = (P(None, "blk", "dep", "grp"), P("dep", "grp", "blk"))
    return jax.shard_map(
        per_device, mesh=mesh, in_specs=in_specs, out_specs=out_specs, check_vma=False
    )
```

```python
import functools
import math

import jax
import jax.numpy as jnp
import ml_dtypes
import numpy as np
from jax import lax
from jax.experimental import pallas as pl
from jax.experimental.pallas import tpu as pltpu
from jax.sharding import PartitionSpec as P

velocity_step = 0.002
viscosity = 0.00125
advect_rate = 0.2
diffuse_rate = 0.05
first_side = (0.8, -0.2, 4.0 / 105.0, -1.0 / 280.0)
second_side = (1.6, -0.2, 8.0 / 315.0, -1.0 / 560.0)
second_centre = -205.0 / 72.0
first_all = tuple(-a for a in reversed(first_side)) + (0.0,) + first_side
second_all = tuple(reversed(second_side)) + (second_centre,) + second_side
slope = tuple(-advect_rate * a for a in first_side)
bend = tuple(diffuse_rate * b for b in second_side)
centre_weight = 1.0 + 3.0 * diffuse_rate * second_centre
highest = lax.Precision.HIGHEST
reach = 4
slab_chunks = 2
lanes = 128
vmem_bytes = 32 * 1024 * 1024
most_vmem_bytes = 60 * 1024 * 1024
light = pl.CostEstimate(flops=1024, bytes_accessed=1024, transcendentals=0)


def ring(axis, step):
    count = lax.axis_size(axis)
    return [(i, (i + step) % count) for i in range(count)]


def exclusive(axis, mask):
    return [(i, i ^ mask) for i in range(lax.axis_size(axis))]


def split_table(values):
    high = values.astype(np.float32).astype(ml_dtypes.bfloat16)
    low = (values - high.astype(np.float64)).astype(np.float32).astype(ml_dtypes.bfloat16)
    return high, low


def right_table(values):
    high, low = split_table(values)
    return np.concatenate([high, high, low], axis=-2)


def circulant_tables(length, cells):
    s = np.arange(length)
    signed = np.where(s > length // 2, s - length, s)
    angle = signed * (np.pi / length)
    sine = np.where(s == 0, 1.0, np.sin(angle))
    parity = 1.0 - 2.0 * (s % 2)
    first = np.where(s == 0, 0.0, 0.5 * parity * np.cos(angle) / sine) * velocity_step
    second = np.where(s == 0, -(length * length) / 12.0 - 1.0 / 6.0, -0.5 * parity / (sine * sine))
    second = second * (velocity_step * viscosity)
    own = np.arange(cells)
    outer = np.zeros(lanes, np.int64)
    used = np.zeros(lanes)
    for lane, cell in ((0, cells), (1, cells + 1), (lanes - 2, -2), (lanes - 1, -1)):
        outer[lane] = cell
        used[lane] = 1.0
    blocks = []
    for distance in range(length // cells):
        main = (distance * cells + own[None, :] - own[:, None]) % length
        side = (distance * cells + outer[None, :] - own[:, None]) % length
        blocks.append(
            np.concatenate([first[main], second[main], first[side] * used, second[side] * used], axis=1)
        )
    return right_table(np.stack(blocks))


def level_table(depth, height):
    size, side = depth * height, 2 * reach
    table = np.zeros((3, depth, height, size + depth * side))
    for z in range(depth):
        for y in range(height):
            for m in range(-reach, reach + 1):
                if m == 0:
                    continue
                first = slope[m - 1] if m > 0 else -slope[-m - 1]
                second = bend[abs(m) - 1]
                if 0 <= y + m < height:
                    at = z * height + y + m
                else:
                    at = size + z * side + (y + m - height if m > 0 else y + m + side)
                table[0, z, y, at] += first
                table[2, z, y, at] += second
                if 0 <= z + m < depth:
                    table[1, z, y, (z + m) * height + y] += first
                    table[2, z, y, (z + m) * height + y] += second
    high, low = split_table(table.reshape(3 * size, -1))
    return np.concatenate([high, high, low], axis=1)


def dot(a, b):
    return jnp.dot(a, b, preferred_element_type=jnp.float32)


def split(value):
    high = value.astype(jnp.bfloat16)
    return high, (value - high.astype(jnp.float32)).astype(jnp.bfloat16)


def left_operand(value):
    high, low = split(value)
    return jnp.concatenate([high, low, high], axis=1)


def segment_kernel(length, info, own_ref, core_ref, chip_ref, far_ref, *refs):
    table_refs, (main_ref, outer_ref) = refs[:4], refs[4:]
    kinds, rows, cells = own_ref.shape
    lines = kinds * rows
    blocks = [own_ref[...].reshape(lines, cells), core_ref[:lines]]
    blocks += [ref[...].reshape(lines, cells) for ref in (chip_ref, far_ref)]
    total = sums = None
    for block, table_ref in zip(blocks, table_refs):
        product = dot(left_operand(block), table_ref[0])
        partial = jnp.sum(block, axis=1, keepdims=True)
        total = product if total is None else total + product
        sums = partial if sums is None else sums + partial
    mean = sums * (1.0 / length)
    even = info[4] == 0
    after = jnp.where(even, blocks[1][:, :lanes], blocks[3][:, :lanes])
    before = jnp.where(even, blocks[3][:, cells - lanes :], blocks[1][:, cells - lanes :])
    place = lax.broadcasted_iota(jnp.int32, after.shape, 1)
    outer = jnp.where(place < lanes // 2, after, before)

    def advance(own, first, second):
        lead = jnp.concatenate([own[:rows]] * kinds, axis=0)
        return own - mean + (second - lead * first)

    main = advance(blocks[0], total[:, :cells], total[:, cells : 2 * cells])
    side = advance(outer, total[:, 2 * cells : 2 * cells + lanes], total[:, 2 * cells + lanes :])
    main_ref[...] = main.reshape(kinds, rows, cells)
    outer_ref[...] = side.reshape(kinds, rows, lanes)


def segment_call(own, core, chip, diagonal, info, length):
    kinds, rows, cells = own.shape
    table = circulant_tables(length, cells)
    whole = pl.BlockSpec(own.shape, lambda g, info: (0, 0, 0))
    sent = pl.BlockSpec(core.shape, lambda g, info: (0, 0))
    tables = [
        pl.BlockSpec((1,) + table.shape[1:], functools.partial(lambda j, g, info: (info[j], 0, 0), j))
        for j in range(4)
    ]
    return pl.pallas_call(
        functools.partial(segment_kernel, length),
        grid_spec=pltpu.PrefetchScalarGridSpec(
            num_scalar_prefetch=1,
            grid=(1,),
            in_specs=[whole, sent, whole, whole] + tables,
            out_specs=[whole, pl.BlockSpec((kinds, rows, lanes), lambda g, info: (0, 0, 0))],
        ),
        out_shape=[
            jax.ShapeDtypeStruct((kinds, rows, cells), jnp.float32),
            jax.ShapeDtypeStruct((kinds, rows, lanes), jnp.float32),
        ],
        compiler_params=pltpu.CompilerParams(vmem_limit_bytes=vmem_bytes),
        cost_estimate=light,
        name="segment",
    )(info, own, core, chip, diagonal, *([jnp.asarray(table)] * 4))


def catmull_weights(fraction):
    square = fraction * fraction
    cube = square * fraction
    return (
        (-cube + 2.0 * square - fraction) * 0.5,
        (3.0 * cube - 5.0 * square + 2.0) * 0.5,
        (-3.0 * cube + 4.0 * square + fraction) * 0.5,
        (cube - square) * 0.5,
    )


def spline_matrix(local_base, fraction, cells, refine):
    tiles = cells // lanes
    row = lax.iota(jnp.int32, 2 * lanes)[:, None]
    half = (lax.iota(jnp.int32, local_base.shape[0]) // (refine * (lanes // 2)))[None, :]
    own = half // 2
    other = (own + jnp.where(half % 2 == 1, 1, tiles)) % (tiles + 1)
    lane = jnp.where(row < lanes, own * lanes + row, other * lanes + row - lanes)
    cell = jnp.where(lane < cells + lanes // 2, lane, lane - cells - lanes)
    gap = cell - local_base[None, :]
    matrix = jnp.zeros(gap.shape, jnp.float32)
    for tap, weight in enumerate(catmull_weights(fraction)):
        matrix = jnp.where(gap == tap - 1, weight[None, :], matrix)
    return matrix


def end_terms(halo, sign):
    grade = curve = None
    place = lax.broadcasted_iota(jnp.int32, halo.shape, 1)
    halo = jnp.where(place >= lanes // 2 if sign < 0 else place < lanes // 2, halo, 0.0)
    for m in range(1, reach + 1):
        near = pltpu.roll(halo, (-sign * m) % lanes, 1)
        first, second = (sign * slope[m - 1]) * near, bend[m - 1] * near
        grade = first if grade is None else grade + first
        curve = second if curve is None else curve + second
    near = place < reach if sign < 0 else place >= lanes - reach
    return jnp.where(near, grade, 0.0), jnp.where(near, curve, 0.0)


def side_terms(ringed, extent):
    size = ringed.shape[1]
    grade = curve = None
    for m in range(1, reach + 1):
        ahead = pltpu.roll(ringed, size - m, 1)[:, :extent]
        behind = pltpu.roll(ringed, m, 1)[:, :extent]
        first, second = slope[m - 1] * (ahead - behind), bend[m - 1] * (ahead + behind)
        grade = first if grade is None else grade + first
        curve = second if curve is None else curve + second
    return grade, curve


def combine_kernel(tiles, parity, main_ref, outer_ref, matrix_ref, mid_ref, left_ref, right_ref, rows_ref, table_ref,
                   core_ref, far_ref, out_ref, fine_ref, seg_high, seg_low, halo_ref):
    step, steps = pl.program_id(0), pl.num_programs(0)
    kinds, rows, cells = main_ref.shape
    depth, height, width = mid_ref.shape

    @pl.when(step == 0)
    def _():
        for ref, begin, size in ((main_ref, 0, cells), (outer_ref, cells, lanes)):
            high, low = split(ref[...].reshape(kinds * rows, size))
            seg_high[:, begin : begin + size] = high
            seg_low[:, begin : begin + size] = low
        even = parity[0] == 0
        after = jnp.where(even, core_ref[:, :rows], far_ref[:, :rows])[:reach]
        before = jnp.where(even, far_ref[:, :rows], core_ref[:, :rows])[reach:]
        gap = jnp.zeros((lanes - 2 * reach, rows), jnp.float32)
        halo_ref[...] = jnp.concatenate([after, gap, before], axis=0).T

    own = step // 2
    other = lax.rem(own + jnp.where(lax.rem(step, 2) == 1, 1, tiles), tiles + 1)
    spans = [pl.ds(pl.multiple_of(at * lanes, lanes), lanes) for at in (own, other)]
    source = jnp.concatenate([ref[:, span] for ref in (seg_high, seg_low, seg_high) for span in spans], axis=1)
    high, low = split(matrix_ref[...])
    fine = dot(source, jnp.concatenate([high, high, low], axis=0))

    values = jnp.concatenate([mid_ref[...].reshape(rows, width), rows_ref[...].reshape(-1, width)], axis=0)
    high, low = split(values)
    level = dot(table_ref[...], jnp.concatenate([high, low, high], axis=0))

    place = lax.broadcasted_iota(jnp.int32, (height, lanes), 1)
    for z in range(depth):
        left = jnp.where(step == 0, 0.0, left_ref[z])
        right = jnp.where(step == steps - 1, 0.0, right_ref[z])
        mid = mid_ref[z]
        grade, curve = side_terms(jnp.concatenate([mid, jnp.where(place < lanes // 2, right, left)], axis=1), width)
        span = slice(z * height, (z + 1) * height)

        def of(array, kind):
            return array[kind * rows + z * height : kind * rows + (z + 1) * height]

        vertical = of(fine, 2)
        out_ref[span] = (centre_weight * mid + (curve + of(level, 2))) + (
            of(fine, 0) * grade + of(fine, 1) * of(level, 0) + vertical * of(level, 1)
        )
        fine_ref[span] = vertical
    for at, sign, begin in ((0, -1, 0), (steps - 1, 1, width - lanes)):

        @pl.when(step == at)
        def _():
            grade, curve = end_terms(halo_ref[...], sign)
            span = slice(begin, begin + lanes)
            out_ref[:, span] += fine[:rows, span] * grade + curve


def combine_call(main, outer, matrix, scalar, outer_rows, core, diagonal, parity):
    kinds, rows, cells = main.shape
    depth, height, points = scalar.shape
    steps = 2 * (cells // lanes)
    width = points // steps
    tiles, last = width // lanes, points // lanes - 1
    table = level_table(depth, height)
    flat_tile = pl.BlockSpec((rows, width), lambda t, parity: (0, t))
    edge = (depth, height, lanes)
    ends = pl.BlockSpec((2 * reach, cells), lambda t, parity: (core.shape[0] // (2 * reach) - 1, 0))
    flat = jax.ShapeDtypeStruct((rows, points), jnp.float32)
    return pl.pallas_call(
        functools.partial(combine_kernel, cells // lanes),
        grid_spec=pltpu.PrefetchScalarGridSpec(
            num_scalar_prefetch=1,
            grid=(steps,),
            in_specs=[
                pl.BlockSpec((kinds, rows, cells), lambda t, parity: (0, 0, 0)),
                pl.BlockSpec((kinds, rows, lanes), lambda t, parity: (0, 0, 0)),
                pl.BlockSpec((2 * lanes, width), lambda t, parity: (0, t)),
                pl.BlockSpec((depth, height, width), lambda t, parity: (0, 0, t)),
                pl.BlockSpec(edge, lambda t, parity: (0, 0, jnp.maximum(t * tiles - 1, 0))),
                pl.BlockSpec(edge, lambda t, parity: (0, 0, jnp.minimum((t + 1) * tiles, last))),
                pl.BlockSpec((depth, 2 * reach, width), lambda t, parity: (0, 0, t)),
                pl.BlockSpec(table.shape, lambda t, parity: (0, 0)),
                ends,
                pl.BlockSpec((2 * reach, cells), lambda t, parity: (0, 0)),
            ],
            out_specs=[flat_tile, flat_tile],
            scratch_shapes=[
                pltpu.VMEM((kinds * rows, cells + lanes), jnp.bfloat16),
                pltpu.VMEM((kinds * rows, cells + lanes), jnp.bfloat16),
                pltpu.VMEM((rows, lanes), jnp.float32),
            ],
        ),
        out_shape=[flat, flat],
        compiler_params=pltpu.CompilerParams(vmem_limit_bytes=vmem_bytes),
        cost_estimate=light,
        name="combine",
    )(parity, main, outer, matrix, scalar, scalar, scalar, outer_rows, jnp.asarray(table), core, diagonal)


def finish_kernel(parts, aliased, direct, part_ref, fine_ref, *refs):
    halos, (out_hbm, out_ref, held_ref, in_sems, out_sems) = refs[: len(parts)], refs[len(parts) + aliased :]
    work, arrivals, sends = [], [], []
    for i, (halo, (first_layer, begin, start, size, chunk)) in enumerate(zip(halos, parts)):
        for x in range(0, size, chunk):
            span, place = pl.ds(x, chunk), pl.ds(start + x, chunk)
            if direct:
                work.append((halo, first_layer, begin, span, place))
                continue
            copy = pltpu.make_async_copy(
                halo.at[:, :, span], held_ref.at[i, :, :, span], in_sems.at[len(arrivals)]
            )
            copy.start()
            arrivals.append(copy)
            work.append((held_ref.at[i], first_layer, begin, span, place))
    for c, (near_ref, first_layer, begin, held, span) in enumerate(work):
        if not direct:
            arrivals[c].wait()
        for p in range(begin, begin + reach):
            grade = curve = None
            for h in range(reach):
                m = first_layer + h - p
                if abs(m) <= reach:
                    near = near_ref[h, :, held]
                    first = (slope[m - 1] if m > 0 else -slope[-m - 1]) * near
                    second = bend[abs(m) - 1] * near
                    grade = first if grade is None else grade + first
                    curve = second if curve is None else curve + second
            out_ref[p, :, span] = part_ref[p, :, span] + (fine_ref[p, :, span] * grade + curve)
        at = pl.ds(begin, reach), slice(None), span
        copy = pltpu.make_async_copy(out_ref.at[at], out_hbm.at[at], out_sems.at[len(sends)])
        copy.start()
        sends.append(copy)
    for copy in sends:
        copy.wait()


def finish_call(part, fine, halos, started=None):
    depth = part.shape[0]
    parts, count = [], 0
    for above, start, halo in halos:
        size = halo.shape[2]
        chunk = math.gcd(size, 512)
        half = (depth, depth - reach) if above else (-reach, 0)
        parts.append(half + (start, size, chunk))
        count += size // chunk
    aliased = started is not None
    held = pl.BlockSpec(memory_space=pltpu.VMEM)
    anywhere = pl.BlockSpec(memory_space=pl.ANY)
    widest = max(halo.shape[2] for _, _, halo in halos)
    return pl.pallas_call(
        functools.partial(finish_kernel, parts, aliased, aliased),
        in_specs=[held, held] + [held if aliased else anywhere] * len(halos) + [anywhere] * aliased,
        out_specs=anywhere,
        out_shape=jax.ShapeDtypeStruct(part.shape, jnp.float32),
        input_output_aliases={2 + len(halos): 0} if aliased else {},
        scratch_shapes=[
            pltpu.VMEM(part.shape, jnp.float32),
            pltpu.VMEM((len(halos), reach, part.shape[1], widest), jnp.float32),
            pltpu.SemaphoreType.DMA((count,)),
            pltpu.SemaphoreType.DMA((count,)),
        ],
        compiler_params=pltpu.CompilerParams(vmem_limit_bytes=vmem_bytes),
        cost_estimate=light,
        name="finish",
    )(part, fine, *[halo for _, _, halo in halos], *([started] if aliased else []))


def tie(value, *gates):
    anywhere = pl.BlockSpec(memory_space=pl.ANY)
    return pl.pallas_call(
        lambda *refs: None,
        in_specs=[anywhere] * (1 + len(gates)),
        out_specs=anywhere,
        out_shape=jax.ShapeDtypeStruct(value.shape, value.dtype),
        input_output_aliases={0: 0},
        cost_estimate=light,
        name="tie",
    )(value, *gates)


def slab_kernel(begin, source_hbm, out_ref, held_ref, in_sems, out_sems):
    layers, _, points = held_ref.shape
    share = points // slab_chunks
    spans = [pl.ds(c * share, share) for c in range(slab_chunks)]
    arrivals = [
        pltpu.make_async_copy(
            source_hbm.at[pl.ds(begin, layers), :, span], held_ref.at[:, :, span], in_sems.at[c]
        )
        for c, span in enumerate(spans)
    ]
    sends = [
        pltpu.make_async_copy(held_ref.at[:, :, span], out_ref.at[:, :, span], out_sems.at[c])
        for c, span in enumerate(spans)
    ]
    for copy in arrivals:
        copy.start()
    for copy, send in zip(arrivals, sends):
        copy.wait()
        send.start()
    for send in sends:
        send.wait()


def slab_call(scalar, width):
    depth, height, _ = scalar.shape
    shape = (reach, height, width)
    anywhere = pl.BlockSpec(memory_space=pl.ANY)
    return pl.pallas_call(
        functools.partial(slab_kernel, depth - reach),
        in_specs=[anywhere],
        out_specs=anywhere,
        out_shape=jax.ShapeDtypeStruct(shape, jnp.float32),
        scratch_shapes=[pltpu.VMEM(shape, jnp.float32)] + [pltpu.SemaphoreType.DMA((slab_chunks,))] * 2,
        compiler_params=pltpu.CompilerParams(vmem_limit_bytes=52 * 1024 * 1024),
        cost_estimate=light,
        name="slab",
    )(scalar)


def depart_kernel(own_hbm, scalar_hbm, gate, down_hbm, late_down_hbm, late_up_hbm, edge_hbm, sent_hbm, end_hbm,
                  own_ref, scalar_ref, ends_ref, edge_ref, in_sems, out_sems):
    kinds, rows, cells = own_ref.shape
    depth, height, points = scalar_ref.shape
    layers = [pl.ds(depth - reach, reach), pl.ds(0, reach)]
    middle = depth - 2 * reach
    arrivals = [
        pltpu.make_async_copy(scalar_hbm.at[span], scalar_ref.at[span], in_sems.at[i])
        for i, span in enumerate(layers + [pl.ds(reach, middle)] * (middle > 0))
    ]
    arrivals.append(pltpu.make_async_copy(own_hbm, own_ref, in_sems.at[3]))
    for copy in arrivals[::-1]:
        copy.start()
    sends = []

    def send(source, target):
        copy = pltpu.make_async_copy(source, target, out_sems.at[len(sends)])
        copy.start()
        sends.append(copy)

    arrivals[-1].wait()
    for kind in range(kinds):
        send(own_ref.at[kind], sent_hbm.at[pl.ds(kind * rows, rows)])
    for copy in arrivals[:-1]:
        copy.wait()
    cut = down_hbm.shape[2]
    send(scalar_ref.at[layers[1], :, pl.ds(0, cut)], down_hbm)
    send(scalar_ref.at[layers[1], :, pl.ds(cut, points - cut)], late_down_hbm)
    send(scalar_ref.at[layers[0], :, pl.ds(cut, points - cut)], late_up_hbm)
    edge_ref[:, :reach] = scalar_ref[:, :reach]
    edge_ref[:, reach:] = scalar_ref[:, height - reach :]
    send(edge_ref, edge_hbm)
    first = scalar_ref[:, :, :lanes].reshape(rows, lanes).T
    last = scalar_ref[:, :, points - lanes :].reshape(rows, lanes).T
    ends_ref[...] = jnp.zeros_like(ends_ref)
    ends_ref[:, :rows] = jnp.concatenate([first[:reach], last[lanes - reach :]], axis=0)
    send(ends_ref, sent_hbm.at[pl.ds(kinds * rows, 2 * reach)])
    send(ends_ref, end_hbm)
    for copy in sends:
        copy.wait()


def depart_call(own, scalar, cut, gate):
    kinds, rows, cells = own.shape
    depth, height, points = scalar.shape
    edge, ends = (depth, 2 * reach, points), (2 * reach, cells)
    shapes = [(reach, height, cut)] + [(reach, height, points - cut)] * 2 + [edge, (kinds * rows + 2 * reach, cells), ends]
    anywhere = pl.BlockSpec(memory_space=pl.ANY)
    return pl.pallas_call(
        depart_kernel,
        in_specs=[anywhere] * 3,
        out_specs=[anywhere] * len(shapes),
        out_shape=[jax.ShapeDtypeStruct(shape, jnp.float32) for shape in shapes],
        scratch_shapes=[
            pltpu.VMEM(own.shape, jnp.float32),
            pltpu.VMEM(scalar.shape, jnp.float32),
            pltpu.VMEM(ends, jnp.float32),
            pltpu.VMEM(edge, jnp.float32),
            pltpu.SemaphoreType.DMA((4,)),
            pltpu.SemaphoreType.DMA((6 + kinds,)),
        ],
        compiler_params=pltpu.CompilerParams(vmem_limit_bytes=most_vmem_bytes),
        cost_estimate=light,
        name="depart",
    )(own, scalar, gate)


def padded_2(block, sides, width):
    for axis, dim in sides:
        count = lax.axis_size(axis)
        forward = [(i, i + 1) for i in range(count - 1)]
        forward.append((count - 1, 0))
        backward = [(target, source) for source, target in forward]
        low = lax.ppermute(
            lax.slice_in_dim(block, block.shape[dim] - width, None, axis=dim), axis, forward
        )
        high = lax.ppermute(lax.slice_in_dim(block, 0, width, axis=dim), axis, backward)
        block = jnp.concatenate([low, block, high], axis=dim)
    return block


def derivative_rows(first_row, count, length):
    rows = first_row + lax.iota(jnp.int32, count)
    columns = lax.iota(jnp.int32, length)
    offset = (rows[:, None] - columns[None, :]) % length
    signed = jnp.where(offset > length // 2, offset - length, offset)
    angle = signed.astype(jnp.float32) * (math.pi / length)
    parity = 1.0 - 2.0 * (offset % 2).astype(jnp.float32)
    same = offset == 0
    sine = jnp.where(same, 1.0, jnp.sin(angle))
    first = jnp.where(same, 0.0, 0.5 * parity * jnp.cos(angle) / sine)
    second = jnp.where(same, -(length * length) / 12.0 - 1.0 / 6.0, -0.5 * parity / (sine * sine))
    average = jnp.full((count, length), 1.0 / length, jnp.float32)
    return jnp.concatenate([first, second, average], axis=0)


def scalar_update(padded, fine):
    extent = (padded.shape[0] - 8, padded.shape[1] - 8, padded.shape[2] - 8)
    centre = lax.slice(padded, (4, 4, 4), (4 + extent[0], 4 + extent[1], 4 + extent[2]))
    gradients = []
    curvature = jnp.zeros(extent, jnp.float32)
    for axis_index in range(3):
        slope = jnp.zeros(extent, jnp.float32)
        for offset in range(9):
            begin = [4, 4, 4]
            begin[axis_index] = offset
            finish = (begin[0] + extent[0], begin[1] + extent[1], begin[2] + extent[2])
            window = lax.slice(padded, tuple(begin), finish)
            if first_all[offset] != 0.0:
                slope = slope + first_all[offset] * window
            curvature = curvature + second_all[offset] * window
        gradients.append(slope)
    advection = fine[2] * gradients[0] + fine[1] * gradients[1] + fine[0] * gradients[2]
    return centre - advect_rate * advection + diffuse_rate * curvature


def general_per_device(velocity, scalar, spline_base, spline_frac):
    cells = velocity.shape[1]
    length = cells * lax.axis_size("blk")
    block = lax.axis_index("blk")
    table = derivative_rows(block * cells, cells, length)
    both = jnp.einsum(
        "km,cmzy->ckzy",
        table,
        lax.all_gather(velocity, "blk", axis=1, tiled=True),
        precision=highest,
    )
    segment = (
        velocity
        - both[:, 2 * cells :]
        + velocity_step * (viscosity * both[:, cells : 2 * cells] - velocity[0:1] * both[:, :cells])
    )
    widened = padded_2(segment, (("blk", 1),), 2)
    weights = catmull_weights(spline_frac)
    local_base = spline_base - (block * cells - 2)
    slots = lax.iota(jnp.int32, cells + 4)[:, None]
    matrix = jnp.zeros((cells + 4, spline_base.shape[0]), jnp.float32)
    for tap_index in range(4):
        matrix = matrix + jnp.where(
            slots == (local_base + (tap_index - 1))[None, :], weights[tap_index][None, :], 0.0
        )
    fine = jnp.einsum("cxzy,xi->czyi", widened, matrix, precision=highest)
    padded = padded_2(scalar, (("grp", 1), ("blk", 2), ("dep", 0)), 4)
    return (segment, scalar_update(padded, fine))


def per_device(velocity, scalar, spline_base, spline_frac):
    kinds, cells, depth, height = velocity.shape
    points = scalar.shape[2]
    rows = depth * height
    count = lax.axis_size("blk")
    if count != 4 or lax.axis_size("grp") != 2 or cells % lanes or rows > cells or (points // 2) % cells or depth != 2 * reach or points % (8 * lanes):
        return general_per_device(velocity, scalar, spline_base, spline_frac)
    length = cells * count
    block = lax.axis_index("blk")

    rows_of_x = jnp.transpose(velocity, (0, 2, 3, 1)).reshape(kinds, rows, cells)
    chip = lax.ppermute(rows_of_x, "blk", exclusive("blk", 2))
    cut = points - points // 8
    up = slab_call(scalar, cut)
    lower = lax.ppermute(up, "dep", ring("dep", 1))
    down, late_down, late_up, edges, own, ends = depart_call(rows_of_x, scalar, cut, up)
    upper = lax.ppermute(down, "dep", ring("dep", -1))
    late_upper = lax.ppermute(late_down, "dep", ring("dep", -1))
    far_ends = lax.ppermute(ends, "blk", exclusive("blk", 3))
    matrix = spline_matrix(spline_base - block * cells, spline_frac, cells, points // cells)
    outer_rows = lax.ppermute(edges, "grp", ring("grp", 1))
    core = lax.ppermute(tie(own, chip), "blk", exclusive("blk", 1))
    chip = tie(chip, far_ends, matrix, outer_rows)
    diagonal = lax.ppermute(chip, "blk", exclusive("blk", 1))
    late_lower = lax.ppermute(tie(late_up, chip), "dep", ring("dep", 1))
    info = jnp.stack([(block - (block ^ j)) % count for j in range(4)] + [block % 2]).astype(jnp.int32)
    main, outer = segment_call(rows_of_x, core, chip, diagonal, info, length)
    part, vertical = combine_call(main, outer, matrix, scalar, outer_rows, core, far_ends, info[4:])
    part, vertical = part.reshape(scalar.shape), vertical.reshape(scalar.shape)
    result = finish_call(part, vertical, [(False, 0, lower), (True, 0, upper)])
    result = finish_call(part, vertical, [(False, cut, late_lower), (True, cut, late_upper)], result)
    segment = jnp.transpose(main.reshape(kinds, depth, height, cells), (0, 3, 1, 2))
    return segment, result


def solution(mesh):
    in_specs = (P(None, "blk", "dep", "grp"), P("dep", "grp", "blk"), P("blk"), P("blk"))
    out_specs = (P(None, "blk", "dep", "grp"), P("dep", "grp", "blk"))
    return jax.shard_map(
        per_device, mesh=mesh, in_specs=in_specs, out_specs=out_specs, check_vma=False
    )
```
